32 devices in a mesh: dp: 8 (over z, y), seq: 4 (over x, core).
Axes of the slice: x: 2, y: 2, z: 4, core: 2. Of those that a mesh axis runs over, the one named last changes fastest.
Arguments:
- tokens: bfloat16 [8, 1024, 2048], P('dp', 'seq'), may hold values from -6 to 6
- cotangent: bfloat16 [8, 1024, 2048], P('dp', 'seq'), may hold values from -6 to 6
- lengths: int32 [8], P('dp'), may hold values from 256 to 1024, as said below
- adapter_ids: int32 [8], P('dp'), may hold values from 0 to 7
- attn_gain: float32 [2048], replicated, may hold values from 0.5 to 1.5
- query_gain: float32 [64], replicated, may hold values from 0.1 to 1.9
- key_gain: float32 [64], replicated, may hold values from 0.1 to 1.9
- ffn_gain: float32 [2048], replicated, may hold values from 0.5 to 1.5
- w_query: bfloat16 [2048, 2048], P(('dp', 'seq')), may hold values from -0.125 to 0.125
- w_key: bfloat16 [2048, 512], P(('dp', 'seq')), may hold values from -0.125 to 0.125
- w_value: bfloat16 [2048, 512], P(('dp', 'seq')), may hold values from -0.125 to 0.125
- w_out: bfloat16 [2048, 2048], P(('dp', 'seq')), may hold values from -1.5 to 1.5
- gate_weight: bfloat16 [2048, 8192], P(('dp', 'seq')), may hold values from -0.125 to 0.125
- w_up: bfloat16 [2048, 8192], P(('dp', 'seq')), may hold values from -0.125 to 0.125
- w_down: bfloat16 [8192, 2048], P(('dp', 'seq')), may hold values from -0.0625 to 0.0625
- a_query: bfloat16 [8, 2048, 16], P(None, ('dp', 'seq')), may hold values from -0.125 to 0.125
- b_query: bfloat16 [8, 2048, 16], P(None, ('dp', 'seq')), may hold values from -1.5 to 1.5
- a_key: bfloat16 [8, 2048, 16], P(None, ('dp', 'seq')), may hold values from -0.125 to 0.125
- b_key: bfloat16 [8, 512, 16], P(None, ('dp', 'seq')), may hold values from -1.5 to 1.5
- a_value: bfloat16 [8, 2048, 16], P(None, ('dp', 'seq')), may hold values from -0.125 to 0.125
- b_value: bfloat16 [8, 512, 16], P(None, ('dp', 'seq')), may hold values from -1.5 to 1.5
- a_out: bfloat16 [8, 2048, 16], P(None, ('dp', 'seq')), may hold values from -1.5 to 1.5
- b_out: bfloat16 [8, 2048, 16], P(None, ('dp', 'seq')), may hold values from -1.5 to 1.5
- a_gate: bfloat16 [8, 2048, 16], P(None, ('dp', 'seq')), may hold values from -0.125 to 0.125
- b_gate: bfloat16 [8, 8192, 16], P(None, ('dp', 'seq')), may hold values from -1.5 to 1.5
- a_up: bfloat16 [8, 2048, 16], P(None, ('dp', 'seq')), may hold values from -0.125 to 0.125
- b_up: bfloat16 [8, 8192, 16], P(None, ('dp', 'seq')), may hold values from -1.5 to 1.5
- a_down: bfloat16 [8, 8192, 16], P(None, ('dp', 'seq')), may hold values from -0.0625 to 0.0625
- b_down: bfloat16 [8, 2048, 16], P(None, ('dp', 'seq')), may hold values from -1.5 to 1.5
Outputs:
- output: bfloat16 [8, 1024, 2048], P('dp', 'seq')
- grad_tokens: bfloat16 [8, 1024, 2048], P('dp', 'seq')
- grad_a_query: float32 [8, 2048, 16], P(None, ('dp', 'seq'))
- grad_b_query: float32 [8, 2048, 16], P(None, ('dp', 'seq'))
- grad_a_key: float32 [8, 2048, 16], P(None, ('dp', 'seq'))
- grad_b_key: float32 [8, 512, 16], P(None, ('dp', 'seq'))
- grad_a_value: float32 [8, 2048, 16], P(None, ('dp', 'seq'))
- grad_b_value: float32 [8, 512, 16], P(None, ('dp', 'seq'))
- grad_a_out: float32 [8, 2048, 16], P(None, ('dp', 'seq'))
- grad_b_out: float32 [8, 2048, 16], P(None, ('dp', 'seq'))
- grad_a_gate: float32 [8, 2048, 16], P(None, ('dp', 'seq'))
- grad_b_gate: float32 [8, 8192, 16], P(None, ('dp', 'seq'))
- grad_a_up: float32 [8, 2048, 16], P(None, ('dp', 'seq'))
- grad_b_up: float32 [8, 8192, 16], P(None, ('dp', 'seq'))
- grad_a_down: float32 [8, 8192, 16], P(None, ('dp', 'seq'))
- grad_b_down: float32 [8, 2048, 16], P(None, ('dp', 'seq'))
The draws below stay inside these ranges and needn't reach their ends.
Inputs may be any that keep to these rules, and one draw needn't show every extreme that they name: `lengths`: one sequence in every draw has all 1024 tokens valid.
All inputs are finite; a program needn't handle non-finite values.
Results may differ from the reference program's by a relative error of at most 0.02.
Values may be sent and summed in bfloat16 or wider, within the bound.
No kernel may reach another device: no remote copies, remote signals or barrier semaphores. Data moves between devices by JAX's collectives and lax.ppermute only.
A program may use at most 384 MiB of HBM per device.

```python
import jax
import jax.numpy as jnp
from jax import lax

D = 2048
H = 32
KV = 8
HD = 64
FF = 8192
RANK = 16
ADAPT = 8
LEN = 1024
SEQS = 8


def draw_lengths(key, part):
    key = jax.random.fold_in(key, 7)
    first_key, second_key = jax.random.split(key)
    drawn = jax.random.randint(first_key, (SEQS,), LEN // 4, LEN + 1)
    chosen = jax.random.randint(second_key, (), 0, SEQS)
    return jnp.where(jnp.arange(SEQS) == chosen, LEN, drawn).astype(jnp.int32)


def touch_ends(entries, rng, low, high):
    longest = entries.shape.index(max(entries.shape))
    spots = []
    for shift in (0, 1):
        where = [jax.random.randint(jax.random.fold_in(rng, axis), (), 0, length) for axis, length in enumerate(entries.shape)]
        where[longest] = (where[longest] + shift) % entries.shape[longest]
        spots.append(tuple(where))
    return entries.at[spots[0]].set(low).at[spots[1]].set(high)


def block_levels(rng, dims, cuts, least, largest):
    level, own = 1.0, jax.random.fold_in(rng, 6)
    for dim, shards_of in cuts:
        steps = jnp.exp(jax.random.uniform(jax.random.fold_in(own, dim), (shards_of,), jnp.float32, least / len(cuts), largest / len(cuts)))
        level = level * jnp.repeat(steps, dims[dim] // shards_of).reshape([-1 if axis == dim else 1 for axis in range(len(dims))])
    return level


def scatter_about(rng, shape, scale, limit, pieces=(), held_as=jnp.bfloat16):
    values = jax.random.normal(rng, shape, jnp.float32) * scale
    if len(pieces) > 0:
        values = block_levels(rng, shape, pieces, -0.22, 0.18) * values
    return jnp.clip(values, min=-limit, max=limit).astype(held_as)


def setup_inputs(seed: int = 0) -> dict:
    seeds = jax.random.split(jax.random.key(seed), 30)
    tokens = scatter_about(seeds[0], (SEQS, LEN, D), 1.0, 6.0, ((0, 8), (1, 4)))
    cotangent = scatter_about(seeds[1], (SEQS, LEN, D), 1.0, 6.0, ((0, 8), (1, 4)))
    lengths = draw_lengths(jax.random.fold_in(seeds[29], 71), 0)
    adapter_ids = touch_ends(jax.random.randint(seeds[3], (SEQS,), 0, ADAPT), jax.random.fold_in(seeds[3], 1), 0, ADAPT - 1).astype(jnp.int32)
    attn_gain = jnp.clip(1.0 + 0.1 * jax.random.normal(seeds[4], (D,), jnp.float32), 0.5, 1.5)
    query_gain = jnp.clip(1.0 + 0.18 * jax.random.normal(seeds[5], (HD,), jnp.float32), 0.1, 1.9)
    key_gain = jnp.clip(1.0 + 0.18 * jax.random.normal(seeds[6], (HD,), jnp.float32), 0.1, 1.9)
    ffn_gain = jnp.clip(1.0 + 0.1 * jax.random.normal(seeds[7], (D,), jnp.float32), 0.5, 1.5)
    w_query = scatter_about(seeds[8], (D, D), D ** -0.5, 0.125, ((0, 32),))
    w_key = scatter_about(seeds[9], (D, KV * HD), D ** -0.5, 0.125, ((0, 32),))
    w_value = scatter_about(seeds[10], (D, KV * HD), D ** -0.5, 0.125, ((0, 32),))
    w_out = scatter_about(seeds[11], (D, D), (max(D * 8 // LEN, 1)) ** -0.5, 1.5, ((0, 32),))
    gate_weight = scatter_about(seeds[12], (D, FF), D ** -0.5, 0.125, ((0, 32),))
    w_up = scatter_about(seeds[13], (D, FF), D ** -0.5, 0.125, ((0, 32),))
    w_down = scatter_about(seeds[14], (FF, D), FF ** -0.5, 0.0625, ((0, 32),))
    a_query = scatter_about(seeds[15], (ADAPT, D, RANK), D ** -0.5, 0.125, ((1, 32),))
    b_query = scatter_about(seeds[16], (ADAPT, D, RANK), RANK ** -0.5, 1.5, ((1, 32),))
    a_key = scatter_about(seeds[17], (ADAPT, D, RANK), D ** -0.5, 0.125, ((1, 32),))
    b_key = scatter_about(seeds[18], (ADAPT, KV * HD, RANK), RANK ** -0.5, 1.5, ((1, 32),))
    a_value = scatter_about(seeds[19], (ADAPT, D, RANK), D ** -0.5, 0.125, ((1, 32),))
    b_value = scatter_about(seeds[20], (ADAPT, KV * HD, RANK), RANK ** -0.5, 1.5, ((1, 32),))
    a_out = scatter_about(seeds[21], (ADAPT, D, RANK), (max(D * 8 // LEN, 1)) ** -0.5, 1.5, ((1, 32),))
    b_out = scatter_about(seeds[22], (ADAPT, D, RANK), RANK ** -0.5, 1.5, ((1, 32),))
    a_gate = scatter_about(seeds[23], (ADAPT, D, RANK), D ** -0.5, 0.125, ((1, 32),))
    b_gate = scatter_about(seeds[24], (ADAPT, FF, RANK), RANK ** -0.5, 1.5, ((1, 32),))
    a_up = scatter_about(seeds[25], (ADAPT, D, RANK), D ** -0.5, 0.125, ((1, 32),))
    b_up = scatter_about(seeds[26], (ADAPT, FF, RANK), RANK ** -0.5, 1.5, ((1, 32),))
    a_down = scatter_about(seeds[27], (ADAPT, FF, RANK), FF ** -0.5, 0.0625, ((1, 32),))
    b_down = scatter_about(seeds[28], (ADAPT, D, RANK), RANK ** -0.5, 1.5, ((1, 32),))
    return dict(tokens=tokens, cotangent=cotangent, lengths=lengths, adapter_ids=adapter_ids, attn_gain=attn_gain, query_gain=query_gain, key_gain=key_gain, ffn_gain=ffn_gain, w_query=w_query, w_key=w_key, w_value=w_value, w_out=w_out, gate_weight=gate_weight, w_up=w_up, w_down=w_down, a_query=a_query, b_query=b_query, a_key=a_key, b_key=b_key, a_value=a_value, b_value=b_value, a_out=a_out, b_out=b_out, a_gate=a_gate, b_gate=b_gate, a_up=a_up, b_up=b_up, a_down=a_down, b_down=b_down)


@jax.custom_vjp
def low(v):
    return lax.optimization_barrier(v.astype(jnp.bfloat16)).astype(jnp.float32)

@jax.custom_vjp
def low_back(v):
    return v

def low_keep(v):
    return (low(v), None)

def low_pass(kept, grad):
    return (grad,)

def back_keep(v):
    return (v, None)

def back_low(kept, grad):
    return (low(grad),)
low.defvjp(low_keep, low_pass)
low_back.defvjp(back_keep, back_low)

def rms_scale(operand, scaling):
    return operand * lax.rsqrt(lax.optimization_barrier(jnp.mean(operand * operand, axis=-1, keepdims=True)) + 1e-05) * scaling

def rotary_tables(positions, size):
    frequency = jnp.power(1000000.0, -jnp.arange(size // 2, dtype=jnp.float32) * 2.0 / size)
    angles = positions.astype(jnp.float32)[:, None] * frequency[None, :]
    return (jnp.cos(angles), jnp.sin(angles))

def rotate(operand, cosine_table, sine_table):
    half_size = operand.shape[-1] // 2
    front = operand[..., :half_size]
    second = operand[..., half_size:]
    return jnp.concatenate([front * cosine_table - second * sine_table, second * cosine_table + front * sine_table], axis=-1)

def prepare(linear, scaling, cosine_table, sine_table, head_count):
    shaped = linear.reshape(linear.shape[:-1] + (head_count, linear.shape[-1] // head_count))
    return rotate(rms_scale(shaped, scaling), cosine_table[:, None, :], sine_table[:, None, :])

def product(left, right):
    return jnp.dot(left, right, precision=lax.Precision.HIGHEST, preferred_element_type=jnp.float32)

def adapted(operand, matrix, lower, adapter_expand):
    adapter_inner = low(low_back(product(operand, lower)))
    return product(operand, matrix) + product(adapter_inner, adapter_expand.T)

def layer(sequence, length, picked, frozen, gain_set, cosine_table, sine_table):
    m_query, m_key, m_value, m_out, m_gate, m_up, m_down = frozen
    attn_gain, query_gain, key_gain, ffn_gain = gain_set
    seq_len = sequence.shape[0]
    positions = jnp.arange(seq_len)
    valid_rows = (positions < length).astype(jnp.float32)[:, None]
    allowed = (positions[None, :] <= positions[:, None]) & (positions[None, :] < length)
    normed = low(rms_scale(sequence, attn_gain))
    query_lin = low_back(adapted(normed, m_query, picked[0], picked[1]))
    key_lin = low_back(adapted(normed, m_key, picked[2], picked[3]))
    value_lin = low(low_back(adapted(normed, m_value, picked[4], picked[5])))
    queries = low(prepare(query_lin, query_gain, cosine_table, sine_table, H))
    keys_all = low(prepare(key_lin, key_gain, cosine_table, sine_table, KV))
    query_heads = queries.reshape(seq_len, KV, H // KV, HD).transpose(1, 2, 0, 3)
    key_heads = keys_all.transpose(1, 0, 2)
    value_heads = value_lin.reshape(seq_len, KV, HD).transpose(1, 0, 2)

    def head_group(member):
        query_part, key_part, value_slice = member
        scores = jnp.einsum('gqd,kd->gqk', query_part, key_part, precision=lax.Precision.HIGHEST, preferred_element_type=jnp.float32)
        scores = low_back(scores * HD ** (-0.5))
        scores = jnp.where(allowed[None], scores, -1e+30)
        row_max = lax.optimization_barrier(jnp.max(scores, axis=-1, keepdims=True))
        exponent = jnp.exp(scores - row_max)
        weights_low = low(exponent / lax.optimization_barrier(jnp.sum(exponent, axis=-1, keepdims=True)))
        return jnp.einsum('gqk,kd->gqd', weights_low, value_slice, precision=lax.Precision.HIGHEST, preferred_element_type=jnp.float32)
    attended = lax.map(jax.checkpoint(head_group), (query_heads, key_heads, value_heads))
    attended = low(low_back(attended.transpose(2, 0, 1, 3).reshape(seq_len, H * HD)))
    hidden = sequence + valid_rows * low_back(adapted(attended, m_out, picked[6], picked[7]))
    normed_two = low(rms_scale(hidden, ffn_gain))
    gate_lin = low_back(adapted(normed_two, m_gate, picked[8], picked[9]))
    upward = low_back(adapted(normed_two, m_up, picked[10], picked[11]))
    active = low(jax.nn.silu(gate_lin) * upward)
    return hidden + valid_rows * low_back(adapted(active, m_down, picked[12], picked[13]))

def reference(tokens, cotangent, lengths, adapter_ids, attn_gain, query_gain, key_gain, ffn_gain, w_query, w_key, w_value, w_out, gate_weight, w_up, w_down, a_query, b_query, a_key, b_key, a_value, b_value, a_out, b_out, a_gate, b_gate, a_up, b_up, a_down, b_down):
    frozen = tuple((matrix.astype(jnp.float32) for matrix in (w_query, w_key, w_value, w_out, gate_weight, w_up, w_down)))
    gain_set = (attn_gain, query_gain, key_gain, ffn_gain)
    stacks = tuple((stack.astype(jnp.float32) for stack in (a_query, b_query, a_key, b_key, a_value, b_value, a_out, b_out, a_gate, b_gate, a_up, b_up, a_down, b_down)))
    cosine_table, sine_table = rotary_tables(jnp.arange(LEN), HD)

    def forward(inputs, adapters):

        def seq_step(carried, member):
            sequence, length, chosen = member
            picked = [lax.dynamic_index_in_dim(stack, chosen, 0, keepdims=False) for stack in adapters]
            return (carried, layer(sequence, length, picked, frozen, gain_set, cosine_table, sine_table))
        return lax.scan(jax.checkpoint(seq_step), jnp.zeros((), jnp.float32), (inputs, lengths, adapter_ids))[1]
    outputs, pullback = jax.vjp(forward, tokens.astype(jnp.float32), stacks)
    grad_inputs, adapter_grads = pullback(cotangent.astype(jnp.float32))
    return (outputs.astype(jnp.bfloat16), grad_inputs.astype(jnp.bfloat16), adapter_grads[0], adapter_grads[1], adapter_grads[2], adapter_grads[3], adapter_grads[4], adapter_grads[5], adapter_grads[6], adapter_grads[7], adapter_grads[8], adapter_grads[9], adapter_grads[10], adapter_grads[11], adapter_grads[12], adapter_grads[13])
```

```python
import functools

import jax
import jax.numpy as jnp
import numpy as np
from jax import lax
from jax.experimental import pallas as pl
from jax.experimental.pallas import tpu as pltpu
from jax.sharding import PartitionSpec as P

H = 32
KV = 8
HD = 64
GROUP = H // KV
ADAPT = 8
RANK = 16
EPS = 1e-05
F32 = jnp.float32
BF16 = jnp.bfloat16


def contract(left, right, left_dim, right_dim):
    return lax.dot_general(
        left, right, (((left_dim,), (right_dim,)), ((), ())), preferred_element_type=F32
    )


def rms_scale(operand, scaling, axis=-1):
    mean = jnp.mean(operand * operand, axis=axis, keepdims=True)
    return operand * lax.rsqrt(mean + EPS) * scaling


def rotary_tables(positions):
    frequency = jnp.power(1000000.0, -jnp.arange(HD // 2, dtype=F32) * 2.0 / HD)
    angles = frequency[:, None] * positions.astype(F32)[None, :]
    return jnp.cos(angles), jnp.sin(angles)


def prepare(linear, scaling, cosine, sine):
    normed = rms_scale(linear, scaling[:, None], axis=1)
    front, second = normed[:, : HD // 2], normed[:, HD // 2 :]
    return jnp.concatenate(
        [front * cosine - second * sine, second * cosine + front * sine], axis=1
    )


def ring_order(size):
    return list(range(0, size, 2)) + list(range(1, size, 2))[::-1]


def ring_pairs(size):
    order = ring_order(size)
    right = [(order[i], order[(i + 1) % size]) for i in range(size)]
    return right, [(b, a) for a, b in right]


def ring_pieces(own):
    size = lax.axis_size("dp")
    right, left = ring_pairs(size)
    pieces = [(0, own)]
    from_left = from_right = own
    for step in range(1, (size - 1) // 2 + 1):
        from_left = lax.ppermute(from_left, "dp", right)
        from_right = lax.ppermute(from_right, "dp", left)
        pieces += [(-step, from_left), (step, from_right)]
    half = own.shape[0] // 2
    top = lax.ppermute(from_left[:half], "dp", right)
    bottom = lax.ppermute(from_right[half:], "dp", left)
    return pieces, (size // 2, top, bottom)


def ring_source(offset):
    size = lax.axis_size("dp")
    order = ring_order(size)
    place = np.argsort(np.array(order))
    here = jnp.asarray(place)[lax.axis_index("dp")]
    return jnp.asarray(np.array(order))[(here + offset) % size]


def ring_gather(own):
    pieces, (far, top, bottom) = ring_pieces(own)
    whole = jnp.zeros((lax.axis_size("dp"),) + own.shape, own.dtype)
    for offset, piece in pieces:
        whole = lax.dynamic_update_slice(whole, piece[None], (ring_source(offset), 0, 0))
    whole = lax.dynamic_update_slice(whole, top[None], (ring_source(far), 0, 0))
    return lax.dynamic_update_slice(whole, bottom[None], (ring_source(far), top.shape[0], 0))


def partner(operand, bit):
    size = lax.axis_size("seq")
    return lax.ppermute(operand, "seq", [(i, i ^ bit) for i in range(size)])


def everywhere_gather(own):
    pieces, (far, top, bottom) = ring_pieces(own)
    pieces = pieces + [(far, jnp.concatenate([top, bottom], axis=0))]
    rows = []
    for _, piece in pieces:
        across = partner(piece, 2)
        rows += [piece, partner(piece, 1), across, partner(across, 1)]
    return jnp.concatenate(rows, axis=0)


def everywhere_order():
    size = lax.axis_size("dp")
    seq = lax.axis_index("seq")
    offsets = [0]
    for step in range(1, (size - 1) // 2 + 1):
        offsets += [-step, step]
    offsets += [size // 2]
    blocks = [ring_source(o) * lax.axis_size("seq") + (seq ^ j) for o in offsets for j in range(4)]
    return jnp.stack(blocks)


def seq_gather(own):
    seq = lax.axis_index("seq")
    side = partner(own, 1)
    across = partner(own, 2)
    corner = partner(across, 1)
    whole = jnp.zeros((lax.axis_size("seq"),) + own.shape, own.dtype)
    rest = (0,) * own.ndim
    for bit, piece in enumerate((own, side, across, corner)):
        whole = lax.dynamic_update_slice(whole, piece[None], (seq ^ bit,) + rest)
    return whole


def seq_exchange(slots):
    seq = lax.axis_index("seq")
    pick = lambda bit: lax.dynamic_index_in_dim(slots, seq ^ bit, 0, keepdims=False)
    got = [pick(0)] + [partner(pick(bit), bit) for bit in (1, 2, 3)]
    whole = jnp.zeros(slots.shape, slots.dtype)
    rest = (0,) * (slots.ndim - 1)
    for bit, piece in enumerate(got):
        whole = lax.dynamic_update_slice(whole, piece[None], (seq ^ bit,) + rest)
    return whole


def seq_reduce(partial, wire=BF16):
    seq = lax.axis_index("seq")
    x, core = seq // 2, seq % 2
    pairs = partial.reshape((2, 2) + partial.shape[1:])
    column = lambda c: lax.dynamic_index_in_dim(pairs, c, 1, keepdims=False)
    arrived = partner(column(1 - core).astype(wire), 1)
    both = column(core).astype(F32) + arrived.astype(F32)
    row = lambda r: lax.dynamic_index_in_dim(both, r, 0, keepdims=False)
    return row(x) + partner(row(1 - x).astype(wire), 2).astype(F32)


def attend_kernel(limit_ref, q_ref, k_ref, v_ref, o_ref, e_ref, r_ref):
    blocks, _, _, block = k_ref.shape
    heads = [q_ref[h * HD : (h + 1) * HD] for h in range(GROUP)]
    queries = jnp.concatenate(heads, axis=1)
    limit = limit_ref[...]
    total = jnp.zeros(limit.shape, F32)
    mixed = jnp.zeros(queries.shape, F32)
    for j in range(blocks):
        scores = contract(k_ref[j, 0], queries, 0, 0)
        places = j * block + lax.broadcasted_iota(jnp.int32, scores.shape, 0)
        raised = jnp.where(places <= limit, jnp.exp(scores), 0.0)
        total = total + jnp.sum(raised, axis=0, keepdims=True)
        low = raised.astype(BF16)
        e_ref[0, j] = low
        mixed = mixed + contract(v_ref[j, 0], low, 1, 0)
    inverse = 1.0 / total
    r_ref[0] = inverse
    mixed = (mixed * inverse).astype(BF16)
    width = q_ref.shape[1]
    for h in range(GROUP):
        o_ref[h * HD : (h + 1) * HD] = mixed[:, h * width : (h + 1) * width]


def attend_back_kernel(
    q_ref, k_ref, v_ref, e_ref, r_ref, o_ref, do_ref, dq_ref, dk_ref, dv_ref
):
    blocks = k_ref.shape[0]
    width = q_ref.shape[1]

    def wide(ref):
        return jnp.concatenate([ref[h * HD : (h + 1) * HD] for h in range(GROUP)], axis=1)

    queries = wide(q_ref)
    grads = wide(do_ref).astype(F32) * r_ref[0]
    dots = jnp.sum(grads * wide(o_ref).astype(F32), axis=0, keepdims=True)
    grads = grads.astype(BF16)
    d_queries = jnp.zeros(queries.shape, F32)
    for j in range(blocks):
        raised = e_ref[0, j]
        d_probs = contract(v_ref[j, 0], grads, 0, 0)
        d_scores = (raised.astype(F32) * (d_probs - dots)).astype(BF16)
        d_queries = d_queries + contract(k_ref[j, 0], d_scores, 1, 0)
        dk_ref[j] = contract(queries, d_scores, 1, 1).astype(BF16)
        dv_ref[j] = contract(grads, raised, 1, 1).astype(BF16)
    for h in range(GROUP):
        dq_ref[h * HD : (h + 1) * HD] = d_queries[:, h * width : (h + 1) * width]


def attend(limit, queries, keys_values):
    blocks, _, _, block = keys_values.shape
    width = queries.shape[1]
    wide = GROUP * width
    head_rows = pl.BlockSpec((GROUP * HD, width), lambda g: (g, 0))
    return pl.pallas_call(
        attend_kernel,
        grid=(KV,),
        in_specs=[
            pl.BlockSpec((1, wide), lambda g: (0, 0)),
            head_rows,
            pl.BlockSpec((blocks, 1, HD, block), lambda g: (0, 0, g, 0)),
            pl.BlockSpec((blocks, 1, HD, block), lambda g: (0, 1, g, 0)),
        ],
        out_specs=[
            head_rows,
            pl.BlockSpec((1, blocks, block, wide), lambda g: (g, 0, 0, 0)),
            pl.BlockSpec((1, 1, wide), lambda g: (g, 0, 0)),
        ],
        out_shape=[
            jax.ShapeDtypeStruct(queries.shape, BF16),
            jax.ShapeDtypeStruct((KV, blocks, block, wide), BF16),
            jax.ShapeDtypeStruct((KV, 1, wide), F32),
        ],
        compiler_params=pltpu.CompilerParams(vmem_limit_bytes=40 * 2**20),
        cost_estimate=pl.CostEstimate(
            flops=16 * H * width * blocks * block * HD,
            bytes_accessed=2 * KV * blocks * block * wide,
            transcendentals=H * width * blocks * block,
        ),
        name="attend",
    )(limit, queries, keys_values, keys_values)


def attend_back(queries, keys_values, raised, inverse, mixed, d_mixed):
    blocks, _, features, block = keys_values.shape
    width = queries.shape[1]
    wide = GROUP * width
    head_rows = pl.BlockSpec((GROUP * HD, width), lambda g: (g, 0))
    key_rows = pl.BlockSpec((blocks, HD, block), lambda g: (0, g, 0))
    return pl.pallas_call(
        attend_back_kernel,
        grid=(KV,),
        in_specs=[
            head_rows,
            pl.BlockSpec((blocks, 1, HD, block), lambda g: (0, 0, g, 0)),
            pl.BlockSpec((blocks, 1, HD, block), lambda g: (0, 1, g, 0)),
            pl.BlockSpec((1, blocks, block, wide), lambda g: (g, 0, 0, 0)),
            pl.BlockSpec((1, 1, wide), lambda g: (g, 0, 0)),
            head_rows,
            head_rows,
        ],
        out_specs=[head_rows, key_rows, key_rows],
        out_shape=[
            jax.ShapeDtypeStruct(queries.shape, F32),
            jax.ShapeDtypeStruct((blocks, features, block), BF16),
            jax.ShapeDtypeStruct((blocks, features, block), BF16),
        ],
        compiler_params=pltpu.CompilerParams(vmem_limit_bytes=40 * 2**20),
        cost_estimate=pl.CostEstimate(
            flops=32 * H * width * blocks * block * HD,
            bytes_accessed=2 * KV * blocks * block * wide,
            transcendentals=0,
        ),
        name="attend_back",
    )(queries, keys_values, keys_values, raised, inverse, mixed, d_mixed)


def shards(
    tokens,
    cotangent,
    lengths,
    adapter_ids,
    attn_gain,
    query_gain,
    key_gain,
    ffn_gain,
    w_query,
    w_key,
    w_value,
    w_out,
    gate_weight,
    w_up,
    w_down,
    a_query,
    b_query,
    a_key,
    b_key,
    a_value,
    b_value,
    a_out,
    b_out,
    a_gate,
    b_gate,
    a_up,
    b_up,
    a_down,
    b_down,
):
    n_dp, n_seq = lax.axis_size("dp"), lax.axis_size("seq")
    seq = lax.axis_index("seq")
    _, block, width = tokens.shape
    length = lengths[0]
    positions = seq * block + jnp.arange(block)
    valid = (positions < length).astype(F32)[:, None]

    w_in = everywhere_gather(jnp.concatenate([w_query, w_key, w_value], axis=1))
    w_back = everywhere_gather(w_out)
    order = everywhere_order()
    back_order = jnp.argsort(order)

    def reorder(rows, by):
        return rows.reshape(by.shape[0], -1, rows.shape[-1])[by].reshape(rows.shape)

    def columns_for_seq(matrix):
        rows = matrix.shape[0]
        slots = matrix.reshape(rows, n_dp, n_seq, -1).transpose(2, 0, 1, 3)
        own = seq_exchange(slots.reshape(n_seq, rows, -1))
        return own.reshape(n_seq * rows, -1)

    w_lower = ring_gather(w_down).reshape(-1, width)
    gate_part = ring_gather(columns_for_seq(gate_weight)).reshape(width, -1)
    up_part = ring_gather(columns_for_seq(w_up)).reshape(width, -1)

    shared = (a_query, a_key, a_value, b_query, b_key, b_value, a_out, b_out, a_gate, a_up, b_down)
    own_part = (b_gate, b_up, a_down)
    stack = jnp.concatenate(shared + own_part, axis=1)
    ids = lax.all_gather(adapter_ids, "dp", tiled=True)
    sent = jnp.take(stack, ids, axis=0).transpose(0, 2, 1)
    mine = lax.all_to_all(sent, "dp", 0, 0, tiled=True)
    edges = np.cumsum([0] + [m.shape[1] for m in shared + own_part])
    cut = int(edges[len(shared)])
    spread = seq_gather(mine[..., :cut])
    whole = []
    for i, member in enumerate(shared):
        part = spread[..., edges[i] : edges[i + 1]]
        whole.append(part.transpose(2, 1, 0, 3).reshape(RANK, -1))
    for i, member in enumerate(own_part, len(shared)):
        part = mine[..., edges[i] : edges[i + 1]]
        whole.append(part.transpose(1, 0, 2).reshape(RANK, -1))
    aq, ak, av, bq, bk, bv, ao, bo, ag, au, bd, bg, bu, ad = whole
    a_in = jnp.concatenate([aq, ak, av], axis=0)
    none = lambda m: jnp.zeros_like(m)
    b_in = jnp.concatenate(
        [
            jnp.concatenate([bq, none(bk), none(bv)], axis=1),
            jnp.concatenate([none(bq), bk, none(bv)], axis=1),
            jnp.concatenate([none(bq), none(bk), bv], axis=1),
        ],
        axis=0,
    )
    a_gu = jnp.concatenate([ag, au], axis=0)

    inputs = tokens[0].astype(F32)
    normed = rms_scale(inputs, attn_gain).astype(BF16)
    normed_t = normed.T
    inner = contract(a_in, normed_t, 1, 0).astype(BF16)
    linear = contract(w_in, reorder(normed_t, order), 0, 0) + contract(b_in, inner, 0, 0)
    n_query, n_key = H * HD, KV * HD
    query_lin = linear[:n_query].reshape(H, HD, block)
    key_lin = linear[n_query : n_query + n_key].reshape(KV, HD, block)
    value_lin = linear[n_query + n_key :]
    cosine, sine = rotary_tables(positions)
    scale = HD**-0.5
    query_prep = lambda v: prepare(v, query_gain, cosine, sine)
    key_prep = lambda v: prepare(v, key_gain, cosine, sine)
    queries = (query_prep(query_lin) * scale).astype(BF16).reshape(n_query, block)
    keys = key_prep(key_lin).astype(BF16).reshape(n_key, block)
    keys_values = seq_gather(jnp.stack([keys, value_lin.astype(BF16)]))

    limit = jnp.minimum(positions, length - 1).astype(jnp.int32)
    limit = jnp.tile(limit, GROUP)[None, :]
    mixed, raised, inverse = attend(limit, queries, keys_values)

    inner_out = contract(ao, mixed, 1, 0).astype(BF16)
    update = contract(reorder(mixed, order), w_back, 0, 0) + contract(inner_out, bo, 0, 0)
    hidden = inputs + valid * update
    normed_two = rms_scale(hidden, ffn_gain).astype(BF16)

    cot = cotangent[0].astype(F32)
    n2 = seq_gather(normed_two).reshape(-1, width)
    gf = seq_gather((valid * cot).astype(BF16)).reshape(-1, width)
    inner_gu = contract(n2, a_gu, 1, 1).astype(BF16)
    gate = contract(n2, gate_part, 1, 0) + contract(inner_gu[:, :RANK], bg, 1, 0)
    up = contract(n2, up_part, 1, 0) + contract(inner_gu[:, RANK:], bu, 1, 0)
    d_inner_down = contract(gf, bd, 1, 1).astype(BF16)
    d_act = contract(gf, w_lower, 1, 1) + contract(d_inner_down, ad, 1, 0)
    sig = jax.nn.sigmoid(gate)
    act = (gate * sig * up).astype(BF16)
    d_gate = (d_act * up * sig * (1.0 + gate * (1.0 - sig))).astype(BF16)
    d_up = (d_act * gate * sig).astype(BF16)
    inner_down = contract(act, ad, 1, 1).astype(BF16)
    lowered = contract(act, w_lower, 1, 0) + contract(inner_down, bd, 1, 0)
    lowered = seq_reduce(lowered.reshape(n_seq, block, width))
    output = (hidden + valid * lowered).astype(BF16)

    d_inner_gu = jnp.concatenate(
        [contract(d_gate, bg, 1, 1), contract(d_up, bu, 1, 1)], axis=1
    ).astype(BF16)
    d_n2 = (
        contract(d_gate, gate_part, 1, 1)
        + contract(d_up, up_part, 1, 1)
        + contract(d_inner_gu, a_gu, 1, 0)
    )
    d_n2 = seq_reduce(d_n2.reshape(n_seq, block, width))
    grad_a_gu = contract(d_inner_gu, n2, 0, 0)
    grad_bg = contract(inner_gu[:, :RANK], d_gate, 0, 0)
    grad_bu = contract(inner_gu[:, RANK:], d_up, 0, 0)
    grad_bd = contract(inner_down, gf, 0, 0)
    grad_ad = contract(d_inner_down, act, 0, 0)

    d_hidden = cot + jax.vjp(lambda v: rms_scale(v, ffn_gain), hidden)[1](d_n2)[0]
    grad_update = (valid * d_hidden).astype(BF16)
    d_inner_out = contract(bo, grad_update, 1, 1).astype(BF16)
    d_mixed = reorder(contract(w_back, grad_update, 1, 1), back_order)
    d_mixed = (d_mixed + contract(ao, d_inner_out, 0, 0)).astype(BF16)
    grad_ao = contract(d_inner_out, mixed, 1, 1)
    grad_bo = contract(inner_out, grad_update, 1, 0)

    d_queries, d_keys, d_values = attend_back(
        queries, keys_values, raised, inverse, mixed, d_mixed
    )
    d_kv = seq_reduce(jnp.stack([d_keys, d_values], axis=1))
    d_query_lin = jax.vjp(query_prep, query_lin)[1](d_queries.reshape(H, HD, block) * scale)[0]
    d_key_lin = jax.vjp(key_prep, key_lin)[1](d_kv[0].reshape(KV, HD, block))[0]
    d_linear = jnp.concatenate(
        [d_query_lin.reshape(n_query, block), d_key_lin.reshape(n_key, block), d_kv[1]], axis=0
    ).astype(BF16)
    d_inner = contract(b_in, d_linear, 1, 0).astype(BF16)
    d_normed = reorder(contract(w_in, d_linear, 1, 0), back_order) + contract(a_in, d_inner, 0, 0)
    d_inputs = d_hidden + jax.vjp(lambda v: rms_scale(v, attn_gain), inputs)[1](d_normed.T)[0]
    grad_a_in = contract(d_inner, normed, 1, 0)
    grad_b_in = contract(inner, d_linear, 1, 1)

    q_end, k_end = n_query, n_query + n_key
    partial = (
        grad_a_in[:RANK],
        grad_a_in[RANK : 2 * RANK],
        grad_a_in[2 * RANK :],
        grad_b_in[:RANK, :q_end],
        grad_b_in[RANK : 2 * RANK, q_end:k_end],
        grad_b_in[2 * RANK :, k_end:],
        grad_ao,
        grad_bo,
        grad_a_gu[:RANK],
        grad_a_gu[RANK:],
        grad_bd,
    )
    partial = jnp.concatenate(
        [g.reshape(RANK, n_dp, n_seq, -1).transpose(2, 1, 0, 3) for g in partial], axis=-1
    )
    complete = [g.reshape(RANK, n_dp, -1).transpose(1, 0, 2) for g in (grad_bg, grad_bu, grad_ad)]
    gathered = jnp.concatenate([seq_reduce(partial, F32)] + complete, axis=-1)
    arrived = lax.all_to_all(gathered, "dp", 0, 0, tiled=True)
    chosen = (ids[:, None] == jnp.arange(ADAPT)[None, :]).astype(F32)
    summed = jnp.sum(chosen[:, :, None, None] * arrived[:, None], axis=0).transpose(0, 2, 1)
    parts = [summed[:, edges[i] : edges[i + 1]] for i in range(len(edges) - 1)]
    gaq, gak, gav, gbq, gbk, gbv, gao, gbo, gag, gau, gbd, gbg, gbu, gad = parts
    return (
        output[None],
        d_inputs.astype(BF16)[None],
        gaq,
        gbq,
        gak,
        gbk,
        gav,
        gbv,
        gao,
        gbo,
        gag,
        gbg,
        gau,
        gbu,
        gad,
        gbd,
    )


def solution(mesh):
    tokens = P("dp", "seq", None)
    matrix = P(("dp", "seq"), None)
    stack = P(None, ("dp", "seq"), None)
    in_specs = (tokens, tokens, P("dp"), P("dp")) + (P(),) * 4 + (matrix,) * 7 + (stack,) * 14
    out_specs = (tokens, tokens) + (stack,) * 14
    return jax.shard_map(shards, mesh=mesh, in_specs=in_specs, out_specs=out_specs, check_vma=False)
```

```python
import functools

import jax
import jax.numpy as jnp
import numpy as np
from jax import lax
from jax.experimental import pallas as pl
from jax.experimental.pallas import tpu as pltpu
from jax.sharding import PartitionSpec as P

H = 32
KV = 8
HD = 64
GROUP = H // KV
ADAPT = 8
RANK = 16
EPS = 1e-05
F32 = jnp.float32
BF16 = jnp.bfloat16


def contract(left, right, left_dim, right_dim):
    return lax.dot_general(
        left, right, (((left_dim,), (right_dim,)), ((), ())), preferred_element_type=F32
    )


def rms_scale(operand, scaling, axis=-1):
    mean = jnp.mean(operand * operand, axis=axis, keepdims=True)
    return operand * lax.rsqrt(mean + EPS) * scaling


def rotary_tables(positions):
    frequency = jnp.power(1000000.0, -jnp.arange(HD // 2, dtype=F32) * 2.0 / HD)
    angles = frequency[:, None] * positions.astype(F32)[None, :]
    return jnp.cos(angles), jnp.sin(angles)


def prepare(linear, scaling, cosine, sine):
    normed = rms_scale(linear, scaling[:, None], axis=1)
    front, second = normed[:, : HD // 2], normed[:, HD // 2 :]
    return jnp.concatenate(
        [front * cosine - second * sine, second * cosine + front * sine], axis=1
    )


def after(value, *others):
    return lax.optimization_barrier((value, others))[0]


def ring_order(size):
    return list(range(0, size, 2)) + list(range(1, size, 2))[::-1]


def ring_pairs(size):
    order = ring_order(size)
    right = [(order[i], order[(i + 1) % size]) for i in range(size)]
    return right, [(b, a) for a, b in right]


def ring_offsets():
    offsets = [0]
    for step in range(1, (lax.axis_size("dp") - 1) // 2 + 1):
        offsets += [-step, step]
    return offsets + [lax.axis_size("dp") // 2]


class Ring:
    def __init__(self, own):
        self.pieces = [own]
        self.left = self.right = own
        self.steps = lax.axis_size("dp") // 2

    def complete(self):
        return len(self.pieces) == lax.axis_size("dp")

    def step(self, clock):
        size = lax.axis_size("dp")
        right, left = ring_pairs(size)
        if len(self.pieces) < size - 1:
            self.left = lax.ppermute(clock(self.left), "dp", right)
            self.right = lax.ppermute(clock(self.right), "dp", left)
            self.pieces += [self.left, self.right]
            return self.left, self.right
        half = self.left.shape[0] // 2
        top = lax.ppermute(clock(self.left[:half]), "dp", right)
        bottom = lax.ppermute(clock(self.right[half:]), "dp", left)
        self.pieces.append((top, bottom))
        return top, bottom


def ring_sources():
    size = lax.axis_size("dp")
    here = lax.axis_index("dp")
    place = jnp.where(here % 2 == 0, here // 2, size - 1 - here // 2)
    sources = []
    for offset in ring_offsets():
        at = (place + offset + size) % size
        sources.append(jnp.where(at < size // 2, 2 * at, 2 * (size - 1 - at) + 1).astype(jnp.int32))
    return sources


class Clock:
    def __init__(self):
        self.done = ()

    def tick(self, *done):
        self.done = done

    def __call__(self, value):
        return after(value, self.done) if self.done else value


class Conveyor:
    def __init__(self, clock, ring, waiting):
        self.clock = clock
        self.waiting = list(waiting)
        self.going = [(ring.step(clock), ring)]

    def push(self):
        ring = Ring(self.waiting.pop(0)())
        self.going.append((ring.step(self.clock), ring))
        return ring

    def advance(self, *computed):
        came, ring = self.going.pop(0)
        self.clock.tick(came, *computed)
        if not ring.complete():
            self.going.append((ring.step(self.clock), ring))
        elif self.waiting:
            self.push()

    def until(self, ring, *computed):
        while not ring.complete() or any(r is ring for _, r in self.going):
            self.advance(*computed)


def partner(operand, bit):
    size = lax.axis_size("seq")
    return lax.ppermute(operand, "seq", [(i, i ^ bit) for i in range(size)])


def seq_pieces(own):
    across = partner(own, 2)
    return [own, partner(own, 1), across, partner(across, 1)]


def seq_reduce(keep, give):
    arrived = partner(give, 1)
    sent = (keep[1].astype(F32) + arrived[1].astype(F32)).astype(BF16)
    own = keep[0].astype(F32) + arrived[0].astype(F32)
    return own + partner(sent, 2).astype(F32), sent


def everywhere_order(sources):
    seq = lax.axis_index("seq")
    return jnp.stack([s * 4 + (seq ^ bit) for s in sources for bit in range(4)]).astype(jnp.int32)


VMEM_LIMIT = 56 * 2**20
SMEM = pl.BlockSpec(memory_space=pltpu.SMEM)
VMEM = pl.BlockSpec(memory_space=pltpu.VMEM)


def call(kernel, name, flops=0, moved=0, **options):
    return pl.pallas_call(
        kernel,
        compiler_params=pltpu.CompilerParams(vmem_limit_bytes=VMEM_LIMIT),
        cost_estimate=pl.CostEstimate(flops=0, bytes_accessed=0, transcendentals=0),
        name=name,
        **options,
    )


def shape(dims, dtype):
    return jax.ShapeDtypeStruct(dims, dtype)


def fixed(*dims):
    return pl.BlockSpec(dims, lambda *_: (0,) * len(dims))


def columns_kernel(n_dp, gate_ref, up_ref, *out_refs):
    size = gate_ref.shape[1] // (4 * n_dp)
    for half, out in enumerate(out_refs):
        for m, ref in enumerate((gate_ref, up_ref)):
            for q in range(n_dp // 2):
                place = (m * (n_dp // 2) + q) * size
                for j in range(4):
                    start = ((half * (n_dp // 2) + q) * 4 + j) * size
                    out[j, :, place : place + size] = ref[:, start : start + size]


def columns_for_seq(gate, up, n_dp):
    rows, total = gate.shape
    return call(
        functools.partial(columns_kernel, n_dp),
        "columns",
        moved=8 * rows * total,
        in_specs=[VMEM] * 2,
        out_shape=[shape((4, rows, total // 4), BF16)] * 2,
    )(gate, up)


ANY = pl.BlockSpec(memory_space=pl.ANY)


def place_kernel(sources_ref, *refs):
    pieces, (out_ref, sems) = refs[:-2], refs[-2:]
    copies = []
    for i, piece in enumerate(pieces):
        rows = piece.shape[0]
        start = pl.multiple_of(sources_ref[i] * rows, rows)
        copies.append(pltpu.make_async_copy(piece, out_ref.at[pl.ds(start, rows)], sems.at[i]))
    for copy in copies:
        copy.start()
    for copy in copies:
        copy.wait()


def finish_kernel(source_ref, whole_ref, top_ref, bottom_ref, out_ref, sems):
    rows = top_ref.shape[0]
    copies = []
    for i, piece in enumerate((top_ref, bottom_ref)):
        start = pl.multiple_of(source_ref[0] * (2 * rows), 2 * rows) + i * rows
        copies.append(pltpu.make_async_copy(piece, out_ref.at[pl.ds(start, rows)], sems.at[i]))
    for copy in copies:
        copy.start()
    for copy in copies:
        copy.wait()


def assemble(pieces, sources):
    rows, columns = pieces[0].shape
    most = len(pieces) - 1
    whole = shape(((most + 1) * rows, columns), BF16)
    begun = call(
        place_kernel,
        "place",
        moved=4 * most * rows * columns,
        in_specs=[SMEM] + [VMEM] * most,
        out_specs=ANY,
        out_shape=whole,
        scratch_shapes=[pltpu.SemaphoreType.DMA((most,))],
    )(jnp.stack(sources[:-1]), *pieces[:-1])
    return call(
        finish_kernel,
        "finish",
        moved=4 * rows * columns,
        in_specs=[SMEM, ANY] + [VMEM] * 2,
        out_specs=ANY,
        out_shape=whole,
        scratch_shapes=[pltpu.SemaphoreType.DMA((2,))],
        input_output_aliases={1: 0},
    )(sources[-1][None], begun, *pieces[-1])


def gather_rows(order_ref, source_ref, target_ref, rows):
    total = source_ref.shape[0]
    wide = min(256, total)
    each = wide // rows
    for i in range(total // wide):
        blocks = []
        for j in range(each):
            start = pl.multiple_of(order_ref[i * each + j] * rows, rows)
            blocks.append(source_ref[pl.ds(start, rows), :])
        target_ref[:, i * wide : (i + 1) * wide] = jnp.concatenate(blocks, axis=0).T


def qkv_kernel(order_ref, normed_ref, inner_ref, b_ref, *refs):
    pieces, (out_ref, left_ref) = refs[:-2], refs[-2:]

    @pl.when(pl.program_id(0) == 0)
    def _():
        gather_rows(order_ref, normed_ref, left_ref, pieces[0].shape[0])

    width = pieces[0].shape[1]
    step = 512
    for c in range(0, width, step):
        right = jnp.concatenate([p[:, c : c + step] for p in pieces], axis=0)
        sums = contract(left_ref[...], right, 1, 0)
        sums = sums + contract(inner_ref[...], b_ref[:, c : c + step], 1, 0)
        out_ref[c : c + step, :] = sums.T


def project_in(order, normed_t, inner, b_in, pieces):
    width, tokens = normed_t.shape
    total = b_in.shape[1]
    step = 1024
    rows = pieces[0].shape[0]
    return call(
        qkv_kernel,
        "project_in",
        flops=2 * width * tokens * total,
        moved=2 * width * total,
        grid=(total // step,),
        in_specs=[
            SMEM,
            fixed(width, tokens),
            fixed(*inner.shape),
            pl.BlockSpec((b_in.shape[0], step), lambda c: (0, c)),
        ]
        + [pl.BlockSpec((rows, step), lambda c: (0, c))] * len(pieces),
        out_specs=pl.BlockSpec((step, tokens), lambda c: (c, 0)),
        out_shape=shape((total, tokens), F32),
        scratch_shapes=[pltpu.VMEM((tokens, width), BF16)],
    )(order, normed_t, inner, b_in, *pieces)


def out_kernel(order_ref, mixed_ref, inner_ref, b_ref, tokens_ref, valid_ref, gain_ref, *refs):
    pieces, (hidden_ref, normed_ref, left_ref) = refs[:-3], refs[-3:]
    c = pl.program_id(0)

    @pl.when(c == 0)
    def _():
        gather_rows(order_ref, mixed_ref, left_ref, pieces[0].shape[0])

    width = pieces[0].shape[1]
    right = jnp.concatenate([p[...] for p in pieces], axis=0)
    sums = contract(left_ref[...], right, 1, 0) + contract(inner_ref[...], b_ref[...], 0, 0)
    sums = tokens_ref[...].astype(F32) + valid_ref[...] * sums
    hidden_ref[:, pl.ds(pl.multiple_of(c * width, width), width)] = sums

    @pl.when(c == pl.num_programs(0) - 1)
    def _():
        hidden = hidden_ref[...]
        normed_ref[...] = rms_scale(hidden, gain_ref[...]).astype(BF16)


def project_out(order, mixed, inner, bo, tokens, valid, gain, pieces):
    features, block = mixed.shape
    width = tokens.shape[1]
    step = 1024
    rows = pieces[0].shape[0]
    skip = (pieces[0].shape[1] - width) // step
    return call(
        out_kernel,
        "project_out",
        flops=2 * features * block * width,
        moved=2 * features * width,
        grid=(width // step,),
        in_specs=[
            SMEM,
            fixed(features, block),
            fixed(*inner.shape),
            pl.BlockSpec((RANK, step), lambda c: (0, c)),
            pl.BlockSpec((block, step), lambda c: (0, c)),
            fixed(block, 1),
            fixed(1, width),
        ]
        + [pl.BlockSpec((rows, step), lambda c: (0, c + skip))] * len(pieces),
        out_specs=[fixed(block, width), fixed(block, width)],
        out_shape=[shape((block, width), F32), shape((block, width), BF16)],
        scratch_shapes=[pltpu.VMEM((block, features), BF16)],
    )(order, mixed, inner, bo, tokens, valid, gain, *pieces)


def scatter_products(order_ref, pieces, right, sums_ref, form):
    rows = pieces[0].shape[0]
    each = max(1, 256 // rows)
    for i in range(0, len(pieces), each):
        left = jnp.concatenate([p[...] for p in pieces[i : i + each]], axis=0)
        product = contract(left, right, 1, form)
        for j in range(each):
            start = pl.multiple_of(order_ref[i + j] * rows, rows)
            sums_ref[pl.ds(start, rows), :] += product[j * rows : (j + 1) * rows]


def out_back_kernel(order_ref, grad_ref, a_ref, inner_ref, *refs):
    pieces, (out_ref, sums_ref) = refs[:-2], refs[-2:]
    c = pl.program_id(0)

    @pl.when(c == 0)
    def _():
        sums_ref[...] = contract(a_ref[...], inner_ref[...], 0, 1)

    scatter_products(order_ref, pieces, grad_ref[...], sums_ref, 1)

    @pl.when(c == pl.num_programs(0) - 1)
    def _():
        out_ref[...] = sums_ref[...].astype(BF16)


def project_out_back(order, grad, ao, d_inner, pieces):
    block, width = grad.shape
    features = ao.shape[1]
    step = 1024
    rows = pieces[0].shape[0]
    skip = (pieces[0].shape[1] - width) // step
    return call(
        out_back_kernel,
        "project_out_back",
        flops=2 * features * block * width,
        moved=2 * features * width,
        grid=(width // step,),
        in_specs=[
            SMEM,
            pl.BlockSpec((block, step), lambda c: (0, c)),
            fixed(*ao.shape),
            fixed(*d_inner.shape),
        ]
        + [pl.BlockSpec((rows, step), lambda c: (0, c + skip))] * len(pieces),
        out_specs=fixed(features, block),
        out_shape=shape((features, block), BF16),
        scratch_shapes=[pltpu.VMEM((features, block), F32)],
    )(order, grad, ao, d_inner, *pieces)


def in_back_kernel(order_ref, grad_ref, a_ref, inner_ref, tokens_ref, gain_ref, base_ref, *refs):
    pieces, (out_ref, sums_ref, turned_ref) = refs[:-3], refs[-3:]
    c = pl.program_id(0)

    @pl.when(c == 0)
    def _():
        sums_ref[...] = contract(a_ref[...], inner_ref[...], 0, 0)

    scatter_products(order_ref, pieces, grad_ref[...], sums_ref, 0)

    @pl.when(c == pl.num_programs(0) - 1)
    def _():
        size = sums_ref.shape[1]
        for i in range(0, sums_ref.shape[0], size):
            turned_ref[:, i : i + size] = sums_ref[i : i + size, :].T
        inputs = tokens_ref[...].astype(F32)
        grad = turned_ref[...] * gain_ref[...]
        scale = lax.rsqrt(jnp.mean(inputs * inputs, axis=-1, keepdims=True) + EPS)
        along = jnp.mean(inputs * grad, axis=-1, keepdims=True) * scale * scale
        out_ref[...] = (base_ref[...] + scale * (grad - inputs * along)).astype(BF16)


def project_in_back(order, d_linear, a_in, d_inner, tokens, gain, base, pieces):
    total, block = d_linear.shape
    width = tokens.shape[1]
    step = 1024
    rows = pieces[0].shape[0]
    return call(
        in_back_kernel,
        "project_in_back",
        flops=2 * total * block * width,
        moved=2 * total * width,
        grid=(total // step,),
        in_specs=[
            SMEM,
            pl.BlockSpec((step, block), lambda c: (c, 0)),
            fixed(*a_in.shape),
            fixed(*d_inner.shape),
            fixed(block, width),
            fixed(1, width),
            fixed(block, width),
        ]
        + [pl.BlockSpec((rows, step), lambda c: (0, c))] * len(pieces),
        out_specs=fixed(block, width),
        out_shape=shape((block, width), BF16),
        scratch_shapes=[pltpu.VMEM((width, block), F32), pltpu.VMEM((block, width), F32)],
    )(order, d_linear, a_in, d_inner, tokens, gain, base, *pieces)


def gather_tokens(refs, whole_ref):
    block = refs[0].shape[0]
    for i, ref in enumerate(refs):
        whole_ref[i * block : (i + 1) * block, :] = ref[...]


def lower_back_kernel(g0, g1, g2, g3, weight_ref, b_ref, a_ref, out_ref, inner_ref, whole_ref):
    @pl.when(pl.program_id(0) == 0)
    def _():
        gather_tokens((g0, g1, g2, g3), whole_ref)
        inner_ref[...] = contract(whole_ref[...], b_ref[...], 1, 1).astype(BF16)

    sums = contract(whole_ref[...], weight_ref[...], 1, 1)
    out_ref[...] = (sums + contract(inner_ref[...], a_ref[...], 1, 0)).astype(BF16)


def lower_back(grads, weight, bd, ad):
    block, width = grads[0].shape
    units = weight.shape[0]
    step = 256
    tokens = 4 * block
    return call(
        lower_back_kernel,
        "lower_back",
        flops=2 * tokens * width * units,
        moved=2 * width * units,
        grid=(units // step,),
        in_specs=[fixed(block, width)] * 4
        + [
            pl.BlockSpec((step, width), lambda j: (j, 0)),
            fixed(RANK, width),
            pl.BlockSpec((RANK, step), lambda j: (0, j)),
        ],
        out_specs=[pl.BlockSpec((tokens, step), lambda j: (0, j)), fixed(tokens, RANK)],
        out_shape=[shape((tokens, units), BF16), shape((tokens, RANK), BF16)],
        scratch_shapes=[pltpu.VMEM((tokens, width), BF16)],
    )(*grads, weight, bd, ad)


def tokens_kernel(n0, n1, n2, n3, a_ref, whole_ref, low_ref):
    gather_tokens((n0, n1, n2, n3), whole_ref)
    low_ref[...] = contract(whole_ref[...], a_ref[...], 1, 1).astype(BF16)


def all_tokens(normed, a_gu):
    block, width = normed[0].shape
    return call(
        tokens_kernel,
        "all_tokens",
        flops=16 * block * width * RANK,
        moved=16 * block * width,
        out_shape=[shape((4 * block, width), BF16), shape((4 * block, 2 * RANK), BF16)],
    )(*normed, a_gu)


def units_kernel(
    whole_ref,
    low_ref,
    gate_ref,
    up_ref,
    bg_ref,
    bu_ref,
    ad_ref,
    d_act_ref,
    act_ref,
    dg_ref,
    du_ref,
    inner_ref,
):
    @pl.when(pl.program_id(0) == 0)
    def _():
        inner_ref[...] = jnp.zeros(inner_ref.shape, F32)

    low_gate, low_up = low_ref[:, :RANK], low_ref[:, RANK:]
    gate = contract(whole_ref[...], gate_ref[...], 1, 0) + contract(low_gate, bg_ref[...], 1, 0)
    up = contract(whole_ref[...], up_ref[...], 1, 0) + contract(low_up, bu_ref[...], 1, 0)
    d_act = d_act_ref[...].astype(F32)
    sig = jax.nn.sigmoid(gate)
    silu = gate * sig
    act = (silu * up).astype(BF16)
    d_gate = (d_act * up * (sig + silu * (1.0 - sig))).astype(BF16)
    d_up = (d_act * silu).astype(BF16)
    act_ref[...] = act
    dg_ref[...] = d_gate
    du_ref[...] = d_up
    inner_ref[:, :RANK] += contract(d_gate, bg_ref[...], 1, 1)
    inner_ref[:, RANK : 2 * RANK] += contract(d_up, bu_ref[...], 1, 1)
    inner_ref[:, 2 * RANK :] += contract(act, ad_ref[...], 1, 1)


def units(part, whole, low, both, bg, bu, ad, d_act):
    tokens, width = whole.shape
    half = both.shape[1] // 2
    step = 256
    steps = half // step
    here = pl.BlockSpec((RANK, step), lambda j: (0, part * steps + j))
    tile = pl.BlockSpec((tokens, step), lambda j: (0, j))
    return call(
        units_kernel,
        "units",
        flops=4 * tokens * width * half,
        moved=4 * width * half,
        grid=(steps,),
        in_specs=[
            fixed(tokens, width),
            fixed(tokens, 2 * RANK),
            pl.BlockSpec((width, step), lambda j: (0, j)),
            pl.BlockSpec((width, step), lambda j: (0, steps + j)),
            here,
            here,
            here,
            pl.BlockSpec((tokens, step), lambda j: (0, part * steps + j)),
        ],
        out_specs=[tile] * 3 + [fixed(tokens, 3 * RANK)],
        out_shape=[shape((tokens, half), BF16)] * 3 + [shape((tokens, 3 * RANK), F32)],
    )(whole, low, both, both, bg, bu, ad, d_act)


def units_grads_kernel(low_ref, d_down_ref, act_ref, dg_ref, du_ref, gbg_ref, gbu_ref, gad_ref):
    gbg_ref[...] = contract(low_ref[:, :RANK], dg_ref[...], 0, 0)
    gbu_ref[...] = contract(low_ref[:, RANK:], du_ref[...], 0, 0)
    gad_ref[...] = contract(d_down_ref[...], act_ref[...], 0, 0)


def units_grads(low, d_down, act, d_gate, d_up):
    tokens, half = act.shape
    step = 256
    tile = pl.BlockSpec((tokens, step), lambda j: (0, j))
    thin = pl.BlockSpec((RANK, step), lambda j: (0, j))
    return call(
        units_grads_kernel,
        "units_grads",
        flops=6 * tokens * half * RANK,
        moved=6 * tokens * half,
        grid=(half // step,),
        in_specs=[fixed(tokens, 2 * RANK), fixed(tokens, RANK), tile, tile, tile],
        out_specs=[thin] * 3,
        out_shape=[shape((RANK, half), F32)] * 3,
    )(low, d_down, act, d_gate, d_up)


def units_back_first_kernel(g_ref, u_ref, w_ref, out_ref):
    half = g_ref.shape[1]
    sums = contract(g_ref[...], w_ref[:, :half], 1, 1) + contract(u_ref[...], w_ref[:, half:], 1, 1)
    out_ref[...] = sums.astype(BF16)


def units_back_first(d_gate, d_up, both):
    tokens, half = d_gate.shape
    width = both.shape[0]
    step = 256
    return call(
        units_back_first_kernel,
        "units_back_first",
        flops=4 * tokens * half * width,
        moved=4 * half * width,
        grid=(width // step,),
        in_specs=[fixed(tokens, half)] * 2 + [pl.BlockSpec((step, 2 * half), lambda n: (n, 0))],
        out_specs=pl.BlockSpec((tokens, step), lambda n: (0, n)),
        out_shape=shape((tokens, width), BF16),
    )(d_gate, d_up, both)


def units_back_kernel(first_ref, g_ref, u_ref, w_ref, low_ref, a_ref, keep_ref, give_ref):
    half = g_ref.shape[1]
    sums = first_ref[...].astype(F32) + contract(low_ref[...], a_ref[...], 1, 0)
    sums = sums + contract(g_ref[...], w_ref[:, :half], 1, 1)
    sums = sums + contract(u_ref[...], w_ref[:, half:], 1, 1)
    sums = sums.astype(BF16)
    block = keep_ref.shape[1]
    keep_ref[0] = sums[:block]
    give_ref[0] = sums[block : 2 * block]
    keep_ref[1] = sums[2 * block : 3 * block]
    give_ref[1] = sums[3 * block :]


def units_back(part, parts, first, d_gate, d_up, both, low, a_gu):
    tokens, half = d_gate.shape
    width = both.shape[0]
    step = 256
    steps = width // parts // step
    place = lambda n: part * steps + n
    out = pl.BlockSpec((2, tokens // 4, step), lambda n: (0, 0, n))
    return call(
        units_back_kernel,
        "units_back",
        flops=4 * tokens * half * width // parts,
        moved=4 * half * width // parts,
        grid=(steps,),
        in_specs=[
            pl.BlockSpec((tokens, step), lambda n: (0, place(n))),
            fixed(tokens, half),
            fixed(tokens, half),
            pl.BlockSpec((step, 2 * half), lambda n: (place(n), 0)),
            fixed(tokens, 2 * RANK),
            pl.BlockSpec((2 * RANK, step), lambda n: (0, place(n))),
        ],
        out_specs=[out, out],
        out_shape=[shape((2, tokens // 4, width // parts), BF16)] * 2,
    )(first, d_gate, d_up, both, low, a_gu)


def lower_kernel(
    aa_ref, ab_ref, weight_ref, low_ref, b_ref, whole_ref, lowgu_ref, g0, g1, g2, g3, keep_ref, give_ref, grad_ref, grad_gu_ref
):
    half = aa_ref.shape[1]
    sums = contract(low_ref[...], b_ref[...], 1, 0)
    sums = sums + contract(aa_ref[...], weight_ref[:half], 1, 0)
    sums = sums + contract(ab_ref[...], weight_ref[half:], 1, 0)
    sums = sums.astype(BF16)
    block = g0.shape[0]
    low = low_ref[...]
    grad = jnp.zeros(grad_ref.shape, F32)
    for i, g in enumerate((g0, g1, g2, g3)):
        out = give_ref if i % 2 else keep_ref
        out[i // 2] = sums[i * block : (i + 1) * block]
        grad = grad + contract(low[i * block : (i + 1) * block], g[...], 0, 0)
    grad_ref[...] = grad
    grad_gu_ref[...] = contract(lowgu_ref[...], whole_ref[...], 0, 0)


def lower(act_a, act_b, weight, low, bd, grads, whole, low_gu):
    block, width = grads[0].shape
    tokens, half = act_a.shape
    step = 256
    tile = pl.BlockSpec((block, step), lambda n: (0, n))
    thin = pl.BlockSpec((RANK, step), lambda n: (0, n))
    out = pl.BlockSpec((2, block, step), lambda n: (0, 0, n))
    return call(
        lower_kernel,
        "lower",
        flops=4 * tokens * half * width,
        moved=4 * half * width,
        grid=(width // step,),
        in_specs=[
            fixed(tokens, half),
            fixed(tokens, half),
            pl.BlockSpec((2 * half, step), lambda n: (0, n)),
            fixed(tokens, RANK),
            thin,
            pl.BlockSpec((tokens, step), lambda n: (0, n)),
            fixed(tokens, 2 * RANK),
        ]
        + [tile] * 4,
        out_specs=[out, out, thin, pl.BlockSpec((2 * RANK, step), lambda n: (0, n))],
        out_shape=[shape((2, block, width), BF16)] * 2
        + [shape((RANK, width), F32), shape((2 * RANK, width), F32)],
    )(act_a, act_b, weight, low, bd, whole, low_gu, *grads)


def wide_heads(ref):
    return jnp.concatenate([ref[h * HD : (h + 1) * HD] for h in range(GROUP)], axis=1)


def attend_kernel(seq_ref, limit_ref, q_ref, kv0, kv1, kv2, kv3, o_ref, e_ref, r_ref):
    queries = wide_heads(q_ref)
    limit = limit_ref[...]
    total = jnp.zeros(limit.shape, F32)
    mixed = jnp.zeros(queries.shape, F32)
    for bit, ref in enumerate((kv0, kv1, kv2, kv3)):
        block = ref.shape[2]
        scores = contract(ref[0, :HD], queries, 0, 0)
        places = (seq_ref[0] ^ bit) * block + lax.broadcasted_iota(jnp.int32, scores.shape, 0)
        raised = jnp.where(places <= limit, jnp.exp(scores), 0.0)
        total = total + jnp.sum(raised, axis=0, keepdims=True)
        low = raised.astype(BF16)
        e_ref[0, bit] = low
        mixed = mixed + contract(ref[0, HD:], low, 1, 0)
    inverse = 1.0 / total
    r_ref[0] = inverse
    mixed = (mixed * inverse).astype(BF16)
    width = q_ref.shape[1]
    for h in range(GROUP):
        o_ref[h * HD : (h + 1) * HD] = mixed[:, h * width : (h + 1) * width]


def attend(seq, limit, queries, keys_values):
    block = keys_values[0].shape[2]
    width = queries.shape[1]
    wide = GROUP * width
    head_rows = pl.BlockSpec((GROUP * HD, width), lambda g: (g, 0))
    return call(
        attend_kernel,
        "attend",
        flops=16 * H * width * 4 * block * HD,
        moved=2 * KV * 4 * block * wide,
        grid=(KV,),
        in_specs=[SMEM, fixed(1, wide), head_rows]
        + [pl.BlockSpec((1, 2 * HD, block), lambda g: (g, 0, 0))] * 4,
        out_specs=[
            head_rows,
            pl.BlockSpec((1, 4, block, wide), lambda g: (g, 0, 0, 0)),
            pl.BlockSpec((1, 1, wide), lambda g: (g, 0, 0)),
        ],
        out_shape=[
            shape(queries.shape, BF16),
            shape((KV, 4, block, wide), BF16),
            shape((KV, 1, wide), F32),
        ],
    )(seq[None], limit, queries, *keys_values)


def attend_back_kernel(q_ref, kv0, kv1, kv2, kv3, e_ref, r_ref, o_ref, do_ref, dq_ref, keep_ref, give_ref):
    width = q_ref.shape[1]
    queries = wide_heads(q_ref)
    grads = wide_heads(do_ref).astype(F32) * r_ref[0]
    dots = jnp.sum(grads * wide_heads(o_ref).astype(F32), axis=0, keepdims=True)
    grads = grads.astype(BF16)
    d_queries = jnp.zeros(queries.shape, F32)
    for bit, ref in enumerate((kv0, kv1, kv2, kv3)):
        out = give_ref if bit % 2 else keep_ref
        raised = e_ref[0, bit]
        d_probs = contract(ref[0, HD:], grads, 0, 0)
        d_scores = (raised.astype(F32) * (d_probs - dots)).astype(BF16)
        d_queries = d_queries + contract(ref[0, :HD], d_scores, 1, 0)
        out[bit // 2, 0, :HD] = contract(queries, d_scores, 1, 1).astype(BF16)
        out[bit // 2, 0, HD:] = contract(grads, raised, 1, 1).astype(BF16)
    for h in range(GROUP):
        dq_ref[h * HD : (h + 1) * HD] = d_queries[:, h * width : (h + 1) * width]


def attend_back(first, count, queries, keys_values, raised, inverse, mixed, d_mixed):
    block = keys_values[0].shape[2]
    width = queries.shape[1]
    wide = GROUP * width
    head_rows = pl.BlockSpec((GROUP * HD, width), lambda g: (first + g, 0))
    shares = pl.BlockSpec((2, 1, 2 * HD, block), lambda g: (0, g, 0, 0))
    return call(
        attend_back_kernel,
        "attend_back",
        flops=32 * count * GROUP * width * 4 * block * HD,
        moved=2 * count * 4 * block * wide,
        grid=(count,),
        in_specs=[head_rows]
        + [pl.BlockSpec((1, 2 * HD, block), lambda g: (first + g, 0, 0))] * 4
        + [
            pl.BlockSpec((1, 4, block, wide), lambda g: (first + g, 0, 0, 0)),
            pl.BlockSpec((1, 1, wide), lambda g: (first + g, 0, 0)),
            head_rows,
            head_rows,
        ],
        out_specs=[pl.BlockSpec((GROUP * HD, width), lambda g: (g, 0)), shares, shares],
        out_shape=[
            shape((count * GROUP * HD, width), F32),
            shape((2, count, 2 * HD, block), BF16),
            shape((2, count, 2 * HD, block), BF16),
        ],
    )(queries, *keys_values, raised, inverse, mixed, d_mixed)


def pick_kernel(ids_ref, *refs):
    out_ref = refs[-1]
    for d in range(out_ref.shape[0]):
        parts = [ref[ids_ref[d]] for ref in refs[:-1]]
        out_ref[d] = jnp.concatenate(parts, axis=1)


def pick(ids, stacks):
    columns = sum(stack.shape[2] for stack in stacks)
    n_dp = ids.shape[0]
    return call(
        pick_kernel,
        "pick",
        moved=4 * n_dp * RANK * columns,
        in_specs=[SMEM] + [VMEM] * len(stacks),
        out_shape=shape((n_dp, RANK, columns), BF16),
    )(ids, *stacks)


def spread_kernel(widths, seq_ref, mine_ref, p1, p2, p3, *refs):
    (in_ref, grow_ref, ao_ref, bo_ref, gu_ref, bd_ref, bg_ref, bu_ref, ad_ref, all_ref) = refs
    local, each, thin = widths
    n_dp = mine_ref.shape[0]
    seq = seq_ref[0]
    base = 3 * local
    all_ref[seq] = mine_ref[:, :, base:]
    for bit, ref in ((1, p1), (2, p2), (3, p3)):
        all_ref[seq ^ bit] = ref[...]

    def factor(start, width):
        parts = [all_ref[j, d, :, start : start + width] for d in range(n_dp) for j in range(4)]
        return jnp.concatenate(parts, axis=1)

    wide = lambda m: factor(m * each, each)
    for i in range(3):
        in_ref[i * RANK : (i + 1) * RANK] = wide(i)
    grow_ref[...] = jnp.zeros(grow_ref.shape, BF16)
    n_query, n_key = 4 * n_dp * each, 4 * n_dp * thin
    grow_ref[:RANK, :n_query] = wide(3)
    for i in range(2):
        start = n_query + i * n_key
        grow_ref[(i + 1) * RANK : (i + 2) * RANK, start : start + n_key] = factor(9 * each + i * thin, thin)
    ao_ref[...] = wide(4)
    bo_ref[...] = wide(5)
    gu_ref[:RANK] = wide(6)
    gu_ref[RANK:] = wide(7)
    bd_ref[...] = wide(8)
    for i, ref in enumerate((bg_ref, bu_ref, ad_ref)):
        for d in range(n_dp):
            ref[:, d * local : (d + 1) * local] = mine_ref[d, :, i * local : (i + 1) * local]


def spread(seq, mine, others, widths):
    local, each, thin = widths
    n_dp = mine.shape[0]
    total = 4 * n_dp * each
    grown = total + 8 * n_dp * thin
    rows = [(3 * RANK, total), (3 * RANK, grown), (RANK, total), (RANK, total), (2 * RANK, total), (RANK, total)]
    rows += [(RANK, n_dp * local)] * 3
    return call(
        functools.partial(spread_kernel, widths),
        "spread",
        moved=4 * 4 * mine.size,
        in_specs=[SMEM] + [VMEM] * 4,
        out_shape=[shape(dims, BF16) for dims in rows],
        scratch_shapes=[pltpu.VMEM((4,) + others[0].shape, BF16)],
    )(seq[None], mine, *others)


def pack_kernel(n_dp, count, seq_ref, *refs):
    ins, (keep_ref, give_ref, all_ref) = refs[:count], refs[count:]
    for d in range(n_dp):
        for j in range(4):
            parts = []
            for ref in ins:
                each = ref.shape[1] // (4 * n_dp)
                at = (d * 4 + j) * each
                parts.append(ref[:, at : at + each])
            all_ref[j, d] = jnp.concatenate(parts, axis=1)
    seq = seq_ref[0]
    for bit in range(4):
        out = give_ref if bit % 2 else keep_ref
        out[bit // 2] = all_ref[seq ^ bit]


def pack(seq, grads, n_dp):
    columns = sum(g.shape[1] for g in grads) // (4 * n_dp)
    dims = (n_dp, RANK, columns)
    return call(
        functools.partial(pack_kernel, n_dp, len(grads)),
        "pack",
        moved=16 * n_dp * RANK * columns * 4,
        in_specs=[SMEM] + [VMEM] * len(grads),
        out_shape=[shape((2,) + dims, F32)] * 2,
        scratch_shapes=[pltpu.VMEM((4,) + dims, F32)],
    )(seq[None], *grads)


def sort_kernel(widths, ids_ref, came_ref, *out_refs):
    came = [came_ref[d] for d in range(came_ref.shape[0])]
    for a in range(ADAPT):
        total = jnp.zeros(came[0].shape, F32)
        for d, value in enumerate(came):
            total = total + jnp.where(ids_ref[d] == a, value, 0.0)
        at = 0
        for ref, width in zip(out_refs, widths):
            ref[a] = total[:, at : at + width]
            at += width


def sort(ids, came, widths):
    outs = call(
        functools.partial(sort_kernel, widths),
        "sort",
        moved=8 * came.size,
        in_specs=[SMEM, VMEM],
        out_shape=[shape((ADAPT, RANK, w), F32) for w in widths],
    )(ids, came)
    return [o.transpose(0, 2, 1) for o in outs]


def shards(
    tokens,
    cotangent,
    lengths,
    adapter_ids,
    attn_gain,
    query_gain,
    key_gain,
    ffn_gain,
    w_query,
    w_key,
    w_value,
    w_out,
    gate_weight,
    w_up,
    w_down,
    a_query,
    b_query,
    a_key,
    b_key,
    a_value,
    b_value,
    a_out,
    b_out,
    a_gate,
    b_gate,
    a_up,
    b_up,
    a_down,
    b_down,
):
    n_dp = lax.axis_size("dp")
    seq = lax.axis_index("seq")
    _, block, width = tokens.shape
    length = lengths[0]
    positions = seq * block + jnp.arange(block)
    valid = (positions < length).astype(F32)[:, None]
    sources = ring_sources()
    clock = Clock()
    n_query, n_key = H * HD, KV * HD
    local, each, thin = b_gate.shape[1], a_query.shape[1], b_key.shape[1]
    widths = (local, each, thin)

    attn = Ring(jnp.concatenate([w_query, w_key, w_value, w_out], axis=1))
    sides, acrosses, corners = [], [], []

    def share(piece):
        sides.append(partner(clock(piece), 1))
        acrosses.append(partner(clock(piece), 2))

    def pass_on(count):
        for _ in range(count):
            corners.append(partner(clock(acrosses[len(corners)]), 1))

    came = attn.step(clock)
    share(attn.pieces[0])
    ids = lax.all_to_all(
        jnp.broadcast_to(adapter_ids[None], (n_dp, 128)), "dp", 0, 0, tiled=True
    )[:, 0]
    slots_a, slots_b = columns_for_seq(gate_weight, w_up, n_dp)
    inputs = tokens[0].astype(F32)
    normed = rms_scale(inputs, attn_gain).astype(BF16)
    cot = cotangent[0].astype(F32)
    grad_out = (valid * cot).astype(BF16)
    stacks = (b_gate, b_up, a_down, a_query, a_key, a_value, b_query, a_out, b_out)
    stacks += (a_gate, a_up, b_down, b_key, b_value)
    ids = after(ids, slots_a, normed, grad_out)
    sent = pick(ids, [m.transpose(0, 2, 1) for m in stacks])
    clock.tick(came, slots_a, slots_b, normed, grad_out, sent)

    came = attn.step(clock)
    share(attn.pieces[1])
    share(attn.pieces[2])
    mine = lax.all_to_all(clock(sent), "dp", 0, 0, tiled=True)
    normed_t = clock(normed).T
    clock.tick(came, normed_t)

    came = attn.step(clock)
    share(attn.pieces[3])
    share(attn.pieces[4])
    swap = lambda slots: lax.all_to_all(clock(slots), "seq", 0, 0, tiled=True)
    swapped_a = swap(slots_a)
    mine = clock(mine)
    others = seq_pieces(mine[..., 3 * local :])[1:]
    pass_on(1)
    clock.tick(came)
    while len(attn.pieces) < n_dp - 1:
        came = attn.step(clock)
        share(attn.pieces[-4])
        share(attn.pieces[-3])
        clock.tick(came)

    came = attn.step(clock)
    lower_ring = Ring(w_down)
    belt = Conveyor(clock, lower_ring, [lambda: clock(swapped_a).reshape(-1, width), lambda: clock(swapped_b).reshape(-1, width)])
    share(attn.pieces[-3])
    share(attn.pieces[-2])
    clock.tick(came)
    attn.pieces.append(jnp.concatenate(attn.pieces.pop(), axis=0))
    share(attn.pieces[-1])
    pass_on(3)
    belt.advance()
    ring_a = belt.push()
    swapped_b = swap(slots_b)
    pass_on(2)
    order = everywhere_order(sources)
    a_in, b_in, ao, bo, a_gu, bd, bg, bu, ad = spread(seq, *clock((mine, others)), widths)
    inner = contract(clock(normed), a_in, 1, 1).astype(BF16)
    belt.advance(inner)
    pass_on(2)
    belt.advance()
    pass_on(len(acrosses) - len(corners))
    attn_pieces = []
    for group in zip(attn.pieces, sides, acrosses, corners):
        attn_pieces += group

    linear = project_in(order, normed_t, inner, b_in, attn_pieces)
    query_lin = linear[:n_query].reshape(H, HD, block)
    key_lin = linear[n_query : n_query + n_key].reshape(KV, HD, block)
    value_lin = linear[n_query + n_key :].reshape(KV, HD, block)
    cosine, sine = rotary_tables(positions)
    scale = HD**-0.5
    query_prep = lambda v: prepare(v, query_gain, cosine, sine)
    key_prep = lambda v: prepare(v, key_gain, cosine, sine)
    keys_values = jnp.concatenate([key_prep(key_lin), value_lin], axis=1).astype(BF16)
    belt.advance(keys_values)
    keys_values = seq_pieces(clock(keys_values))
    queries = (query_prep(clock(query_lin)) * scale).astype(BF16).reshape(n_query, block)
    limit = jnp.minimum(positions, length - 1).astype(jnp.int32)
    limit = jnp.tile(limit, GROUP)[None, :]
    belt.advance(queries)
    grads = seq_pieces(after(clock(grad_out), keys_values[0], keys_values[2]))
    mixed, raised, inverse = attend(seq, limit, clock(queries), keys_values)

    belt.until(lower_ring, mixed)
    w_lower = assemble(clock(lower_ring.pieces), sources)
    inner_out = contract(ao, clock(mixed), 1, 0).astype(BF16)
    hidden, normed_two = project_out(
        order, clock(mixed), inner_out, bo, tokens[0], valid, ffn_gain[None], attn_pieces
    )
    belt.advance(normed_two)

    n2 = seq_pieces(clock(normed_two))
    d_act, d_down = lower_back(grads, clock(w_lower), bd, ad)
    belt.until(ring_a, d_act)
    ring_b = belt.going[-1][1]
    n2, low_n2 = all_tokens(clock(n2), a_gu)
    both_a = assemble(clock(ring_a.pieces), sources)
    act_a, dg_a, du_a, inner_a = units(0, n2, low_n2, both_a, bg, bu, ad, d_act)
    belt.advance(act_a)
    first = units_back_first(clock(dg_a), du_a, both_a)
    belt.advance(first)
    gbg_a, gbu_a, gad_a = units_grads(low_n2, d_down, clock(act_a), dg_a, du_a)
    belt.until(ring_b, gbg_a)
    both_b = assemble(clock(ring_b.pieces), sources)
    act_b, dg_b, du_b, inner_b = units(1, n2, low_n2, both_b, bg, bu, ad, d_act)
    low = (inner_a + inner_b).astype(BF16)
    low_gu, low_down = low[:, : 2 * RANK], low[:, 2 * RANK :]
    d_n2, parts = [], 2
    for part in range(parts):
        keep, give = units_back(part, parts, first, dg_b, du_b, both_b, low_gu, a_gu)
        first = after(first, keep)
        reduced, sent = seq_reduce(keep, give)
        d_n2.append(reduced)
    d_n2 = jnp.concatenate(d_n2, axis=1)

    act_b = after(act_b, sent)
    gbg_b, gbu_b, gad_b = units_grads(low_n2, d_down, act_b, dg_b, du_b)
    keep, give, grad_bd, grad_a_gu = lower(act_a, act_b, w_lower, low_down, bd, grads, n2, low_gu)
    lowered, _ = seq_reduce(keep, give)
    output = (hidden + valid * lowered).astype(BF16)

    d_hidden = cot + jax.vjp(lambda v: rms_scale(v, ffn_gain), hidden)[1](d_n2)[0]
    grad_update = (valid * d_hidden).astype(BF16)
    d_inner_out = contract(grad_update, bo, 1, 1).astype(BF16)
    d_mixed = project_out_back(order, grad_update, ao, d_inner_out, attn_pieces)
    d_queries, d_kv = [], []
    for part in range(2):
        count = KV // 2
        d_query, keep, give = attend_back(
            part * count, count, queries, keys_values, raised, inverse, mixed, d_mixed
        )
        d_kv.append(seq_reduce(keep, give)[0])
        d_queries.append(d_query)
    d_queries = jnp.concatenate(d_queries, axis=0).reshape(H, HD, block) * scale
    d_kv = jnp.concatenate(d_kv, axis=0)
    d_query_lin = jax.vjp(query_prep, query_lin)[1](d_queries)[0]
    d_key_lin = jax.vjp(key_prep, key_lin)[1](d_kv[:, :HD])[0]
    d_linear = jnp.concatenate(
        [
            d_query_lin.reshape(n_query, block),
            d_key_lin.reshape(n_key, block),
            d_kv[:, HD:].reshape(n_key, block),
        ],
        axis=0,
    ).astype(BF16)
    d_inner = contract(b_in, d_linear, 1, 0).astype(BF16)
    grad_tokens = project_in_back(
        order, d_linear, a_in, d_inner, tokens[0], attn_gain[None], d_hidden, attn_pieces
    )

    def owners(grads, alone):
        keep, give = pack(seq, grads, n_dp)
        both = keep + partner(give, 1)
        summed = both[0] + partner(both[1], 2)
        sizes = [g.shape[1] // (4 * n_dp) for g in grads]
        if alone:
            summed = jnp.concatenate([summed] + alone, axis=2)
            sizes += [g.shape[2] for g in alone]
        return sort(ids, lax.all_to_all(summed, "dp", 0, 0, tiled=True), sizes)

    grad_ao = contract(d_inner_out, mixed, 0, 1)
    grad_bo = contract(inner_out, grad_update, 1, 0)
    cat = lambda a, b: jnp.concatenate([a, b], axis=1).reshape(RANK, n_dp, -1).transpose(1, 0, 2)
    gao, gbo, gag, gau, gbd, gbg, gbu, gad = owners(
        [grad_ao, grad_bo, grad_a_gu[:RANK], grad_a_gu[RANK:], grad_bd],
        [cat(gbg_a, gbg_b), cat(gbu_a, gbu_b), cat(gad_a, gad_b)],
    )
    grad_a_in = contract(d_inner, normed, 1, 0)
    grad_b_in = contract(inner, d_linear, 0, 1)
    q_end, k_end = n_query, n_query + n_key
    gaq, gak, gav, gbq, gbk, gbv = owners(
        [
            grad_a_in[:RANK],
            grad_a_in[RANK : 2 * RANK],
            grad_a_in[2 * RANK :],
            grad_b_in[:RANK, :q_end],
            grad_b_in[RANK : 2 * RANK, q_end:k_end],
            grad_b_in[2 * RANK :, k_end:],
        ],
        [],
    )
    return (
        output[None],
        grad_tokens[None],
        gaq,
        gbq,
        gak,
        gbk,
        gav,
        gbv,
        gao,
        gbo,
        gag,
        gbg,
        gau,
        gbu,
        gad,
        gbd,
    )


def solution(mesh):
    tokens = P("dp", "seq", None)
    matrix = P(("dp", "seq"), None)
    stack = P(None, ("dp", "seq"), None)
    in_specs = (tokens, tokens, P("dp"), P("dp")) + (P(),) * 4 + (matrix,) * 7 + (stack,) * 14
    out_specs = (tokens, tokens) + (stack,) * 14
    return jax.shard_map(shards, mesh=mesh, in_specs=in_specs, out_specs=out_specs, check_vma=False)
```

```python
import functools

import jax
import jax.numpy as jnp
import numpy as np
from jax import lax
from jax.experimental import pallas as pl
from jax.experimental.pallas import tpu as pltpu
from jax.sharding import PartitionSpec as P

H = 32
KV = 8
HD = 64
GROUP = H // KV
ADAPT = 8
RANK = 16
EPS = 1e-05
F32 = jnp.float32
BF16 = jnp.bfloat16


def contract(left, right, left_dim, right_dim):
    return lax.dot_general(
        left, right, (((left_dim,), (right_dim,)), ((), ())), preferred_element_type=F32
    )


def rms_scale(operand, scaling, axis=-1):
    mean = jnp.mean(operand * operand, axis=axis, keepdims=True)
    return operand * lax.rsqrt(mean + EPS) * scaling


def rotary_tables(positions):
    frequency = jnp.power(1000000.0, -jnp.arange(HD // 2, dtype=F32) * 2.0 / HD)
    angles = frequency[:, None] * positions.astype(F32)[None, :]
    return jnp.cos(angles), jnp.sin(angles)


def prepare(linear, scaling, cosine, sine):
    normed = rms_scale(linear, scaling[:, None], axis=1)
    front, second = normed[:, : HD // 2], normed[:, HD // 2 :]
    return jnp.concatenate(
        [front * cosine - second * sine, second * cosine + front * sine], axis=1
    )


def after(value, *others):
    return lax.optimization_barrier((value, others))[0]


def ring_order(size):
    return list(range(0, size, 2)) + list(range(1, size, 2))[::-1]


def ring_pairs(size):
    order = ring_order(size)
    right = [(order[i], order[(i + 1) % size]) for i in range(size)]
    return right, [(b, a) for a, b in right]


def ring_offsets():
    offsets = [0]
    for step in range(1, (lax.axis_size("dp") - 1) // 2 + 1):
        offsets += [-step, step]
    return offsets + [lax.axis_size("dp") // 2]


class Ring:
    def __init__(self, own):
        self.pieces = [own]
        self.left = self.right = own
        self.steps = lax.axis_size("dp") // 2

    def complete(self):
        return len(self.pieces) == lax.axis_size("dp")

    def step(self, clock):
        size = lax.axis_size("dp")
        right, left = ring_pairs(size)
        if len(self.pieces) < size - 1:
            self.left = lax.ppermute(clock(self.left), "dp", right)
            self.right = lax.ppermute(clock(self.right), "dp", left)
            self.pieces += [self.left, self.right]
            return self.left, self.right
        half = self.left.shape[0] // 2
        top = lax.ppermute(clock(self.left[:half]), "dp", right)
        bottom = lax.ppermute(clock(self.right[half:]), "dp", left)
        self.pieces.append((top, bottom))
        return top, bottom


def ring_sources():
    size = lax.axis_size("dp")
    here = lax.axis_index("dp")
    place = jnp.where(here % 2 == 0, here // 2, size - 1 - here // 2)
    sources = []
    for offset in ring_offsets():
        at = (place + offset + size) % size
        sources.append(jnp.where(at < size // 2, 2 * at, 2 * (size - 1 - at) + 1).astype(jnp.int32))
    return sources


class Clock:
    def __init__(self):
        self.done = ()

    def tick(self, *done):
        self.done = done

    def __call__(self, value):
        return after(value, self.done) if self.done else value


class Conveyor:
    def __init__(self, clock, waiting):
        self.clock = clock
        self.waiting = list(waiting)
        self.going = []
        self.rings = []

    def push(self):
        ring = Ring(self.waiting.pop(0)())
        self.going.append((ring.step(self.clock), ring))
        self.rings.append(ring)
        return ring

    def advance(self, *computed):
        if not self.going:
            self.clock.tick(self.clock.done, computed)
            return
        came, ring = self.going.pop(0)
        self.clock.tick(came, *computed)
        if not ring.complete():
            self.going.append((ring.step(self.clock), ring))
            if ring.complete() and self.waiting:
                self.push()

    def until(self, ring, *computed):
        self.clock.tick(self.clock.done, computed)
        while not ring.complete() or any(r is ring for _, r in self.going):
            self.advance(self.clock.done)


def partner(operand, bit):
    size = lax.axis_size("seq")
    return lax.ppermute(operand, "seq", [(i, i ^ bit) for i in range(size)])


def seq_pieces(own):
    across = partner(own, 2)
    return [own, partner(own, 1), across, partner(across, 1)]


def seq_reduce(keep, give):
    arrived = partner(give, 1)
    sent = (keep[1].astype(F32) + arrived[1].astype(F32)).astype(BF16)
    own = keep[0].astype(F32) + arrived[0].astype(F32)
    return own + partner(sent, 2).astype(F32), sent


def everywhere_order(sources):
    seq = lax.axis_index("seq")
    return jnp.stack([s * 4 + (seq ^ bit) for s in sources for bit in range(4)]).astype(jnp.int32)


VMEM_LIMIT = 56 * 2**20
SMEM = pl.BlockSpec(memory_space=pltpu.SMEM)
VMEM = pl.BlockSpec(memory_space=pltpu.VMEM)


def call(kernel, name, flops=0, moved=0, **options):
    return pl.pallas_call(
        kernel,
        compiler_params=pltpu.CompilerParams(vmem_limit_bytes=VMEM_LIMIT),
        cost_estimate=pl.CostEstimate(flops=0, bytes_accessed=0, transcendentals=0),
        name=name,
        **options,
    )


def shape(dims, dtype):
    return jax.ShapeDtypeStruct(dims, dtype)


def fixed(*dims):
    return pl.BlockSpec(dims, lambda *_: (0,) * len(dims))


def columns_kernel(n_dp, gate_ref, up_ref, *out_refs):
    size = gate_ref.shape[1] // (4 * n_dp)
    for half, out in enumerate(out_refs):
        for m, ref in enumerate((gate_ref, up_ref)):
            for q in range(n_dp // 2):
                place = (m * (n_dp // 2) + q) * size
                for j in range(4):
                    start = ((half * (n_dp // 2) + q) * 4 + j) * size
                    out[j, :, place : place + size] = ref[:, start : start + size]


def columns_for_seq(gate, up, n_dp):
    rows, total = gate.shape
    return call(
        functools.partial(columns_kernel, n_dp),
        "columns",
        moved=8 * rows * total,
        in_specs=[VMEM] * 2,
        out_shape=[shape((4, rows, total // 4), BF16)] * 2,
    )(gate, up)


ANY = pl.BlockSpec(memory_space=pl.ANY)


def place_kernel(count, sources_ref, *refs):
    pieces, outs, sems = refs[: -count - 1], refs[-count - 1 : -1], refs[-1]
    copies = []
    for i, piece in enumerate(pieces):
        rows = piece.shape[0] // count
        start = pl.multiple_of(sources_ref[i] * rows, rows)
        for j, out in enumerate(outs):
            part = piece.at[pl.ds(j * rows, rows)]
            copies.append(pltpu.make_async_copy(part, out.at[pl.ds(start, rows)], sems.at[i, j]))
    for copy in copies:
        copy.start()
    for copy in copies:
        copy.wait()


def finish_kernel(count, source_ref, *refs):
    (top_ref, bottom_ref), outs, sems = refs[count : count + 2], refs[count + 2 : -1], refs[-1]
    copies = []
    if count == 2:
        rows = top_ref.shape[0]
        start = pl.multiple_of(source_ref[0] * rows, rows)
        for i, piece in enumerate((top_ref, bottom_ref)):
            copies.append(pltpu.make_async_copy(piece, outs[i].at[pl.ds(start, rows)], sems.at[i]))
    else:
        rows = top_ref.shape[0]
        for i, piece in enumerate((top_ref, bottom_ref)):
            start = pl.multiple_of(source_ref[0] * (2 * rows), 2 * rows) + i * rows
            copies.append(pltpu.make_async_copy(piece, outs[0].at[pl.ds(start, rows)], sems.at[i]))
    for copy in copies:
        copy.start()
    for copy in copies:
        copy.wait()


def place(pieces, sources, count):
    rows, columns = pieces[0].shape
    most = len(pieces)
    return call(
        functools.partial(place_kernel, count),
        "place",
        in_specs=[SMEM] + [VMEM] * most,
        out_specs=[ANY] * count,
        out_shape=[shape(((most + 1) * rows // count, columns), BF16)] * count,
        scratch_shapes=[pltpu.SemaphoreType.DMA((most, count))],
    )(jnp.stack(sources[:-1]), *pieces)


def finish(begun, pieces, sources):
    count = len(begun)
    return call(
        functools.partial(finish_kernel, count),
        "finish",
        in_specs=[SMEM] + [ANY] * count + [VMEM] * 2,
        out_specs=[ANY] * count,
        out_shape=[shape(m.shape, BF16) for m in begun],
        scratch_shapes=[pltpu.SemaphoreType.DMA((2,))],
        input_output_aliases={i + 1: i for i in range(count)},
    )(sources[-1][None], *begun, *pieces[-1])


def gather_rows(order_ref, source_ref, target_ref, rows):
    total = source_ref.shape[0]
    wide = min(256, total)
    each = wide // rows
    for i in range(total // wide):
        blocks = []
        for j in range(each):
            start = pl.multiple_of(order_ref[i * each + j] * rows, rows)
            blocks.append(source_ref[pl.ds(start, rows), :])
        target_ref[:, i * wide : (i + 1) * wide] = jnp.concatenate(blocks, axis=0).T


def qkv_kernel(order_ref, normed_ref, inner_ref, b_ref, *refs):
    pieces, (out_ref, left_ref) = refs[:-2], refs[-2:]

    @pl.when(pl.program_id(0) == 0)
    def _():
        gather_rows(order_ref, normed_ref, left_ref, pieces[0].shape[0])

    width = pieces[0].shape[1]
    step = 512
    for c in range(0, width, step):
        right = jnp.concatenate([p[:, c : c + step] for p in pieces], axis=0)
        sums = contract(left_ref[...], right, 1, 0)
        sums = sums + contract(inner_ref[...], b_ref[:, c : c + step], 1, 0)
        out_ref[c : c + step, :] = sums.T


def project_in(order, normed_t, inner, b_in, pieces):
    width, tokens = normed_t.shape
    total = b_in.shape[1]
    step = 1024
    rows = pieces[0].shape[0]
    return call(
        qkv_kernel,
        "project_in",
        flops=2 * width * tokens * total,
        moved=2 * width * total,
        grid=(total // step,),
        in_specs=[
            SMEM,
            fixed(width, tokens),
            fixed(*inner.shape),
            pl.BlockSpec((b_in.shape[0], step), lambda c: (0, c)),
        ]
        + [pl.BlockSpec((rows, step), lambda c: (0, c))] * len(pieces),
        out_specs=pl.BlockSpec((step, tokens), lambda c: (c, 0)),
        out_shape=shape((total, tokens), F32),
        scratch_shapes=[pltpu.VMEM((tokens, width), BF16)],
    )(order, normed_t, inner, b_in, *pieces)


def out_kernel(order_ref, mixed_ref, inner_ref, b_ref, tokens_ref, valid_ref, gain_ref, *refs):
    pieces, (hidden_ref, normed_ref, left_ref) = refs[:-3], refs[-3:]
    c = pl.program_id(0)

    @pl.when(c == 0)
    def _():
        gather_rows(order_ref, mixed_ref, left_ref, pieces[0].shape[0])

    width = pieces[0].shape[1]
    right = jnp.concatenate([p[...] for p in pieces], axis=0)
    sums = contract(left_ref[...], right, 1, 0) + contract(inner_ref[...], b_ref[...], 0, 0)
    sums = tokens_ref[...].astype(F32) + valid_ref[...] * sums
    hidden_ref[:, pl.ds(pl.multiple_of(c * width, width), width)] = sums

    @pl.when(c == pl.num_programs(0) - 1)
    def _():
        hidden = hidden_ref[...]
        normed_ref[...] = rms_scale(hidden, gain_ref[...]).astype(BF16)


def project_out(order, mixed, inner, bo, tokens, valid, gain, pieces):
    features, block = mixed.shape
    width = tokens.shape[1]
    step = 1024
    rows = pieces[0].shape[0]
    skip = (pieces[0].shape[1] - width) // step
    return call(
        out_kernel,
        "project_out",
        flops=2 * features * block * width,
        moved=2 * features * width,
        grid=(width // step,),
        in_specs=[
            SMEM,
            fixed(features, block),
            fixed(*inner.shape),
            pl.BlockSpec((RANK, step), lambda c: (0, c)),
            pl.BlockSpec((block, step), lambda c: (0, c)),
            fixed(block, 1),
            fixed(1, width),
        ]
        + [pl.BlockSpec((rows, step), lambda c: (0, c + skip))] * len(pieces),
        out_specs=[fixed(block, width), fixed(block, width)],
        out_shape=[shape((block, width), F32), shape((block, width), BF16)],
        scratch_shapes=[pltpu.VMEM((block, features), BF16)],
    )(order, mixed, inner, bo, tokens, valid, gain, *pieces)


def scatter_products(order_ref, pieces, right, sums_ref, form):
    rows = pieces[0].shape[0]
    each = max(1, 256 // rows)
    for i in range(0, len(pieces), each):
        left = jnp.concatenate([p[...] for p in pieces[i : i + each]], axis=0)
        product = contract(left, right, 1, form)
        for j in range(each):
            start = pl.multiple_of(order_ref[i + j] * rows, rows)
            sums_ref[pl.ds(start, rows), :] += product[j * rows : (j + 1) * rows]


def out_back_kernel(order_ref, grad_ref, a_ref, inner_ref, *refs):
    pieces, (out_ref, sums_ref) = refs[:-2], refs[-2:]
    c = pl.program_id(0)

    @pl.when(c == 0)
    def _():
        sums_ref[...] = contract(a_ref[...], inner_ref[...], 0, 1)

    scatter_products(order_ref, pieces, grad_ref[...], sums_ref, 1)

    @pl.when(c == pl.num_programs(0) - 1)
    def _():
        out_ref[...] = sums_ref[...].astype(BF16)


def project_out_back(order, grad, ao, d_inner, pieces):
    block, width = grad.shape
    features = ao.shape[1]
    step = 1024
    rows = pieces[0].shape[0]
    skip = (pieces[0].shape[1] - width) // step
    return call(
        out_back_kernel,
        "project_out_back",
        flops=2 * features * block * width,
        moved=2 * features * width,
        grid=(width // step,),
        in_specs=[
            SMEM,
            pl.BlockSpec((block, step), lambda c: (0, c)),
            fixed(*ao.shape),
            fixed(*d_inner.shape),
        ]
        + [pl.BlockSpec((rows, step), lambda c: (0, c + skip))] * len(pieces),
        out_specs=fixed(features, block),
        out_shape=shape((features, block), BF16),
        scratch_shapes=[pltpu.VMEM((features, block), F32)],
    )(order, grad, ao, d_inner, *pieces)


def in_back_kernel(order_ref, grad_ref, a_ref, inner_ref, tokens_ref, gain_ref, base_ref, *refs):
    pieces, (out_ref, sums_ref, turned_ref) = refs[:-3], refs[-3:]
    c = pl.program_id(0)

    @pl.when(c == 0)
    def _():
        sums_ref[...] = contract(a_ref[...], inner_ref[...], 0, 0)

    scatter_products(order_ref, pieces, grad_ref[...], sums_ref, 0)

    @pl.when(c == pl.num_programs(0) - 1)
    def _():
        size = sums_ref.shape[1]
        for i in range(0, sums_ref.shape[0], size):
            turned_ref[:, i : i + size] = sums_ref[i : i + size, :].T
        inputs = tokens_ref[...].astype(F32)
        grad = turned_ref[...] * gain_ref[...]
        scale = lax.rsqrt(jnp.mean(inputs * inputs, axis=-1, keepdims=True) + EPS)
        along = jnp.mean(inputs * grad, axis=-1, keepdims=True) * scale * scale
        out_ref[...] = (base_ref[...] + scale * (grad - inputs * along)).astype(BF16)


def project_in_back(order, d_linear, a_in, d_inner, tokens, gain, base, pieces):
    total, block = d_linear.shape
    width = tokens.shape[1]
    step = 1024
    rows = pieces[0].shape[0]
    return call(
        in_back_kernel,
        "project_in_back",
        flops=2 * total * block * width,
        moved=2 * total * width,
        grid=(total // step,),
        in_specs=[
            SMEM,
            pl.BlockSpec((step, block), lambda c: (c, 0)),
            fixed(*a_in.shape),
            fixed(*d_inner.shape),
            fixed(block, width),
            fixed(1, width),
            fixed(block, width),
        ]
        + [pl.BlockSpec((rows, step), lambda c: (0, c))] * len(pieces),
        out_specs=fixed(block, width),
        out_shape=shape((block, width), BF16),
        scratch_shapes=[pltpu.VMEM((width, block), F32), pltpu.VMEM((block, width), F32)],
    )(order, d_linear, a_in, d_inner, tokens, gain, base, *pieces)


def gather_tokens(refs, whole_ref):
    block = refs[0].shape[0]
    for i, ref in enumerate(refs):
        whole_ref[i * block : (i + 1) * block, :] = ref[...]


def lower_back_kernel(g0, g1, g2, g3, weight_ref, b_ref, a_ref, out_ref, inner_ref, whole_ref):
    @pl.when(pl.program_id(0) == 0)
    def _():
        gather_tokens((g0, g1, g2, g3), whole_ref)
        inner_ref[...] = contract(whole_ref[...], b_ref[...], 1, 1).astype(BF16)

    sums = contract(whole_ref[...], weight_ref[...], 1, 1)
    out_ref[...] = (sums + contract(inner_ref[...], a_ref[...], 1, 0)).astype(BF16)


def lower_back(grads, weight, bd, ad):
    block, width = grads[0].shape
    units = weight.shape[0]
    step = 256
    tokens = 4 * block
    return call(
        lower_back_kernel,
        "lower_back",
        flops=2 * tokens * width * units,
        moved=2 * width * units,
        grid=(units // step,),
        in_specs=[fixed(block, width)] * 4
        + [
            pl.BlockSpec((step, width), lambda j: (j, 0)),
            fixed(RANK, width),
            pl.BlockSpec((RANK, step), lambda j: (0, j)),
        ],
        out_specs=[pl.BlockSpec((tokens, step), lambda j: (0, j)), fixed(tokens, RANK)],
        out_shape=[shape((tokens, units), BF16), shape((tokens, RANK), BF16)],
        scratch_shapes=[pltpu.VMEM((tokens, width), BF16)],
    )(*grads, weight, bd, ad)


def tokens_kernel(n0, n1, n2, n3, a_ref, whole_ref, low_ref):
    gather_tokens((n0, n1, n2, n3), whole_ref)
    low_ref[...] = contract(whole_ref[...], a_ref[...], 1, 1).astype(BF16)


def all_tokens(normed, a_gu):
    block, width = normed[0].shape
    return call(
        tokens_kernel,
        "all_tokens",
        flops=16 * block * width * RANK,
        moved=16 * block * width,
        out_shape=[shape((4 * block, width), BF16), shape((4 * block, 2 * RANK), BF16)],
    )(*normed, a_gu)


def units_kernel(
    whole_ref,
    low_ref,
    gate_ref,
    up_ref,
    bg_ref,
    bu_ref,
    ad_ref,
    d_act_ref,
    act_ref,
    dg_ref,
    du_ref,
    inner_ref,
):
    @pl.when(pl.program_id(0) == 0)
    def _():
        inner_ref[...] = jnp.zeros(inner_ref.shape, F32)

    low_gate, low_up = low_ref[:, :RANK], low_ref[:, RANK:]
    gate = contract(whole_ref[...], gate_ref[...], 1, 0) + contract(low_gate, bg_ref[...], 1, 0)
    up = contract(whole_ref[...], up_ref[...], 1, 0) + contract(low_up, bu_ref[...], 1, 0)
    d_act = d_act_ref[...].astype(F32)
    sig = jax.nn.sigmoid(gate)
    silu = gate * sig
    act = (silu * up).astype(BF16)
    d_gate = (d_act * up * (sig + silu * (1.0 - sig))).astype(BF16)
    d_up = (d_act * silu).astype(BF16)
    act_ref[...] = act
    dg_ref[...] = d_gate
    du_ref[...] = d_up
    inner_ref[:, :RANK] += contract(d_gate, bg_ref[...], 1, 1)
    inner_ref[:, RANK : 2 * RANK] += contract(d_up, bu_ref[...], 1, 1)
    inner_ref[:, 2 * RANK :] += contract(act, ad_ref[...], 1, 1)


def units(part, whole, low, both, bg, bu, ad, d_act):
    tokens, width = whole.shape
    half = both.shape[1] // 2
    step = 256
    steps = half // step
    here = pl.BlockSpec((RANK, step), lambda j: (0, part * steps + j))
    tile = pl.BlockSpec((tokens, step), lambda j: (0, j))
    return call(
        units_kernel,
        "units",
        flops=4 * tokens * width * half,
        moved=4 * width * half,
        grid=(steps,),
        in_specs=[
            fixed(tokens, width),
            fixed(tokens, 2 * RANK),
            pl.BlockSpec((width, step), lambda j: (0, j)),
            pl.BlockSpec((width, step), lambda j: (0, steps + j)),
            here,
            here,
            here,
            pl.BlockSpec((tokens, step), lambda j: (0, part * steps + j)),
        ],
        out_specs=[tile] * 3 + [fixed(tokens, 3 * RANK)],
        out_shape=[shape((tokens, half), BF16)] * 3 + [shape((tokens, 3 * RANK), F32)],
    )(whole, low, both, both, bg, bu, ad, d_act)


def units_grads_kernel(low_ref, d_down_ref, act_ref, dg_ref, du_ref, gbg_ref, gbu_ref, gad_ref):
    gbg_ref[...] = contract(low_ref[:, :RANK], dg_ref[...], 0, 0)
    gbu_ref[...] = contract(low_ref[:, RANK:], du_ref[...], 0, 0)
    gad_ref[...] = contract(d_down_ref[...], act_ref[...], 0, 0)


def units_grads(low, d_down, act, d_gate, d_up):
    tokens, half = act.shape
    step = 256
    tile = pl.BlockSpec((tokens, step), lambda j: (0, j))
    thin = pl.BlockSpec((RANK, step), lambda j: (0, j))
    return call(
        units_grads_kernel,
        "units_grads",
        flops=6 * tokens * half * RANK,
        moved=6 * tokens * half,
        grid=(half // step,),
        in_specs=[fixed(tokens, 2 * RANK), fixed(tokens, RANK), tile, tile, tile],
        out_specs=[thin] * 3,
        out_shape=[shape((RANK, half), F32)] * 3,
    )(low, d_down, act, d_gate, d_up)


def units_back_first_kernel(g_ref, u_ref, w_ref, out_ref):
    half = g_ref.shape[1]
    sums = contract(g_ref[...], w_ref[:, :half], 1, 1) + contract(u_ref[...], w_ref[:, half:], 1, 1)
    out_ref[...] = sums.astype(BF16)


def units_back_first(d_gate, d_up, both):
    tokens, half = d_gate.shape
    width = both.shape[0]
    step = 256
    return call(
        units_back_first_kernel,
        "units_back_first",
        flops=4 * tokens * half * width,
        moved=4 * half * width,
        grid=(width // step,),
        in_specs=[fixed(tokens, half)] * 2 + [pl.BlockSpec((step, 2 * half), lambda n: (n, 0))],
        out_specs=pl.BlockSpec((tokens, step), lambda n: (0, n)),
        out_shape=shape((tokens, width), BF16),
    )(d_gate, d_up, both)


def units_back_kernel(first_ref, g_ref, u_ref, w_ref, low_ref, a_ref, keep_ref, give_ref):
    half = g_ref.shape[1]
    sums = first_ref[...].astype(F32) + contract(low_ref[...], a_ref[...], 1, 0)
    sums = sums + contract(g_ref[...], w_ref[:, :half], 1, 1)
    sums = sums + contract(u_ref[...], w_ref[:, half:], 1, 1)
    sums = sums.astype(BF16)
    block = keep_ref.shape[1]
    keep_ref[0] = sums[:block]
    give_ref[0] = sums[block : 2 * block]
    keep_ref[1] = sums[2 * block : 3 * block]
    give_ref[1] = sums[3 * block :]


def units_back(part, parts, first, d_gate, d_up, both, low, a_gu):
    tokens, half = d_gate.shape
    width = both.shape[0]
    step = 256
    steps = width // parts // step
    place = lambda n: part * steps + n
    out = pl.BlockSpec((2, tokens // 4, step), lambda n: (0, 0, n))
    return call(
        units_back_kernel,
        "units_back",
        flops=4 * tokens * half * width // parts,
        moved=4 * half * width // parts,
        grid=(steps,),
        in_specs=[
            pl.BlockSpec((tokens, step), lambda n: (0, place(n))),
            fixed(tokens, half),
            fixed(tokens, half),
            pl.BlockSpec((step, 2 * half), lambda n: (place(n), 0)),
            fixed(tokens, 2 * RANK),
            pl.BlockSpec((2 * RANK, step), lambda n: (0, place(n))),
        ],
        out_specs=[out, out],
        out_shape=[shape((2, tokens // 4, width // parts), BF16)] * 2,
    )(first, d_gate, d_up, both, low, a_gu)


def lower_kernel(
    aa_ref, ab_ref, weight_ref, low_ref, b_ref, whole_ref, lowgu_ref, g0, g1, g2, g3, keep_ref, give_ref, grad_ref, grad_gu_ref
):
    half = aa_ref.shape[1]
    sums = contract(low_ref[...], b_ref[...], 1, 0)
    sums = sums + contract(aa_ref[...], weight_ref[:half], 1, 0)
    sums = sums + contract(ab_ref[...], weight_ref[half:], 1, 0)
    sums = sums.astype(BF16)
    block = g0.shape[0]
    low = low_ref[...]
    grad = jnp.zeros(grad_ref.shape, F32)
    for i, g in enumerate((g0, g1, g2, g3)):
        out = give_ref if i % 2 else keep_ref
        out[i // 2] = sums[i * block : (i + 1) * block]
        grad = grad + contract(low[i * block : (i + 1) * block], g[...], 0, 0)
    grad_ref[...] = grad
    grad_gu_ref[...] = contract(lowgu_ref[...], whole_ref[...], 0, 0)


def lower(act_a, act_b, weight, low, bd, grads, whole, low_gu):
    block, width = grads[0].shape
    tokens, half = act_a.shape
    step = 256
    tile = pl.BlockSpec((block, step), lambda n: (0, n))
    thin = pl.BlockSpec((RANK, step), lambda n: (0, n))
    out = pl.BlockSpec((2, block, step), lambda n: (0, 0, n))
    return call(
        lower_kernel,
        "lower",
        flops=4 * tokens * half * width,
        moved=4 * half * width,
        grid=(width // step,),
        in_specs=[
            fixed(tokens, half),
            fixed(tokens, half),
            pl.BlockSpec((2 * half, step), lambda n: (0, n)),
            fixed(tokens, RANK),
            thin,
            pl.BlockSpec((tokens, step), lambda n: (0, n)),
            fixed(tokens, 2 * RANK),
        ]
        + [tile] * 4,
        out_specs=[out, out, thin, pl.BlockSpec((2 * RANK, step), lambda n: (0, n))],
        out_shape=[shape((2, block, width), BF16)] * 2
        + [shape((RANK, width), F32), shape((2 * RANK, width), F32)],
    )(act_a, act_b, weight, low, bd, whole, low_gu, *grads)


def wide_heads(ref):
    return jnp.concatenate([ref[h * HD : (h + 1) * HD] for h in range(GROUP)], axis=1)


def attend_kernel(seq_ref, limit_ref, q_ref, kv0, kv1, kv2, kv3, o_ref, e_ref, r_ref):
    queries = wide_heads(q_ref)
    limit = limit_ref[...]
    total = jnp.zeros(limit.shape, F32)
    mixed = jnp.zeros(queries.shape, F32)
    for bit, ref in enumerate((kv0, kv1, kv2, kv3)):
        block = ref.shape[2]
        scores = contract(ref[0, :HD], queries, 0, 0)
        places = (seq_ref[0] ^ bit) * block + lax.broadcasted_iota(jnp.int32, scores.shape, 0)
        raised = jnp.where(places <= limit, jnp.exp(scores), 0.0)
        total = total + jnp.sum(raised, axis=0, keepdims=True)
        low = raised.astype(BF16)
        e_ref[0, bit] = low
        mixed = mixed + contract(ref[0, HD:], low, 1, 0)
    inverse = 1.0 / total
    r_ref[0] = inverse
    mixed = (mixed * inverse).astype(BF16)
    width = q_ref.shape[1]
    for h in range(GROUP):
        o_ref[h * HD : (h + 1) * HD] = mixed[:, h * width : (h + 1) * width]


def attend(seq, limit, queries, keys_values):
    block = keys_values[0].shape[2]
    width = queries.shape[1]
    wide = GROUP * width
    head_rows = pl.BlockSpec((GROUP * HD, width), lambda g: (g, 0))
    return call(
        attend_kernel,
        "attend",
        flops=16 * H * width * 4 * block * HD,
        moved=2 * KV * 4 * block * wide,
        grid=(KV,),
        in_specs=[SMEM, fixed(1, wide), head_rows]
        + [pl.BlockSpec((1, 2 * HD, block), lambda g: (g, 0, 0))] * 4,
        out_specs=[
            head_rows,
            pl.BlockSpec((1, 4, block, wide), lambda g: (g, 0, 0, 0)),
            pl.BlockSpec((1, 1, wide), lambda g: (g, 0, 0)),
        ],
        out_shape=[
            shape(queries.shape, BF16),
            shape((KV, 4, block, wide), BF16),
            shape((KV, 1, wide), F32),
        ],
    )(seq[None], limit, queries, *keys_values)


def attend_back_kernel(q_ref, kv0, kv1, kv2, kv3, e_ref, r_ref, o_ref, do_ref, dq_ref, keep_ref, give_ref):
    width = q_ref.shape[1]
    queries = wide_heads(q_ref)
    grads = wide_heads(do_ref).astype(F32) * r_ref[0]
    dots = jnp.sum(grads * wide_heads(o_ref).astype(F32), axis=0, keepdims=True)
    grads = grads.astype(BF16)
    d_queries = jnp.zeros(queries.shape, F32)
    for bit, ref in enumerate((kv0, kv1, kv2, kv3)):
        out = give_ref if bit % 2 else keep_ref
        raised = e_ref[0, bit]
        d_probs = contract(ref[0, HD:], grads, 0, 0)
        d_scores = (raised.astype(F32) * (d_probs - dots)).astype(BF16)
        d_queries = d_queries + contract(ref[0, :HD], d_scores, 1, 0)
        out[bit // 2, 0, :HD] = contract(queries, d_scores, 1, 1).astype(BF16)
        out[bit // 2, 0, HD:] = contract(grads, raised, 1, 1).astype(BF16)
    for h in range(GROUP):
        dq_ref[h * HD : (h + 1) * HD] = d_queries[:, h * width : (h + 1) * width]


def attend_back(first, count, queries, keys_values, raised, inverse, mixed, d_mixed):
    block = keys_values[0].shape[2]
    width = queries.shape[1]
    wide = GROUP * width
    head_rows = pl.BlockSpec((GROUP * HD, width), lambda g: (first + g, 0))
    shares = pl.BlockSpec((2, 1, 2 * HD, block), lambda g: (0, g, 0, 0))
    return call(
        attend_back_kernel,
        "attend_back",
        flops=32 * count * GROUP * width * 4 * block * HD,
        moved=2 * count * 4 * block * wide,
        grid=(count,),
        in_specs=[head_rows]
        + [pl.BlockSpec((1, 2 * HD, block), lambda g: (first + g, 0, 0))] * 4
        + [
            pl.BlockSpec((1, 4, block, wide), lambda g: (first + g, 0, 0, 0)),
            pl.BlockSpec((1, 1, wide), lambda g: (first + g, 0, 0)),
            head_rows,
            head_rows,
        ],
        out_specs=[pl.BlockSpec((GROUP * HD, width), lambda g: (g, 0)), shares, shares],
        out_shape=[
            shape((count * GROUP * HD, width), F32),
            shape((2, count, 2 * HD, block), BF16),
            shape((2, count, 2 * HD, block), BF16),
        ],
    )(queries, *keys_values, raised, inverse, mixed, d_mixed)


def pick_kernel(ids_ref, *refs):
    out_ref = refs[-1]
    for d in range(out_ref.shape[0]):
        parts = [ref[ids_ref[d]] for ref in refs[:-1]]
        out_ref[d] = jnp.concatenate(parts, axis=1)


def pick(ids, stacks):
    columns = sum(stack.shape[2] for stack in stacks)
    n_dp = ids.shape[0]
    return call(
        pick_kernel,
        "pick",
        moved=4 * n_dp * RANK * columns,
        in_specs=[SMEM] + [VMEM] * len(stacks),
        out_shape=shape((n_dp, RANK, columns), BF16),
    )(ids, *stacks)


def spread_kernel(widths, seq_ref, mine_ref, p1, p2, p3, *refs):
    (in_ref, grow_ref, ao_ref, bo_ref, gu_ref, bd_ref, bg_ref, bu_ref, ad_ref, all_ref) = refs
    local, each, thin = widths
    n_dp = mine_ref.shape[0]
    seq = seq_ref[0]
    base = 3 * local
    all_ref[seq] = mine_ref[:, :, base:]
    for bit, ref in ((1, p1), (2, p2), (3, p3)):
        all_ref[seq ^ bit] = ref[...]

    def factor(start, width):
        parts = [all_ref[j, d, :, start : start + width] for d in range(n_dp) for j in range(4)]
        return jnp.concatenate(parts, axis=1)

    wide = lambda m: factor(m * each, each)
    for i in range(3):
        in_ref[i * RANK : (i + 1) * RANK] = wide(i)
    grow_ref[...] = jnp.zeros(grow_ref.shape, BF16)
    n_query, n_key = 4 * n_dp * each, 4 * n_dp * thin
    grow_ref[:RANK, :n_query] = wide(3)
    for i in range(2):
        start = n_query + i * n_key
        grow_ref[(i + 1) * RANK : (i + 2) * RANK, start : start + n_key] = factor(9 * each + i * thin, thin)
    ao_ref[...] = wide(4)
    bo_ref[...] = wide(5)
    gu_ref[:RANK] = wide(6)
    gu_ref[RANK:] = wide(7)
    bd_ref[...] = wide(8)
    for i, ref in enumerate((bg_ref, bu_ref, ad_ref)):
        for d in range(n_dp):
            ref[:, d * local : (d + 1) * local] = mine_ref[d, :, i * local : (i + 1) * local]


def spread(seq, mine, others, widths):
    local, each, thin = widths
    n_dp = mine.shape[0]
    total = 4 * n_dp * each
    grown = total + 8 * n_dp * thin
    rows = [(3 * RANK, total), (3 * RANK, grown), (RANK, total), (RANK, total), (2 * RANK, total), (RANK, total)]
    rows += [(RANK, n_dp * local)] * 3
    return call(
        functools.partial(spread_kernel, widths),
        "spread",
        moved=4 * 4 * mine.size,
        in_specs=[SMEM] + [VMEM] * 4,
        out_shape=[shape(dims, BF16) for dims in rows],
        scratch_shapes=[pltpu.VMEM((4,) + others[0].shape, BF16)],
    )(seq[None], mine, *others)


def pack_kernel(n_dp, count, seq_ref, *refs):
    ins, (keep_ref, give_ref, all_ref) = refs[:count], refs[count:]
    for d in range(n_dp):
        for j in range(4):
            parts = []
            for ref in ins:
                each = ref.shape[1] // (4 * n_dp)
                at = (d * 4 + j) * each
                parts.append(ref[:, at : at + each])
            all_ref[j, d] = jnp.concatenate(parts, axis=1)
    seq = seq_ref[0]
    for bit in range(4):
        out = give_ref if bit % 2 else keep_ref
        out[bit // 2] = all_ref[seq ^ bit]


def pack(seq, grads, n_dp):
    columns = sum(g.shape[1] for g in grads) // (4 * n_dp)
    dims = (n_dp, RANK, columns)
    return call(
        functools.partial(pack_kernel, n_dp, len(grads)),
        "pack",
        moved=16 * n_dp * RANK * columns * 4,
        in_specs=[SMEM] + [VMEM] * len(grads),
        out_shape=[shape((2,) + dims, F32)] * 2,
        scratch_shapes=[pltpu.VMEM((4,) + dims, F32)],
    )(seq[None], *grads)


def sort_kernel(widths, ids_ref, came_ref, *out_refs):
    came = [came_ref[d] for d in range(came_ref.shape[0])]
    for a in range(ADAPT):
        total = jnp.zeros(came[0].shape, F32)
        for d, value in enumerate(came):
            total = total + jnp.where(ids_ref[d] == a, value, 0.0)
        at = 0
        for ref, width in zip(out_refs, widths):
            part = total[:, at : at + width]
            ref[a] = part.T if width < 64 else part
            at += width


def sort(ids, came, widths):
    outs = call(
        functools.partial(sort_kernel, widths),
        "sort",
        moved=8 * came.size,
        in_specs=[SMEM, VMEM],
        out_shape=[shape((ADAPT, w, RANK) if w < 64 else (ADAPT, RANK, w), F32) for w in widths],
    )(ids, came)
    return [o if w < 64 else o.transpose(0, 2, 1) for o, w in zip(outs, widths)]


def shards(
    tokens,
    cotangent,
    lengths,
    adapter_ids,
    attn_gain,
    query_gain,
    key_gain,
    ffn_gain,
    w_query,
    w_key,
    w_value,
    w_out,
    gate_weight,
    w_up,
    w_down,
    a_query,
    b_query,
    a_key,
    b_key,
    a_value,
    b_value,
    a_out,
    b_out,
    a_gate,
    b_gate,
    a_up,
    b_up,
    a_down,
    b_down,
):
    n_dp = lax.axis_size("dp")
    seq = lax.axis_index("seq")
    _, block, width = tokens.shape
    length = lengths[0]
    positions = seq * block + jnp.arange(block)
    valid = (positions < length).astype(F32)[:, None]
    sources = ring_sources()
    clock = Clock()
    n_query, n_key = H * HD, KV * HD
    local, each, thin = b_gate.shape[1], a_query.shape[1], b_key.shape[1]
    widths = (local, each, thin)

    attn = Ring(jnp.concatenate([w_query, w_key, w_value, w_out], axis=1))
    first_came, age = None, 0
    queue = [attn.pieces[0]]
    sides, acrosses, corners, going = [], [], [], []
    arrived = slot = 0
    last = attn.steps - 1
    while len(corners) < n_dp + 1:
        waits, new = [], []
        if not attn.complete():
            new = attn.step(clock)
            waits += new
            if attn.complete():
                ended = new
                new = [new]
        elif first_came is not None:
            age += 1
            if age == 3:
                waits += first_came
                first_came = None
        elif not first_ring.complete():
            first_came, age = first_ring.step(lambda v: after(v, ended) if len(first_ring.pieces) == 1 else clock(v)), 0
        while len(acrosses) < len(queue) and len(going) < 2:
            acrosses.append(partner(clock(queue[len(acrosses)]), 2))
            going.append(len(acrosses))
        for _ in range(3):
            if len(corners) < arrived:
                corners.append(partner(clock(acrosses[len(corners)]), 1))
                waits.append(corners[-1])
            elif len(sides) < len(queue):
                sides.append(partner(clock(queue[len(sides)]), 1))
                waits.append(sides[-1])
        if slot == 0:
            slots_a, slots_b = columns_for_seq(gate_weight, w_up, n_dp)
            ids = lax.all_to_all(
                jnp.broadcast_to(adapter_ids[None], (n_dp, 128)), "dp", 0, 0, tiled=True
            )[:, 0]
            stacks = (b_gate, b_up, a_down, a_query, a_key, a_value, b_query, a_out, b_out)
            stacks += (a_gate, a_up, b_down, b_key, b_value)
            sent = pick(ids, [m.transpose(0, 2, 1) for m in stacks])
            waits += [sent, slots_a]
        if slot == 1:
            swapped_a = lax.all_to_all(clock(slots_a), "seq", 0, 0, tiled=True)
        if slot == 2:
            mine = lax.all_to_all(clock(sent), "dp", 0, 0, tiled=True)
            first_ring = Ring(jnp.concatenate([w_down, swapped_a.reshape(-1, width)], axis=0))
            waits.append(first_ring.pieces[0])
        if slot == last + 2:
            inputs = clock(tokens)[0].astype(F32)
            normed = rms_scale(inputs, attn_gain).astype(BF16)
            normed_t = normed.T
            cot = cotangent[0].astype(F32)
            grad_out = (valid * clock(cot)).astype(BF16)
            waits += [normed_t, grad_out]
        if going and (slot == 0 or len(going) == 2 or len(queue) == n_dp + 1):
            waits.append(acrosses[going[0] - 1])
        else:
            going = going[:0] + going
        clock.tick(*waits)
        if going and any(w is acrosses[going[0] - 1] for w in waits):
            arrived = going.pop(0)
        if slot == 2:
            queue.append(clock(mine)[..., 3 * local :])
        queue += [jnp.concatenate(p, axis=0) if isinstance(p, tuple) else p for p in new]
        slot += 1
    others = [sides.pop(5), acrosses.pop(5), corners.pop(5)]
    queue.pop(5)
    attn_pieces = []
    for group in zip(queue, sides, acrosses, corners):
        attn_pieces += group
    order = everywhere_order(sources)

    belt = Conveyor(clock, [lambda: swapped_b.reshape(-1, width)])
    if first_came is None and not first_ring.complete():
        first_came = first_ring.step(clock)
    if first_came is not None:
        belt.going.append((first_came, first_ring))
    a_in, b_in, ao, bo, a_gu, bd, bg, bu, ad = spread(seq, mine, clock(others), widths)
    inner = contract(normed, a_in, 1, 1).astype(BF16)

    linear = project_in(order, normed_t, inner, b_in, attn_pieces)
    query_lin = linear[:n_query].reshape(H, HD, block)
    key_lin = linear[n_query : n_query + n_key].reshape(KV, HD, block)
    value_lin = linear[n_query + n_key :].reshape(KV, HD, block)
    cosine, sine = rotary_tables(positions)
    scale = HD**-0.5
    query_prep = lambda v: prepare(v, query_gain, cosine, sine)
    key_prep = lambda v: prepare(v, key_gain, cosine, sine)
    keys_values = jnp.concatenate([key_prep(key_lin), value_lin], axis=1).astype(BF16)
    keys_values = seq_pieces(keys_values)
    queries = (query_prep(query_lin) * scale).astype(BF16).reshape(n_query, block)
    limit = jnp.minimum(positions, length - 1).astype(jnp.int32)
    limit = jnp.tile(limit, GROUP)[None, :]
    belt.advance(queries)
    grads = seq_pieces(after(grad_out, keys_values[2]))
    mixed, raised, inverse = attend(seq, limit, queries, keys_values)
    swapped_b = lax.all_to_all(after(slots_b, queries), "seq", 0, 0, tiled=True)
    belt.advance(mixed)

    inner_out = contract(ao, mixed, 1, 0).astype(BF16)
    hidden, normed_two = project_out(
        order, mixed, inner_out, bo, tokens[0], valid, ffn_gain[None], attn_pieces
    )

    n2 = seq_pieces(normed_two)
    while not first_ring.complete():
        belt.advance(normed_two)
    ring_b = belt.rings[0]
    begun = place(clock(first_ring.pieces[:-1]), sources, 2)
    belt.until(first_ring, begun)
    w_lower, both_a = finish(begun, first_ring.pieces, sources)
    d_act, d_down = lower_back(clock(grads), w_lower, bd, ad)
    belt.advance(d_act)
    n2, low_n2 = all_tokens(n2, a_gu)
    act_a, dg_a, du_a, inner_a = units(0, n2, low_n2, both_a, bg, bu, ad, d_act)
    belt.advance(act_a)
    first = units_back_first(clock(dg_a), du_a, both_a)
    gbg_a, gbu_a, gad_a = units_grads(low_n2, d_down, after(act_a, first), dg_a, du_a)
    while not ring_b.complete():
        belt.advance(gbg_a)
    begun = place(clock(ring_b.pieces[:-1]), sources, 1)
    belt.until(ring_b, begun)
    (both_b,) = finish(begun, ring_b.pieces, sources)
    act_b, dg_b, du_b, inner_b = units(1, n2, low_n2, both_b, bg, bu, ad, d_act)
    low = (inner_a + inner_b).astype(BF16)
    low_gu, low_down = low[:, : 2 * RANK], low[:, 2 * RANK :]
    keep, give = units_back(0, 2, first, dg_b, du_b, both_b, low_gu, a_gu)
    left, sent = seq_reduce(keep, give)
    keep, give = units_back(1, 2, after(first, sent), dg_b, du_b, both_b, low_gu, a_gu)
    right, sent = seq_reduce(keep, give)
    gbg_b, gbu_b, gad_b = units_grads(low_n2, d_down, after(act_b, sent), dg_b, du_b)

    act_b = after(act_b, left, gbg_b)
    keep, give, grad_bd, grad_a_gu = lower(act_a, act_b, w_lower, low_down, bd, grads, n2, low_gu)
    left, right = after((left, right), keep)

    d_n2 = jnp.concatenate([left, right], axis=1)
    d_hidden = cot + jax.vjp(lambda v: rms_scale(v, ffn_gain), hidden)[1](d_n2)[0]
    grad_update = (valid * d_hidden).astype(BF16)
    keep, give = after((keep, give), grad_update)
    lowered, sent = seq_reduce(keep, give)
    d_inner_out = contract(grad_update, bo, 1, 1).astype(BF16)
    d_mixed = project_out_back(order, after(grad_update, sent), ao, d_inner_out, attn_pieces)
    d_queries, d_kv = [], []
    for part in range(2):
        count = KV // 2
        d_query, keep, give = attend_back(
            part * count, count, queries, keys_values, raised, inverse, mixed, d_mixed
        )
        if part == 0:
            give = after(give, lowered)
        reduced, sent = seq_reduce(keep, give)
        d_mixed = after(d_mixed, sent)
        d_kv.append(reduced)
        d_queries.append(d_query)
    def owners(grads, alone):
        keep, give = pack(seq, grads, n_dp)
        both = keep + partner(give, 1)
        summed = both[0] + partner(both[1], 2)
        sizes = [g.shape[1] // (4 * n_dp) for g in grads]
        if alone:
            summed = jnp.concatenate([summed] + alone, axis=2)
            sizes += [g.shape[2] for g in alone]
        return sort(ids, lax.all_to_all(summed, "dp", 0, 0, tiled=True), sizes)

    grad_ao = contract(d_inner_out, mixed, 0, 1)
    grad_bo = contract(inner_out, grad_update, 1, 0)
    cat = lambda a, b: jnp.concatenate([a, b], axis=1).reshape(RANK, n_dp, -1).transpose(1, 0, 2)
    some = [grad_ao, grad_bo, grad_a_gu[:RANK], grad_a_gu[RANK:], grad_bd]
    owned = owners(
        after(some, d_query),
        [cat(gbg_a, gbg_b), cat(gbu_a, gbu_b), cat(gad_a, gad_b)],
    )
    gao, gbo, gag, gau, gbd, gbg, gbu, gad = owned

    d_queries = jnp.concatenate(d_queries, axis=0).reshape(H, HD, block) * scale
    output = (hidden + valid * after(lowered, d_queries)).astype(BF16)
    d_kv = jnp.concatenate(after(d_kv, output), axis=0)
    d_query_lin = jax.vjp(query_prep, query_lin)[1](d_queries)[0]
    d_key_lin = jax.vjp(key_prep, key_lin)[1](d_kv[:, :HD])[0]
    d_linear = jnp.concatenate(
        [
            d_query_lin.reshape(n_query, block),
            d_key_lin.reshape(n_key, block),
            d_kv[:, HD:].reshape(n_key, block),
        ],
        axis=0,
    ).astype(BF16)
    d_inner = contract(b_in, d_linear, 1, 0).astype(BF16)
    grad_tokens = project_in_back(
        order, d_linear, a_in, d_inner, tokens[0], attn_gain[None], after(d_hidden, *owned), attn_pieces
    )

    grad_a_in = contract(d_inner, normed, 1, 0)
    grad_b_in = contract(inner, d_linear, 0, 1)
    q_end, k_end = n_query, n_query + n_key
    gaq, gak, gav, gbq, gbk, gbv = owners(
        [
            grad_a_in[:RANK],
            grad_a_in[RANK : 2 * RANK],
            grad_a_in[2 * RANK :],
            grad_b_in[:RANK, :q_end],
            grad_b_in[RANK : 2 * RANK, q_end:k_end],
            grad_b_in[2 * RANK :, k_end:],
        ],
        [],
    )
    return (
        output[None],
        grad_tokens[None],
        gaq,
        gbq,
        gak,
        gbk,
        gav,
        gbv,
        gao,
        gbo,
        gag,
        gbg,
        gau,
        gbu,
        gad,
        gbd,
    )


def solution(mesh):
    tokens = P("dp", "seq", None)
    matrix = P(("dp", "seq"), None)
    stack = P(None, ("dp", "seq"), None)
    in_specs = (tokens, tokens, P("dp"), P("dp")) + (P(),) * 4 + (matrix,) * 7 + (stack,) * 14
    out_specs = (tokens, tokens) + (stack,) * 14
    return jax.shard_map(shards, mesh=mesh, in_specs=in_specs, out_specs=out_specs, check_vma=False)
```

```python
import functools

import jax
import jax.numpy as jnp
import numpy as np
from jax import lax
from jax.experimental import pallas as pl
from jax.experimental.pallas import tpu as pltpu
from jax.sharding import PartitionSpec as P

H = 32
KV = 8
HD = 64
GROUP = H // KV
ADAPT = 8
RANK = 16
EPS = 1e-05
F32 = jnp.float32
BF16 = jnp.bfloat16


def contract(left, right, left_dim, right_dim):
    return lax.dot_general(
        left, right, (((left_dim,), (right_dim,)), ((), ())), preferred_element_type=F32
    )


def rms_scale(operand, scaling, axis=-1):
    mean = jnp.mean(operand * operand, axis=axis, keepdims=True)
    return operand * lax.rsqrt(mean + EPS) * scaling


def rotary_tables(positions):
    frequency = jnp.power(1000000.0, -jnp.arange(HD // 2, dtype=F32) * 2.0 / HD)
    angles = frequency[:, None] * positions.astype(F32)[None, :]
    return jnp.cos(angles), jnp.sin(angles)


def prepare(linear, scaling, cosine, sine):
    normed = rms_scale(linear, scaling[:, None], axis=1)
    front, second = normed[:, : HD // 2], normed[:, HD // 2 :]
    return jnp.concatenate(
        [front * cosine - second * sine, second * cosine + front * sine], axis=1
    )


def after(value, *others):
    return lax.optimization_barrier((value, others))[0]


def ring_order(size):
    return list(range(0, size, 2)) + list(range(1, size, 2))[::-1]


def ring_pairs(size):
    order = ring_order(size)
    right = [(order[i], order[(i + 1) % size]) for i in range(size)]
    return right, [(b, a) for a, b in right]


def ring_offsets():
    offsets = [0]
    for step in range(1, (lax.axis_size("dp") - 1) // 2 + 1):
        offsets += [-step, step]
    return offsets + [lax.axis_size("dp") // 2]


class Ring:
    def __init__(self, own):
        self.pieces = [own]
        self.left = self.right = own
        self.steps = lax.axis_size("dp") // 2

    def complete(self):
        return len(self.pieces) == lax.axis_size("dp")

    def step(self, clock):
        size = lax.axis_size("dp")
        right, left = ring_pairs(size)
        if len(self.pieces) < size - 1:
            self.left = lax.ppermute(clock(self.left), "dp", right)
            self.right = lax.ppermute(clock(self.right), "dp", left)
            self.pieces += [self.left, self.right]
            return self.left, self.right
        half = self.left.shape[0] // 2
        top = lax.ppermute(clock(self.left[:half]), "dp", right)
        bottom = lax.ppermute(clock(self.right[half:]), "dp", left)
        self.pieces.append((top, bottom))
        return top, bottom


def ring_sources():
    size = lax.axis_size("dp")
    here = lax.axis_index("dp")
    place = jnp.where(here % 2 == 0, here // 2, size - 1 - here // 2)
    sources = []
    for offset in ring_offsets():
        at = (place + offset + size) % size
        sources.append(jnp.where(at < size // 2, 2 * at, 2 * (size - 1 - at) + 1).astype(jnp.int32))
    return sources


class Clock:
    def __init__(self):
        self.done = ()

    def tick(self, *done):
        self.done = done

    def __call__(self, value):
        return after(value, self.done) if self.done else value


class Conveyor:
    def __init__(self, clock, waiting):
        self.clock = clock
        self.waiting = list(waiting)
        self.going = []
        self.rings = []

    def push(self):
        ring = Ring(self.waiting.pop(0)())
        self.going.append((ring.step(self.clock), ring))
        self.rings.append(ring)
        return ring

    def advance(self, *computed):
        if not self.going:
            self.clock.tick(self.clock.done, computed)
            return
        came, ring = self.going.pop(0)
        self.clock.tick(came, *computed)
        if not ring.complete():
            self.going.append((ring.step(self.clock), ring))
            if ring.complete() and self.waiting:
                self.push()

    def until(self, ring, *computed):
        self.clock.tick(self.clock.done, computed)
        while not ring.complete() or any(r is ring for _, r in self.going):
            self.advance(self.clock.done)


def partner(operand, bit):
    size = lax.axis_size("seq")
    return lax.ppermute(operand, "seq", [(i, i ^ bit) for i in range(size)])


def seq_pieces(own):
    across = partner(own, 2)
    return [own, partner(own, 1), across, partner(across, 1)]


def seq_shares(keep, give):
    arrived = partner(give, 1)
    sent = (keep[1].astype(F32) + arrived[1].astype(F32)).astype(BF16)
    return (keep, arrived, partner(sent, 2)), sent


def total(shares):
    keep, arrived, across = shares
    return keep[0].astype(F32) + arrived[0].astype(F32) + across.astype(F32)


def everywhere_order(sources):
    seq = lax.axis_index("seq")
    return jnp.stack([s * 4 + (seq ^ bit) for s in sources for bit in range(4)]).astype(jnp.int32)


VMEM_LIMIT = 56 * 2**20
SMEM = pl.BlockSpec(memory_space=pltpu.SMEM)
VMEM = pl.BlockSpec(memory_space=pltpu.VMEM)


def call(kernel, name, flops=0, **options):
    return pl.pallas_call(
        kernel,
        compiler_params=pltpu.CompilerParams(vmem_limit_bytes=VMEM_LIMIT),
        cost_estimate=pl.CostEstimate(flops=int(flops), bytes_accessed=0, transcendentals=0),
        name=name,
        **options,
    )


def shape(dims, dtype):
    return jax.ShapeDtypeStruct(dims, dtype)


def fixed(*dims):
    return pl.BlockSpec(dims, lambda *_: (0,) * len(dims))


def columns_kernel(n_dp, gate_ref, up_ref, *out_refs):
    size = gate_ref.shape[1] // (4 * n_dp)
    for half, out in enumerate(out_refs):
        for m, ref in enumerate((gate_ref, up_ref)):
            for q in range(n_dp // 2):
                place = (m * (n_dp // 2) + q) * size
                for j in range(4):
                    start = ((half * (n_dp // 2) + q) * 4 + j) * size
                    out[j, :, place : place + size] = ref[:, start : start + size]


def columns_for_seq(gate, up, n_dp):
    rows, total = gate.shape
    return call(
        functools.partial(columns_kernel, n_dp),
        "columns",
        in_specs=[VMEM] * 2,
        out_shape=[shape((4, rows, total // 4), BF16)] * 2,
    )(gate, up)


ANY = pl.BlockSpec(memory_space=pl.ANY)


def place_kernel(count, sources_ref, *refs):
    pieces, outs, sems = refs[: -count - 1], refs[-count - 1 : -1], refs[-1]
    copies = []
    for i, piece in enumerate(pieces):
        rows = piece.shape[0] // count
        start = pl.multiple_of(sources_ref[i] * rows, rows)
        for j, out in enumerate(outs):
            part = piece.at[pl.ds(j * rows, rows)]
            copies.append(pltpu.make_async_copy(part, out.at[pl.ds(start, rows)], sems.at[i, j]))
    for copy in copies:
        copy.start()
    for copy in copies:
        copy.wait()


def finish_kernel(count, source_ref, *refs):
    (top_ref, bottom_ref), outs, sems = refs[count : count + 2], refs[count + 2 : -1], refs[-1]
    copies = []
    if count == 2:
        rows = top_ref.shape[0]
        start = pl.multiple_of(source_ref[0] * rows, rows)
        for i, piece in enumerate((top_ref, bottom_ref)):
            copies.append(pltpu.make_async_copy(piece, outs[i].at[pl.ds(start, rows)], sems.at[i]))
    else:
        rows = top_ref.shape[0]
        for i, piece in enumerate((top_ref, bottom_ref)):
            start = pl.multiple_of(source_ref[0] * (2 * rows), 2 * rows) + i * rows
            copies.append(pltpu.make_async_copy(piece, outs[0].at[pl.ds(start, rows)], sems.at[i]))
    for copy in copies:
        copy.start()
    for copy in copies:
        copy.wait()


def place(pieces, sources, count):
    rows, columns = pieces[0].shape
    most = len(pieces)
    return call(
        functools.partial(place_kernel, count),
        "place",
        in_specs=[SMEM] + [VMEM] * most,
        out_specs=[ANY] * count,
        out_shape=[shape(((most + 1) * rows // count, columns), BF16)] * count,
        scratch_shapes=[pltpu.SemaphoreType.DMA((most, count))],
    )(jnp.stack(sources[:-1]), *pieces)


def finish(begun, pieces, sources):
    count = len(begun)
    return call(
        functools.partial(finish_kernel, count),
        "finish",
        in_specs=[SMEM] + [ANY] * count + [VMEM] * 2,
        out_specs=[ANY] * count,
        out_shape=[shape(m.shape, BF16) for m in begun],
        scratch_shapes=[pltpu.SemaphoreType.DMA((2,))],
        input_output_aliases={i + 1: i for i in range(count)},
    )(sources[-1][None], *begun, *pieces[-1])


def gather_rows(order_ref, source_ref, target_ref, rows):
    total = source_ref.shape[0]
    wide = min(256, total)
    each = wide // rows
    for i in range(total // wide):
        blocks = []
        for j in range(each):
            start = pl.multiple_of(order_ref[i * each + j] * rows, rows)
            blocks.append(source_ref[pl.ds(start, rows), :])
        target_ref[:, i * wide : (i + 1) * wide] = jnp.concatenate(blocks, axis=0).T


def qkv_kernel(order_ref, normed_ref, inner_ref, b_ref, *refs):
    pieces, (out_ref, left_ref) = refs[:-2], refs[-2:]

    @pl.when(pl.program_id(0) == 0)
    def _():
        gather_rows(order_ref, normed_ref, left_ref, pieces[0].shape[0])

    width = pieces[0].shape[1]
    step = 512
    for c in range(0, width, step):
        right = jnp.concatenate([p[:, c : c + step] for p in pieces], axis=0)
        sums = contract(left_ref[...], right, 1, 0)
        sums = sums + contract(inner_ref[...], b_ref[:, c : c + step], 1, 0)
        out_ref[c : c + step, :] = sums.T


def project_in(order, normed_t, inner, b_in, pieces):
    width, tokens = normed_t.shape
    total = b_in.shape[1]
    step = 1024
    rows = pieces[0].shape[0]
    return call(
        qkv_kernel,
        "project_in",
        grid=(total // step,),
        in_specs=[
            SMEM,
            fixed(width, tokens),
            fixed(*inner.shape),
            pl.BlockSpec((b_in.shape[0], step), lambda c: (0, c)),
        ]
        + [pl.BlockSpec((rows, step), lambda c: (0, c))] * len(pieces),
        out_specs=pl.BlockSpec((step, tokens), lambda c: (c, 0)),
        out_shape=shape((total, tokens), F32),
        scratch_shapes=[pltpu.VMEM((tokens, width), BF16)],
    )(order, normed_t, inner, b_in, *pieces)


def out_kernel(order_ref, mixed_ref, inner_ref, b_ref, tokens_ref, valid_ref, gain_ref, *refs):
    pieces, (hidden_ref, normed_ref, left_ref) = refs[:-3], refs[-3:]
    c = pl.program_id(0)

    @pl.when(c == 0)
    def _():
        gather_rows(order_ref, mixed_ref, left_ref, pieces[0].shape[0])

    width = pieces[0].shape[1]
    right = jnp.concatenate([p[...] for p in pieces], axis=0)
    sums = contract(left_ref[...], right, 1, 0) + contract(inner_ref[...], b_ref[...], 0, 0)
    sums = tokens_ref[...].astype(F32) + valid_ref[...] * sums
    hidden_ref[:, pl.ds(pl.multiple_of(c * width, width), width)] = sums

    @pl.when(c == pl.num_programs(0) - 1)
    def _():
        hidden = hidden_ref[...]
        normed_ref[...] = rms_scale(hidden, gain_ref[...]).astype(BF16)


def project_out(order, mixed, inner, bo, tokens, valid, gain, pieces):
    features, block = mixed.shape
    width = tokens.shape[1]
    step = 1024
    rows = pieces[0].shape[0]
    skip = (pieces[0].shape[1] - width) // step
    return call(
        out_kernel,
        "project_out",
        grid=(width // step,),
        in_specs=[
            SMEM,
            fixed(features, block),
            fixed(*inner.shape),
            pl.BlockSpec((RANK, step), lambda c: (0, c)),
            pl.BlockSpec((block, step), lambda c: (0, c)),
            fixed(block, 1),
            fixed(1, width),
        ]
        + [pl.BlockSpec((rows, step), lambda c: (0, c + skip))] * len(pieces),
        out_specs=[fixed(block, width), fixed(block, width)],
        out_shape=[shape((block, width), F32), shape((block, width), BF16)],
        scratch_shapes=[pltpu.VMEM((block, features), BF16)],
    )(order, mixed, inner, bo, tokens, valid, gain, *pieces)


def scatter_products(order_ref, pieces, right, sums_ref, form):
    rows = pieces[0].shape[0]
    each = max(1, 256 // rows)
    for i in range(0, len(pieces), each):
        left = jnp.concatenate([p[...] for p in pieces[i : i + each]], axis=0)
        product = contract(left, right, 1, form)
        for j in range(each):
            start = pl.multiple_of(order_ref[i + j] * rows, rows)
            sums_ref[pl.ds(start, rows), :] += product[j * rows : (j + 1) * rows]


def out_back_kernel(order_ref, grad_ref, a_ref, inner_ref, *refs):
    pieces, (out_ref, sums_ref) = refs[:-2], refs[-2:]
    c = pl.program_id(0)

    @pl.when(c == 0)
    def _():
        sums_ref[...] = contract(a_ref[...], inner_ref[...], 0, 1)

    scatter_products(order_ref, pieces, grad_ref[...], sums_ref, 1)

    @pl.when(c == pl.num_programs(0) - 1)
    def _():
        out_ref[...] = sums_ref[...].astype(BF16)


def project_out_back(order, grad, ao, d_inner, pieces):
    block, width = grad.shape
    features = ao.shape[1]
    step = 1024
    rows = pieces[0].shape[0]
    skip = (pieces[0].shape[1] - width) // step
    return call(
        out_back_kernel,
        "project_out_back",
        grid=(width // step,),
        in_specs=[
            SMEM,
            pl.BlockSpec((block, step), lambda c: (0, c)),
            fixed(*ao.shape),
            fixed(*d_inner.shape),
        ]
        + [pl.BlockSpec((rows, step), lambda c: (0, c + skip))] * len(pieces),
        out_specs=fixed(features, block),
        out_shape=shape((features, block), BF16),
        scratch_shapes=[pltpu.VMEM((features, block), F32)],
    )(order, grad, ao, d_inner, *pieces)


def in_back_kernel(order_ref, grad_ref, a_ref, inner_ref, tokens_ref, gain_ref, base_ref, *refs):
    pieces, (out_ref, sums_ref, turned_ref) = refs[:-3], refs[-3:]
    c = pl.program_id(0)

    @pl.when(c == 0)
    def _():
        sums_ref[...] = contract(a_ref[...], inner_ref[...], 0, 0)

    scatter_products(order_ref, pieces, grad_ref[...], sums_ref, 0)

    @pl.when(c == pl.num_programs(0) - 1)
    def _():
        size = sums_ref.shape[1]
        for i in range(0, sums_ref.shape[0], size):
            turned_ref[:, i : i + size] = sums_ref[i : i + size, :].T
        inputs = tokens_ref[...].astype(F32)
        grad = turned_ref[...] * gain_ref[...]
        scale = lax.rsqrt(jnp.mean(inputs * inputs, axis=-1, keepdims=True) + EPS)
        along = jnp.mean(inputs * grad, axis=-1, keepdims=True) * scale * scale
        out_ref[...] = (base_ref[...] + scale * (grad - inputs * along)).astype(BF16)


def project_in_back(order, d_linear, a_in, d_inner, tokens, gain, base, pieces):
    total, block = d_linear.shape
    width = tokens.shape[1]
    step = 1024
    rows = pieces[0].shape[0]
    return call(
        in_back_kernel,
        "project_in_back",
        grid=(total // step,),
        in_specs=[
            SMEM,
            pl.BlockSpec((step, block), lambda c: (c, 0)),
            fixed(*a_in.shape),
            fixed(*d_inner.shape),
            fixed(block, width),
            fixed(1, width),
            fixed(block, width),
        ]
        + [pl.BlockSpec((rows, step), lambda c: (0, c))] * len(pieces),
        out_specs=fixed(block, width),
        out_shape=shape((block, width), BF16),
        scratch_shapes=[pltpu.VMEM((width, block), F32), pltpu.VMEM((block, width), F32)],
    )(order, d_linear, a_in, d_inner, tokens, gain, base, *pieces)


def hidden_back_kernel(l0, l1, l2, r0, r1, r2, hidden_ref, cot_ref, valid_ref, gain_ref, b_ref, dh_ref, gu_ref, inner_ref):
    half = l2.shape[1]
    for i, refs in enumerate(((l0, l1, l2), (r0, r1, r2))):
        part = slice(i * half, (i + 1) * half)
        grad = refs[0][0].astype(F32) + refs[1][0].astype(F32) + refs[2][...].astype(F32)
        dh_ref[:, part] = grad * gain_ref[:, part]
    hidden, grad = hidden_ref[...], dh_ref[...]
    scale = lax.rsqrt(jnp.mean(hidden * hidden, axis=-1, keepdims=True) + EPS)
    along = jnp.mean(hidden * grad, axis=-1, keepdims=True) * scale * scale
    grad = cot_ref[...].astype(F32) + scale * (grad - hidden * along)
    dh_ref[...] = grad
    low = (valid_ref[...] * grad).astype(BF16)
    gu_ref[...] = low
    inner_ref[...] = contract(low, b_ref[...], 1, 1).astype(BF16)


def hidden_back(left, right, hidden, cot, valid, gain, bo):
    block, width = hidden.shape
    return call(
        hidden_back_kernel,
        "hidden_back",
        flops=7e9,
        out_shape=[shape((block, width), F32), shape((block, width), BF16), shape((block, RANK), BF16)],
    )(*left, *right, hidden, cot, valid, gain, bo)


def gather_tokens(refs, whole_ref):
    block = refs[0].shape[0]
    for i, ref in enumerate(refs):
        whole_ref[i * block : (i + 1) * block, :] = ref[...]


def lower_back_kernel(g0, g1, g2, g3, weight_ref, b_ref, a_ref, out_ref, inner_ref, whole_ref):
    @pl.when(pl.program_id(0) == 0)
    def _():
        gather_tokens((g0, g1, g2, g3), whole_ref)
        inner_ref[...] = contract(whole_ref[...], b_ref[...], 1, 1).astype(BF16)

    sums = contract(whole_ref[...], weight_ref[...], 1, 1)
    out_ref[...] = (sums + contract(inner_ref[...], a_ref[...], 1, 0)).astype(BF16)


def lower_back(grads, weight, bd, ad):
    block, width = grads[0].shape
    units = weight.shape[0]
    step = 256
    tokens = 4 * block
    return call(
        lower_back_kernel,
        "lower_back",
        grid=(units // step,),
        in_specs=[fixed(block, width)] * 4
        + [
            pl.BlockSpec((step, width), lambda j: (j, 0)),
            fixed(RANK, width),
            pl.BlockSpec((RANK, step), lambda j: (0, j)),
        ],
        out_specs=[pl.BlockSpec((tokens, step), lambda j: (0, j)), fixed(tokens, RANK)],
        out_shape=[shape((tokens, units), BF16), shape((tokens, RANK), BF16)],
        scratch_shapes=[pltpu.VMEM((tokens, width), BF16)],
    )(*grads, weight, bd, ad)


def tokens_kernel(n0, n1, n2, n3, a_ref, whole_ref, low_ref):
    gather_tokens((n0, n1, n2, n3), whole_ref)
    low_ref[...] = contract(whole_ref[...], a_ref[...], 1, 1).astype(BF16)


def all_tokens(normed, a_gu):
    block, width = normed[0].shape
    return call(
        tokens_kernel,
        "all_tokens",
        out_shape=[shape((4 * block, width), BF16), shape((4 * block, 2 * RANK), BF16)],
    )(*normed, a_gu)


def units_kernel(
    whole_ref,
    low_ref,
    gate_ref,
    up_ref,
    bg_ref,
    bu_ref,
    ad_ref,
    d_act_ref,
    act_ref,
    dg_ref,
    du_ref,
    inner_ref,
):
    @pl.when(pl.program_id(0) == 0)
    def _():
        inner_ref[...] = jnp.zeros(inner_ref.shape, F32)

    low_gate, low_up = low_ref[:, :RANK], low_ref[:, RANK:]
    gate = contract(whole_ref[...], gate_ref[...], 1, 0) + contract(low_gate, bg_ref[...], 1, 0)
    up = contract(whole_ref[...], up_ref[...], 1, 0) + contract(low_up, bu_ref[...], 1, 0)
    d_act = d_act_ref[...].astype(F32)
    sig = jax.nn.sigmoid(gate)
    silu = gate * sig
    act = (silu * up).astype(BF16)
    d_gate = (d_act * up * (sig + silu * (1.0 - sig))).astype(BF16)
    d_up = (d_act * silu).astype(BF16)
    act_ref[...] = act
    dg_ref[...] = d_gate
    du_ref[...] = d_up
    inner_ref[:, :RANK] += contract(d_gate, bg_ref[...], 1, 1)
    inner_ref[:, RANK : 2 * RANK] += contract(d_up, bu_ref[...], 1, 1)
    inner_ref[:, 2 * RANK :] += contract(act, ad_ref[...], 1, 1)


def units(part, whole, low, both, bg, bu, ad, d_act):
    tokens, width = whole.shape
    half = both.shape[1] // 2
    step = 256
    steps = half // step
    here = pl.BlockSpec((RANK, step), lambda j: (0, part * steps + j))
    tile = pl.BlockSpec((tokens, step), lambda j: (0, j))
    return call(
        units_kernel,
        "units",
        grid=(steps,),
        in_specs=[
            fixed(tokens, width),
            fixed(tokens, 2 * RANK),
            pl.BlockSpec((width, step), lambda j: (0, j)),
            pl.BlockSpec((width, step), lambda j: (0, steps + j)),
            here,
            here,
            here,
            pl.BlockSpec((tokens, step), lambda j: (0, part * steps + j)),
        ],
        out_specs=[tile] * 3 + [fixed(tokens, 3 * RANK)],
        out_shape=[shape((tokens, half), BF16)] * 3 + [shape((tokens, 3 * RANK), F32)],
    )(whole, low, both, both, bg, bu, ad, d_act)


def units_grads_kernel(low_ref, d_down_ref, act_ref, dg_ref, du_ref, gbg_ref, gbu_ref, gad_ref):
    gbg_ref[...] = contract(low_ref[:, :RANK], dg_ref[...], 0, 0)
    gbu_ref[...] = contract(low_ref[:, RANK:], du_ref[...], 0, 0)
    gad_ref[...] = contract(d_down_ref[...], act_ref[...], 0, 0)


def units_grads(low, d_down, act, d_gate, d_up):
    tokens, half = act.shape
    step = 256
    tile = pl.BlockSpec((tokens, step), lambda j: (0, j))
    thin = pl.BlockSpec((RANK, step), lambda j: (0, j))
    return call(
        units_grads_kernel,
        "units_grads",
        grid=(half // step,),
        in_specs=[fixed(tokens, 2 * RANK), fixed(tokens, RANK), tile, tile, tile],
        out_specs=[thin] * 3,
        out_shape=[shape((RANK, half), F32)] * 3,
    )(low, d_down, act, d_gate, d_up)


def units_back_first_kernel(g_ref, u_ref, w_ref, out_ref):
    half = g_ref.shape[1]
    sums = contract(g_ref[...], w_ref[:, :half], 1, 1) + contract(u_ref[...], w_ref[:, half:], 1, 1)
    out_ref[...] = sums.astype(BF16)


def units_back_first(d_gate, d_up, both):
    tokens, half = d_gate.shape
    width = both.shape[0]
    step = 256
    return call(
        units_back_first_kernel,
        "units_back_first",
        grid=(width // step,),
        in_specs=[fixed(tokens, half)] * 2 + [pl.BlockSpec((step, 2 * half), lambda n: (n, 0))],
        out_specs=pl.BlockSpec((tokens, step), lambda n: (0, n)),
        out_shape=shape((tokens, width), BF16),
    )(d_gate, d_up, both)


def units_back_kernel(first_ref, g_ref, u_ref, w_ref, ia_ref, ib_ref, a_ref, keep_ref, give_ref):
    half = g_ref.shape[1]
    low = (ia_ref[...] + ib_ref[...]).astype(BF16)[:, : 2 * RANK]
    sums = first_ref[...].astype(F32) + contract(low, a_ref[...], 1, 0)
    sums = sums + contract(g_ref[...], w_ref[:, :half], 1, 1)
    sums = sums + contract(u_ref[...], w_ref[:, half:], 1, 1)
    sums = sums.astype(BF16)
    block = keep_ref.shape[1]
    keep_ref[0] = sums[:block]
    give_ref[0] = sums[block : 2 * block]
    keep_ref[1] = sums[2 * block : 3 * block]
    give_ref[1] = sums[3 * block :]


def units_back(part, parts, first, d_gate, d_up, both, inners, a_gu):
    tokens, half = d_gate.shape
    width = both.shape[0]
    step = 256
    steps = width // parts // step
    place = lambda n: part * steps + n
    out = pl.BlockSpec((2, tokens // 4, step), lambda n: (0, 0, n))
    return call(
        units_back_kernel,
        "units_back",
        grid=(steps,),
        in_specs=[
            pl.BlockSpec((tokens, step), lambda n: (0, place(n))),
            fixed(tokens, half),
            fixed(tokens, half),
            pl.BlockSpec((step, 2 * half), lambda n: (place(n), 0)),
            fixed(tokens, 3 * RANK),
            fixed(tokens, 3 * RANK),
            pl.BlockSpec((2 * RANK, step), lambda n: (0, place(n))),
        ],
        out_specs=[out, out],
        out_shape=[shape((2, tokens // 4, width // parts), BF16)] * 2,
    )(first, d_gate, d_up, both, *inners, a_gu)


def lower_kernel(
    aa_ref, ab_ref, weight_ref, ia_ref, ib_ref, b_ref, whole_ref, g0, g1, g2, g3, keep_ref, give_ref, grad_ref, grad_gu_ref
):
    inner = (ia_ref[...] + ib_ref[...]).astype(BF16)
    low = inner[:, 2 * RANK :]
    half = aa_ref.shape[1]
    sums = contract(low, b_ref[...], 1, 0)
    sums = sums + contract(aa_ref[...], weight_ref[:half], 1, 0)
    sums = sums + contract(ab_ref[...], weight_ref[half:], 1, 0)
    sums = sums.astype(BF16)
    block = g0.shape[0]
    grad = jnp.zeros(grad_ref.shape, F32)
    for i, g in enumerate((g0, g1, g2, g3)):
        out = give_ref if i % 2 else keep_ref
        out[i // 2] = sums[i * block : (i + 1) * block]
        grad = grad + contract(low[i * block : (i + 1) * block], g[...], 0, 0)
    grad_ref[...] = grad
    grad_gu_ref[...] = contract(inner[:, : 2 * RANK], whole_ref[...], 0, 0)


def lower(act_a, act_b, weight, inners, bd, grads, whole):
    block, width = grads[0].shape
    tokens, half = act_a.shape
    step = 256
    tile = pl.BlockSpec((block, step), lambda n: (0, n))
    thin = pl.BlockSpec((RANK, step), lambda n: (0, n))
    out = pl.BlockSpec((2, block, step), lambda n: (0, 0, n))
    return call(
        lower_kernel,
        "lower",
        grid=(width // step,),
        in_specs=[
            fixed(tokens, half),
            fixed(tokens, half),
            pl.BlockSpec((2 * half, step), lambda n: (0, n)),
            fixed(tokens, 3 * RANK),
            fixed(tokens, 3 * RANK),
            thin,
            pl.BlockSpec((tokens, step), lambda n: (0, n)),
        ]
        + [tile] * 4,
        out_specs=[out, out, thin, pl.BlockSpec((2 * RANK, step), lambda n: (0, n))],
        out_shape=[shape((2, block, width), BF16)] * 2
        + [shape((RANK, width), F32), shape((2 * RANK, width), F32)],
    )(act_a, act_b, weight, *inners, bd, whole, *grads)


def wide_heads(ref):
    return jnp.concatenate([ref[h * HD : (h + 1) * HD] for h in range(GROUP)], axis=1)


def attend_kernel(seq_ref, limit_ref, q_ref, kv0, kv1, kv2, kv3, o_ref, e_ref, r_ref):
    queries = wide_heads(q_ref)
    limit = limit_ref[...]
    total = jnp.zeros(limit.shape, F32)
    mixed = jnp.zeros(queries.shape, F32)
    for bit, ref in enumerate((kv0, kv1, kv2, kv3)):
        block = ref.shape[2]
        scores = contract(ref[0, :HD], queries, 0, 0)
        places = (seq_ref[0] ^ bit) * block + lax.broadcasted_iota(jnp.int32, scores.shape, 0)
        raised = jnp.where(places <= limit, jnp.exp(scores), 0.0)
        total = total + jnp.sum(raised, axis=0, keepdims=True)
        low = raised.astype(BF16)
        e_ref[0, bit] = low
        mixed = mixed + contract(ref[0, HD:], low, 1, 0)
    inverse = 1.0 / total
    r_ref[0] = inverse
    mixed = (mixed * inverse).astype(BF16)
    width = q_ref.shape[1]
    for h in range(GROUP):
        o_ref[h * HD : (h + 1) * HD] = mixed[:, h * width : (h + 1) * width]


def attend(seq, limit, queries, keys_values):
    block = keys_values[0].shape[2]
    width = queries.shape[1]
    wide = GROUP * width
    head_rows = pl.BlockSpec((GROUP * HD, width), lambda g: (g, 0))
    return call(
        attend_kernel,
        "attend",
        grid=(KV,),
        in_specs=[SMEM, fixed(1, wide), head_rows]
        + [pl.BlockSpec((1, 2 * HD, block), lambda g: (g, 0, 0))] * 4,
        out_specs=[
            head_rows,
            pl.BlockSpec((1, 4, block, wide), lambda g: (g, 0, 0, 0)),
            pl.BlockSpec((1, 1, wide), lambda g: (g, 0, 0)),
        ],
        out_shape=[
            shape(queries.shape, BF16),
            shape((KV, 4, block, wide), BF16),
            shape((KV, 1, wide), F32),
        ],
    )(seq[None], limit, queries, *keys_values)


def attend_back_kernel(q_ref, kv0, kv1, kv2, kv3, e_ref, r_ref, o_ref, do_ref, dq_ref, keep_ref, give_ref):
    width = q_ref.shape[1]
    queries = wide_heads(q_ref)
    grads = wide_heads(do_ref).astype(F32) * r_ref[0]
    dots = jnp.sum(grads * wide_heads(o_ref).astype(F32), axis=0, keepdims=True)
    grads = grads.astype(BF16)
    d_queries = jnp.zeros(queries.shape, F32)
    for bit, ref in enumerate((kv0, kv1, kv2, kv3)):
        out = give_ref if bit % 2 else keep_ref
        raised = e_ref[0, bit]
        d_probs = contract(ref[0, HD:], grads, 0, 0)
        d_scores = (raised.astype(F32) * (d_probs - dots)).astype(BF16)
        d_queries = d_queries + contract(ref[0, :HD], d_scores, 1, 0)
        out[bit // 2, 0, :HD] = contract(queries, d_scores, 1, 1).astype(BF16)
        out[bit // 2, 0, HD:] = contract(grads, raised, 1, 1).astype(BF16)
    for h in range(GROUP):
        dq_ref[h * HD : (h + 1) * HD] = d_queries[:, h * width : (h + 1) * width]


def attend_back(first, count, queries, keys_values, raised, inverse, mixed, d_mixed):
    block = keys_values[0].shape[2]
    width = queries.shape[1]
    wide = GROUP * width
    head_rows = pl.BlockSpec((GROUP * HD, width), lambda g: (first + g, 0))
    shares = pl.BlockSpec((2, 1, 2 * HD, block), lambda g: (0, g, 0, 0))
    return call(
        attend_back_kernel,
        "attend_back",
        grid=(count,),
        in_specs=[head_rows]
        + [pl.BlockSpec((1, 2 * HD, block), lambda g: (first + g, 0, 0))] * 4
        + [
            pl.BlockSpec((1, 4, block, wide), lambda g: (first + g, 0, 0, 0)),
            pl.BlockSpec((1, 1, wide), lambda g: (first + g, 0, 0)),
            head_rows,
            head_rows,
        ],
        out_specs=[pl.BlockSpec((GROUP * HD, width), lambda g: (g, 0)), shares, shares],
        out_shape=[
            shape((count * GROUP * HD, width), F32),
            shape((2, count, 2 * HD, block), BF16),
            shape((2, count, 2 * HD, block), BF16),
        ],
    )(queries, *keys_values, raised, inverse, mixed, d_mixed)


def pick_kernel(ids_ref, *refs):
    out_ref = refs[-1]
    for d in range(out_ref.shape[0]):
        parts = [ref[ids_ref[d]] for ref in refs[:-1]]
        out_ref[d] = jnp.concatenate(parts, axis=1)


def pick(ids, stacks):
    columns = sum(stack.shape[2] for stack in stacks)
    n_dp = ids.shape[0]
    return call(
        pick_kernel,
        "pick",
        in_specs=[SMEM] + [VMEM] * len(stacks),
        out_shape=shape((n_dp, RANK, columns), BF16),
    )(ids, *stacks)


def spread_kernel(widths, seq_ref, mine_ref, p1, p2, p3, *refs):
    (in_ref, grow_ref, ao_ref, bo_ref, gu_ref, bd_ref, bg_ref, bu_ref, ad_ref, all_ref) = refs
    local, each, thin = widths
    n_dp = mine_ref.shape[0]
    seq = seq_ref[0]
    base = 3 * local
    all_ref[seq] = mine_ref[:, :, base:]
    for bit, ref in ((1, p1), (2, p2), (3, p3)):
        all_ref[seq ^ bit] = ref[...]

    def factor(start, width):
        parts = [all_ref[j, d, :, start : start + width] for d in range(n_dp) for j in range(4)]
        return jnp.concatenate(parts, axis=1)

    wide = lambda m: factor(m * each, each)
    for i in range(3):
        in_ref[i * RANK : (i + 1) * RANK] = wide(i)
    grow_ref[...] = jnp.zeros(grow_ref.shape, BF16)
    n_query, n_key = 4 * n_dp * each, 4 * n_dp * thin
    grow_ref[:RANK, :n_query] = wide(3)
    for i in range(2):
        start = n_query + i * n_key
        grow_ref[(i + 1) * RANK : (i + 2) * RANK, start : start + n_key] = factor(9 * each + i * thin, thin)
    ao_ref[...] = wide(4)
    bo_ref[...] = wide(5)
    gu_ref[:RANK] = wide(6)
    gu_ref[RANK:] = wide(7)
    bd_ref[...] = wide(8)
    for i, ref in enumerate((bg_ref, bu_ref, ad_ref)):
        for d in range(n_dp):
            ref[:, d * local : (d + 1) * local] = mine_ref[d, :, i * local : (i + 1) * local]


def spread(seq, mine, others, widths):
    local, each, thin = widths
    n_dp = mine.shape[0]
    total = 4 * n_dp * each
    grown = total + 8 * n_dp * thin
    rows = [(3 * RANK, total), (3 * RANK, grown), (RANK, total), (RANK, total), (2 * RANK, total), (RANK, total)]
    rows += [(RANK, n_dp * local)] * 3
    return call(
        functools.partial(spread_kernel, widths),
        "spread",
        in_specs=[SMEM] + [VMEM] * 4,
        out_shape=[shape(dims, BF16) for dims in rows],
        scratch_shapes=[pltpu.VMEM((4,) + others[0].shape, BF16)],
    )(seq[None], mine, *others)


def pack_kernel(n_dp, count, seq_ref, *refs):
    ins, refs = refs[:count], refs[count:]
    alone, (keep_ref, give_ref, alone_ref, all_ref) = refs[:-4], refs[-4:]
    for d in range(n_dp):
        for j in range(4):
            parts = []
            for ref in ins:
                each = ref.shape[1] // (4 * n_dp)
                at = (d * 4 + j) * each
                parts.append(ref[:, at : at + each])
            all_ref[j, d] = jnp.concatenate(parts, axis=1).astype(BF16)
    seq = seq_ref[0]
    for bit in range(4):
        out = give_ref if bit % 2 else keep_ref
        out[bit // 2] = all_ref[seq ^ bit]
    for i in range(0, len(alone), 2):
        for half in range(2):
            size = alone[i].shape[1] // (n_dp // 2)
            for d in range(n_dp // 2):
                place = slice((i // 2) * size, (i // 2 + 1) * size)
                part = alone[i + half][:, d * size : (d + 1) * size]
                alone_ref[half * (n_dp // 2) + d, :, place] = part.astype(BF16)


def pack(seq, grads, n_dp, alone):
    columns = sum(g.shape[1] for g in grads) // (4 * n_dp)
    dims = (n_dp, RANK, columns)
    outs = [shape((2,) + dims, BF16)] * 2
    outs.append(shape((n_dp, RANK, sum(g.shape[1] for g in alone) // n_dp), BF16))
    return call(
        functools.partial(pack_kernel, n_dp, len(grads)),
        "pack",
        in_specs=[SMEM] + [VMEM] * (len(grads) + len(alone)),
        out_shape=outs,
        scratch_shapes=[pltpu.VMEM((4,) + dims, BF16)],
    )(seq[None], *grads, *alone)


def sort_kernel(widths, ids_ref, came_ref, *out_refs):
    came = [came_ref[d].astype(F32) for d in range(came_ref.shape[0])]
    for a in range(ADAPT):
        total = jnp.zeros(came[0].shape, F32)
        for d, value in enumerate(came):
            total = total + jnp.where(ids_ref[d] == a, value, 0.0)
        at = 0
        for ref, width in zip(out_refs, widths):
            part = total[:, at : at + width]
            ref[a] = part.T if width < 64 else part
            at += width


def sort(ids, came, widths):
    outs = call(
        functools.partial(sort_kernel, widths),
        "sort",
        in_specs=[SMEM, VMEM],
        out_shape=[shape((ADAPT, w, RANK) if w < 64 else (ADAPT, RANK, w), F32) for w in widths],
    )(ids, came)
    return [o if w < 64 else o.transpose(0, 2, 1) for o, w in zip(outs, widths)]


def shards(
    tokens,
    cotangent,
    lengths,
    adapter_ids,
    attn_gain,
    query_gain,
    key_gain,
    ffn_gain,
    w_query,
    w_key,
    w_value,
    w_out,
    gate_weight,
    w_up,
    w_down,
    a_query,
    b_query,
    a_key,
    b_key,
    a_value,
    b_value,
    a_out,
    b_out,
    a_gate,
    b_gate,
    a_up,
    b_up,
    a_down,
    b_down,
):
    n_dp = lax.axis_size("dp")
    seq = lax.axis_index("seq")
    _, block, width = tokens.shape
    length = lengths[0]
    positions = seq * block + jnp.arange(block)
    valid = (positions < length).astype(F32)[:, None]
    sources = ring_sources()
    clock = Clock()
    n_query, n_key = H * HD, KV * HD
    local, each, thin = b_gate.shape[1], a_query.shape[1], b_key.shape[1]
    widths = (local, each, thin)

    attn = Ring(jnp.concatenate([w_query, w_key, w_value, w_out], axis=1))
    first_came, age = None, 0
    queue = [attn.pieces[0]]
    sides, acrosses, corners, going = [], [], [], []
    arrived = slot = 0
    last = attn.steps - 1
    while len(corners) < n_dp + 1:
        waits, new = [], []
        if not attn.complete():
            new = attn.step(clock)
            waits += new
            if attn.complete():
                ended = new
                new = [new]
        elif first_came is not None:
            age += 1
            if age == 3:
                waits += first_came
                first_came = None
        elif not first_ring.complete():
            first_came, age = first_ring.step(lambda v: after(v, ended) if len(first_ring.pieces) == 1 else clock(v)), 0
        while len(acrosses) < len(queue) and len(going) < 2:
            acrosses.append(partner(clock(queue[len(acrosses)]), 2))
            going.append(len(acrosses))
        for _ in range(3):
            if len(corners) < arrived:
                corners.append(partner(clock(acrosses[len(corners)]), 1))
                waits.append(corners[-1])
            elif len(sides) < len(queue):
                sides.append(partner(clock(queue[len(sides)]), 1))
                waits.append(sides[-1])
        if slot == 0:
            slots_a, slots_b = columns_for_seq(gate_weight, w_up, n_dp)
            ids = lax.all_to_all(
                jnp.broadcast_to(adapter_ids[None], (n_dp, 128)), "dp", 0, 0, tiled=True
            )[:, 0]
            stacks = (b_gate, b_up, a_down, a_query, a_key, a_value, b_query, a_out, b_out)
            stacks += (a_gate, a_up, b_down, b_key, b_value)
            sent = pick(ids, [m.transpose(0, 2, 1) for m in stacks])
            waits += [sent, slots_a]
        if slot == 1:
            swapped_a = lax.all_to_all(clock(slots_a), "seq", 0, 0, tiled=True)
        if slot == 2:
            mine = lax.all_to_all(clock(sent), "dp", 0, 0, tiled=True)
            first_ring = Ring(jnp.concatenate([w_down, swapped_a.reshape(-1, width)], axis=0))
            waits.append(first_ring.pieces[0])
        if slot == last + 2:
            inputs = clock(tokens)[0].astype(F32)
            normed = rms_scale(inputs, attn_gain).astype(BF16)
            normed_t = normed.T
            cot = cotangent[0].astype(F32)
            grad_out = (valid * clock(cot)).astype(BF16)
            waits += [normed_t, grad_out]
        if going and (slot == 0 or len(going) == 2 or len(queue) == n_dp + 1):
            waits.append(acrosses[going[0] - 1])
        else:
            going = going[:0] + going
        clock.tick(*waits)
        if going and any(w is acrosses[going[0] - 1] for w in waits):
            arrived = going.pop(0)
        if slot == 2:
            queue.append(clock(mine)[..., 3 * local :])
        queue += [jnp.concatenate(p, axis=0) if isinstance(p, tuple) else p for p in new]
        slot += 1
    others = [sides.pop(5), acrosses.pop(5), corners.pop(5)]
    queue.pop(5)
    attn_pieces = []
    for group in zip(queue, sides, acrosses, corners):
        attn_pieces += group
    order = everywhere_order(sources)

    belt = Conveyor(clock, [lambda: swapped_b.reshape(-1, width)])
    if first_came is None and not first_ring.complete():
        first_came = first_ring.step(clock)
    if first_came is not None:
        belt.going.append((first_came, first_ring))
    a_in, b_in, ao, bo, a_gu, bd, bg, bu, ad = spread(seq, mine, clock(others), widths)
    inner = contract(normed, a_in, 1, 1).astype(BF16)

    linear = project_in(order, normed_t, inner, b_in, attn_pieces)
    query_lin = linear[:n_query].reshape(H, HD, block)
    key_lin = linear[n_query : n_query + n_key].reshape(KV, HD, block)
    value_lin = linear[n_query + n_key :].reshape(KV, HD, block)
    cosine, sine = rotary_tables(positions)
    scale = HD**-0.5
    query_prep = lambda v: prepare(v, query_gain, cosine, sine)
    key_prep = lambda v: prepare(v, key_gain, cosine, sine)
    keys_values = jnp.concatenate([key_prep(key_lin), value_lin], axis=1).astype(BF16)
    keys_values = seq_pieces(keys_values)
    queries = (query_prep(query_lin) * scale).astype(BF16).reshape(n_query, block)
    limit = jnp.minimum(positions, length - 1).astype(jnp.int32)
    limit = jnp.tile(limit, GROUP)[None, :]
    belt.advance(queries)
    grads = seq_pieces(after(grad_out, keys_values[2]))
    mixed, raised, inverse = attend(seq, limit, queries, keys_values)
    swapped_b = lax.all_to_all(after(slots_b, queries), "seq", 0, 0, tiled=True)
    belt.advance(mixed)

    inner_out = contract(ao, mixed, 1, 0).astype(BF16)
    hidden, normed_two = project_out(
        order, mixed, inner_out, bo, tokens[0], valid, ffn_gain[None], attn_pieces
    )

    n2 = seq_pieces(normed_two)
    while not first_ring.complete():
        belt.advance(normed_two)
    ring_b = belt.rings[0]
    begun = place(clock(first_ring.pieces[:-1]), sources, 2)
    belt.until(first_ring, begun)
    w_lower, both_a = finish(begun, first_ring.pieces, sources)
    d_act, d_down = lower_back(clock(grads), w_lower, bd, ad)
    belt.advance(d_act)
    n2, low_n2 = all_tokens(n2, a_gu)
    act_a, dg_a, du_a, inner_a = units(0, n2, low_n2, both_a, bg, bu, ad, d_act)
    belt.advance(act_a)
    first = units_back_first(clock(dg_a), du_a, both_a)
    gbg_a, gbu_a, gad_a = units_grads(low_n2, d_down, after(act_a, first), dg_a, du_a)
    while not ring_b.complete():
        belt.advance(gbg_a)
    begun = place(clock(ring_b.pieces[:-1]), sources, 1)
    belt.until(ring_b, begun)
    (both_b,) = finish(begun, ring_b.pieces, sources)
    act_b, dg_b, du_b, inner_b = units(1, n2, low_n2, both_b, bg, bu, ad, d_act)
    inners = (inner_a, inner_b)
    keep, give = units_back(0, 2, first, dg_b, du_b, both_b, inners, a_gu)
    left, sent = seq_shares(keep, give)
    keep, give = units_back(1, 2, after(first, sent), dg_b, du_b, both_b, inners, a_gu)
    right, sent = seq_shares(keep, give)

    keep, give, grad_bd, grad_a_gu = lower(
        act_a, after(act_b, sent), w_lower, inners, bd, grads, n2
    )

    d_hidden, grad_update, d_inner_out = hidden_back(
        after(left[:2], keep) + left[2:], after(right[:2], keep) + right[2:], hidden, cotangent[0], valid, ffn_gain[None], bo
    )
    lowered, sent = seq_shares(*after((keep, give), grad_update))
    d_mixed = project_out_back(order, after(grad_update, sent), ao, d_inner_out, attn_pieces)
    count = KV // 2
    back = lambda part, d_mixed: attend_back(
        part * count, count, queries, keys_values, raised, inverse, mixed, d_mixed
    )
    d_query, keep, give = back(0, d_mixed)
    gbg_b, gbu_b, gad_b = units_grads(low_n2, d_down, after(act_b, d_query), dg_b, du_b)
    give, gbg_b = after((give, gbg_b), lowered[2])
    first_kv, sent = seq_shares(keep, give)
    other_query, keep, give = back(1, after(d_mixed, sent))
    other_kv, sent = seq_shares(keep, give)

    first_kv = total(after(first_kv, other_query))
    d_query = after(jnp.concatenate([d_query, other_query], axis=0), first_kv)
    d_queries = d_query.reshape(H, HD, block) * scale
    d_kv = jnp.concatenate([first_kv, total(other_kv)], axis=0)
    d_query_lin = jax.vjp(query_prep, query_lin)[1](d_queries)[0]
    d_key_lin = jax.vjp(key_prep, key_lin)[1](d_kv[:, :HD])[0]
    d_linear = jnp.concatenate(
        [
            d_query_lin.reshape(n_query, block),
            d_key_lin.reshape(n_key, block),
            d_kv[:, HD:].reshape(n_key, block),
        ],
        axis=0,
    ).astype(BF16)
    output = (hidden + valid * total(after(lowered, d_linear))).astype(BF16)
    d_inner = contract(b_in, d_linear, 1, 0).astype(BF16)
    grad_tokens = project_in_back(
        order, d_linear, a_in, d_inner, tokens[0], attn_gain[None], d_hidden, attn_pieces
    )

    grad_ao = contract(d_inner_out, mixed, 0, 1)
    grad_bo = contract(inner_out, grad_update, 1, 0)
    grad_a_in = contract(d_inner, normed, 1, 0)
    grad_b_in = contract(inner, d_linear, 0, 1)
    q_end, k_end = n_query, n_query + n_key
    partial = [grad_ao, grad_bo, grad_a_gu[:RANK], grad_a_gu[RANK:], grad_bd]
    partial += [grad_a_in[i * RANK : (i + 1) * RANK] for i in range(3)]
    partial += [grad_b_in[:RANK, :q_end]]
    partial += [grad_b_in[RANK : 2 * RANK, q_end:k_end], grad_b_in[2 * RANK :, k_end:]]
    whole = (gbg_a, gbg_b, gbu_a, gbu_b, gad_a, gad_b)
    keep, give, whole = pack(seq, partial, n_dp, whole)
    (keep, arrived, across), _ = seq_shares(keep, give)
    summed = total((keep, arrived, across)).astype(BF16)
    summed = after(jnp.concatenate([summed, whole], axis=2), grad_tokens)
    sizes = [each] * 9 + [thin] * 2 + [local] * 3
    came = lax.all_to_all(summed, "dp", 0, 0, tiled=True)
    gao, gbo, gag, gau, gbd, gaq, gak, gav, gbq, gbk, gbv, gbg, gbu, gad = sort(ids, came, sizes)
    return (
        output[None],
        grad_tokens[None],
        gaq,
        gbq,
        gak,
        gbk,
        gav,
        gbv,
        gao,
        gbo,
        gag,
        gbg,
        gau,
        gbu,
        gad,
        gbd,
    )


def solution(mesh):
    tokens = P("dp", "seq", None)
    matrix = P(("dp", "seq"), None)
    stack = P(None, ("dp", "seq"), None)
    in_specs = (tokens, tokens, P("dp"), P("dp")) + (P(),) * 4 + (matrix,) * 7 + (stack,) * 14
    out_specs = (tokens, tokens) + (stack,) * 14
    return jax.shard_map(shards, mesh=mesh, in_specs=in_specs, out_specs=out_specs, check_vma=False)
```

```python
import functools

import jax
import jax.numpy as jnp
import numpy as np
from jax import lax
from jax.experimental import pallas as pl
from jax.experimental.pallas import tpu as pltpu
from jax.sharding import PartitionSpec as P

H = 32
KV = 8
HD = 64
GROUP = H // KV
ADAPT = 8
RANK = 16
EPS = 1e-05
F32 = jnp.float32
BF16 = jnp.bfloat16


def contract(left, right, left_dim, right_dim):
    return lax.dot_general(
        left, right, (((left_dim,), (right_dim,)), ((), ())), preferred_element_type=F32
    )


def rms_scale(operand, scaling, axis=-1):
    mean = jnp.mean(operand * operand, axis=axis, keepdims=True)
    return operand * lax.rsqrt(mean + EPS) * scaling


def rotary_tables(positions):
    frequency = jnp.power(1000000.0, -jnp.arange(HD // 2, dtype=F32) * 2.0 / HD)
    angles = frequency[:, None] * positions.astype(F32)[None, :]
    return jnp.cos(angles), jnp.sin(angles)


def prepare(linear, scaling, cosine, sine):
    normed = rms_scale(linear, scaling[:, None], axis=1)
    front, second = normed[:, : HD // 2], normed[:, HD // 2 :]
    return jnp.concatenate(
        [front * cosine - second * sine, second * cosine + front * sine], axis=1
    )


def after(value, *others):
    return lax.optimization_barrier((value, others))[0]


def ring_order(size):
    return list(range(0, size, 2)) + list(range(1, size, 2))[::-1]


def ring_pairs(size):
    order = ring_order(size)
    right = [(order[i], order[(i + 1) % size]) for i in range(size)]
    return right, [(b, a) for a, b in right]


def ring_offsets():
    offsets = [0]
    for step in range(1, (lax.axis_size("dp") - 1) // 2 + 1):
        offsets += [-step, step]
    return offsets + [lax.axis_size("dp") // 2]


class Ring:
    def __init__(self, own):
        self.pieces = [own]
        self.left = self.right = own
        self.steps = lax.axis_size("dp") // 2

    def complete(self):
        return len(self.pieces) == lax.axis_size("dp")

    def step(self, clock):
        size = lax.axis_size("dp")
        right, left = ring_pairs(size)
        if len(self.pieces) < size - 1:
            self.left = lax.ppermute(clock(self.left), "dp", right)
            self.right = lax.ppermute(clock(self.right), "dp", left)
            self.pieces += [self.left, self.right]
            return self.left, self.right
        half = self.left.shape[0] // 2
        last_left, last_right = clock((self.left, self.right))
        top = lax.ppermute(last_left[:half], "dp", right)
        bottom = lax.ppermute(last_right[half:], "dp", left)
        self.pieces.append((top, bottom))
        return top, bottom


def ring_sources():
    size = lax.axis_size("dp")
    here = lax.axis_index("dp")
    place = jnp.where(here % 2 == 0, here // 2, size - 1 - here // 2)
    sources = []
    for offset in ring_offsets():
        at = (place + offset + size) % size
        sources.append(jnp.where(at < size // 2, 2 * at, 2 * (size - 1 - at) + 1).astype(jnp.int32))
    return sources


class Clock:
    def __init__(self):
        self.done = ()

    def tick(self, *done):
        self.done = done

    def __call__(self, value):
        return after(value, self.done) if self.done else value


class Conveyor:
    def __init__(self, clock, waiting):
        self.clock = clock
        self.waiting = list(waiting)
        self.going = []
        self.rings = []

    def push(self):
        ring = Ring(self.waiting.pop(0)())
        self.going.append((ring.step(self.clock), ring))
        self.rings.append(ring)
        return ring

    def advance(self, *computed):
        if not self.going:
            self.clock.tick(self.clock.done, computed)
            return
        came, ring = self.going.pop(0)
        self.clock.tick(came, *computed)
        if not ring.complete():
            self.going.append((ring.step(self.clock), ring))
            if ring.complete() and self.waiting:
                self.push()

    def until(self, ring, *computed):
        self.clock.tick(self.clock.done, computed)
        while not ring.complete() or any(r is ring for _, r in self.going):
            self.advance(self.clock.done)


def partner(operand, bit):
    size = lax.axis_size("seq")
    return lax.ppermute(operand, "seq", [(i, i ^ bit) for i in range(size)])


def seq_pieces(own):
    across = partner(own, 2)
    return [own, partner(own, 1), across, partner(across, 1)]


def seq_shares(keep, give):
    arrived = partner(give, 1)
    sent = (keep[1].astype(F32) + arrived[1].astype(F32)).astype(BF16)
    return (keep, arrived, partner(sent, 2)), sent


def total(shares):
    keep, arrived, across = shares
    return keep[0].astype(F32) + arrived[0].astype(F32) + across.astype(F32)


def everywhere_order(sources):
    seq = lax.axis_index("seq")
    return jnp.stack([s * 4 + (seq ^ bit) for s in sources for bit in range(4)]).astype(jnp.int32)


VMEM_LIMIT = 56 * 2**20
SMEM = pl.BlockSpec(memory_space=pltpu.SMEM)
VMEM = pl.BlockSpec(memory_space=pltpu.VMEM)


def call(kernel, name, flops=0, **options):
    return pl.pallas_call(
        kernel,
        compiler_params=pltpu.CompilerParams(vmem_limit_bytes=VMEM_LIMIT),
        cost_estimate=pl.CostEstimate(flops=int(flops), bytes_accessed=0, transcendentals=0),
        name=name,
        **options,
    )


def shape(dims, dtype):
    return jax.ShapeDtypeStruct(dims, dtype)


def fixed(*dims):
    return pl.BlockSpec(dims, lambda *_: (0,) * len(dims))


def columns_kernel(n_dp, gate_ref, up_ref, *out_refs):
    size = gate_ref.shape[1] // (4 * n_dp)
    for half, out in enumerate(out_refs):
        for m, ref in enumerate((gate_ref, up_ref)):
            for q in range(n_dp // 2):
                place = (m * (n_dp // 2) + q) * size
                for j in range(4):
                    start = ((half * (n_dp // 2) + q) * 4 + j) * size
                    out[j, :, place : place + size] = ref[:, start : start + size]


def columns_for_seq(gate, up, n_dp):
    rows, total = gate.shape
    return call(
        functools.partial(columns_kernel, n_dp),
        "columns",
        in_specs=[VMEM] * 2,
        out_shape=[shape((4, rows, total // 4), BF16)] * 2,
    )(gate, up)


ANY = pl.BlockSpec(memory_space=pl.ANY)


def place_kernel(count, sources_ref, *refs):
    pieces, outs, sems = refs[: -count - 1], refs[-count - 1 : -1], refs[-1]
    copies = []
    for i, piece in enumerate(pieces):
        rows = piece.shape[0] // count
        start = pl.multiple_of(sources_ref[i] * rows, rows)
        for j, out in enumerate(outs):
            part = piece.at[pl.ds(j * rows, rows)]
            copies.append(pltpu.make_async_copy(part, out.at[pl.ds(start, rows)], sems.at[i, j]))
    for copy in copies:
        copy.start()
    for copy in copies:
        copy.wait()


def finish_kernel(count, source_ref, *refs):
    (top_ref, bottom_ref), outs, sems = refs[count : count + 2], refs[count + 2 : -1], refs[-1]
    copies = []
    if count == 2:
        rows = top_ref.shape[0]
        start = pl.multiple_of(source_ref[0] * rows, rows)
        for i, piece in enumerate((top_ref, bottom_ref)):
            copies.append(pltpu.make_async_copy(piece, outs[i].at[pl.ds(start, rows)], sems.at[i]))
    else:
        rows = top_ref.shape[0]
        for i, piece in enumerate((top_ref, bottom_ref)):
            start = pl.multiple_of(source_ref[0] * (2 * rows), 2 * rows) + i * rows
            copies.append(pltpu.make_async_copy(piece, outs[0].at[pl.ds(start, rows)], sems.at[i]))
    for copy in copies:
        copy.start()
    for copy in copies:
        copy.wait()


def place(pieces, sources, count):
    rows, columns = pieces[0].shape
    most = len(pieces)
    return call(
        functools.partial(place_kernel, count),
        "place",
        in_specs=[SMEM] + [VMEM] * most,
        out_specs=[ANY] * count,
        out_shape=[shape(((most + 1) * rows // count, columns), BF16)] * count,
        scratch_shapes=[pltpu.SemaphoreType.DMA((most, count))],
    )(jnp.stack(sources[:-1]), *pieces)


def finish(begun, pieces, sources):
    count = len(begun)
    return call(
        functools.partial(finish_kernel, count),
        "finish",
        in_specs=[SMEM] + [ANY] * count + [VMEM] * 2,
        out_specs=[ANY] * count,
        out_shape=[shape(m.shape, BF16) for m in begun],
        scratch_shapes=[pltpu.SemaphoreType.DMA((2,))],
        input_output_aliases={i + 1: i for i in range(count)},
    )(sources[-1][None], *begun, *pieces[-1])


def gather_rows(order_ref, source_ref, target_ref, rows):
    total = source_ref.shape[0]
    wide = min(256, total)
    each = wide // rows
    for i in range(total // wide):
        blocks = []
        for j in range(each):
            start = pl.multiple_of(order_ref[i * each + j] * rows, rows)
            blocks.append(source_ref[pl.ds(start, rows), :])
        target_ref[:, i * wide : (i + 1) * wide] = jnp.concatenate(blocks, axis=0).T


def qkv_kernel(order_ref, normed_ref, inner_ref, b_ref, *refs):
    pieces, (out_ref, left_ref) = refs[:-2], refs[-2:]

    @pl.when(pl.program_id(0) == 0)
    def _():
        gather_rows(order_ref, normed_ref, left_ref, pieces[0].shape[0])

    width = pieces[0].shape[1]
    step = 512
    for c in range(0, width, step):
        right = jnp.concatenate([p[:, c : c + step] for p in pieces], axis=0)
        sums = contract(left_ref[...], right, 1, 0)
        sums = sums + contract(inner_ref[...], b_ref[:, c : c + step], 1, 0)
        out_ref[c : c + step, :] = sums.T


def project_in(order, normed_t, inner, b_in, pieces):
    width, tokens = normed_t.shape
    total = b_in.shape[1]
    step = 1024
    rows = pieces[0].shape[0]
    return call(
        qkv_kernel,
        "project_in",
        grid=(total // step,),
        in_specs=[
            SMEM,
            fixed(width, tokens),
            fixed(*inner.shape),
            pl.BlockSpec((b_in.shape[0], step), lambda c: (0, c)),
        ]
        + [pl.BlockSpec((rows, step), lambda c: (0, c))] * len(pieces),
        out_specs=pl.BlockSpec((step, tokens), lambda c: (c, 0)),
        out_shape=shape((total, tokens), F32),
        scratch_shapes=[pltpu.VMEM((tokens, width), BF16)],
    )(order, normed_t, inner, b_in, *pieces)


def out_kernel(order_ref, mixed_ref, inner_ref, b_ref, tokens_ref, valid_ref, gain_ref, *refs):
    pieces, (hidden_ref, normed_ref, left_ref) = refs[:-3], refs[-3:]
    c = pl.program_id(0)

    @pl.when(c == 0)
    def _():
        gather_rows(order_ref, mixed_ref, left_ref, pieces[0].shape[0])

    width = pieces[0].shape[1]
    right = jnp.concatenate([p[...] for p in pieces], axis=0)
    sums = contract(left_ref[...], right, 1, 0) + contract(inner_ref[...], b_ref[...], 0, 0)
    sums = tokens_ref[...].astype(F32) + valid_ref[...] * sums
    hidden_ref[:, pl.ds(pl.multiple_of(c * width, width), width)] = sums

    @pl.when(c == pl.num_programs(0) - 1)
    def _():
        hidden = hidden_ref[...]
        normed_ref[...] = rms_scale(hidden, gain_ref[...]).astype(BF16)


def project_out(order, mixed, inner, bo, tokens, valid, gain, pieces):
    features, block = mixed.shape
    width = tokens.shape[1]
    step = 1024
    rows = pieces[0].shape[0]
    skip = (pieces[0].shape[1] - width) // step
    return call(
        out_kernel,
        "project_out",
        grid=(width // step,),
        in_specs=[
            SMEM,
            fixed(features, block),
            fixed(*inner.shape),
            pl.BlockSpec((RANK, step), lambda c: (0, c)),
            pl.BlockSpec((block, step), lambda c: (0, c)),
            fixed(block, 1),
            fixed(1, width),
        ]
        + [pl.BlockSpec((rows, step), lambda c: (0, c + skip))] * len(pieces),
        out_specs=[fixed(block, width), fixed(block, width)],
        out_shape=[shape((block, width), F32), shape((block, width), BF16)],
        scratch_shapes=[pltpu.VMEM((block, features), BF16)],
    )(order, mixed, inner, bo, tokens, valid, gain, *pieces)


def scatter_products(order_ref, pieces, right, sums_ref, form):
    rows = pieces[0].shape[0]
    each = max(1, 256 // rows)
    for i in range(0, len(pieces), each):
        left = jnp.concatenate([p[...] for p in pieces[i : i + each]], axis=0)
        product = contract(left, right, 1, form)
        for j in range(each):
            start = pl.multiple_of(order_ref[i + j] * rows, rows)
            sums_ref[pl.ds(start, rows), :] += product[j * rows : (j + 1) * rows]


def out_back_kernel(order_ref, grad_ref, a_ref, inner_ref, *refs):
    pieces, (out_ref, sums_ref) = refs[:-2], refs[-2:]
    c = pl.program_id(0)

    @pl.when(c == 0)
    def _():
        sums_ref[...] = contract(a_ref[...], inner_ref[...], 0, 1)

    scatter_products(order_ref, pieces, grad_ref[...], sums_ref, 1)

    @pl.when(c == pl.num_programs(0) - 1)
    def _():
        out_ref[...] = sums_ref[...].astype(BF16)


def project_out_back(order, grad, ao, d_inner, pieces):
    block, width = grad.shape
    features = ao.shape[1]
    step = 1024
    rows = pieces[0].shape[0]
    skip = (pieces[0].shape[1] - width) // step
    return call(
        out_back_kernel,
        "project_out_back",
        grid=(width // step,),
        in_specs=[
            SMEM,
            pl.BlockSpec((block, step), lambda c: (0, c)),
            fixed(*ao.shape),
            fixed(*d_inner.shape),
        ]
        + [pl.BlockSpec((rows, step), lambda c: (0, c + skip))] * len(pieces),
        out_specs=fixed(features, block),
        out_shape=shape((features, block), BF16),
        scratch_shapes=[pltpu.VMEM((features, block), F32)],
    )(order, grad, ao, d_inner, *pieces)


def in_back_kernel(order_ref, grad_ref, a_ref, inner_ref, tokens_ref, gain_ref, base_ref, *refs):
    pieces, (out_ref, sums_ref, turned_ref) = refs[:-3], refs[-3:]
    c = pl.program_id(0)

    @pl.when(c == 0)
    def _():
        sums_ref[...] = contract(a_ref[...], inner_ref[...], 0, 0)

    scatter_products(order_ref, pieces, grad_ref[...], sums_ref, 0)

    @pl.when(c == pl.num_programs(0) - 1)
    def _():
        size = sums_ref.shape[1]
        for i in range(0, sums_ref.shape[0], size):
            turned_ref[:, i : i + size] = sums_ref[i : i + size, :].T
        inputs = tokens_ref[...].astype(F32)
        grad = turned_ref[...] * gain_ref[...]
        scale = lax.rsqrt(jnp.mean(inputs * inputs, axis=-1, keepdims=True) + EPS)
        along = jnp.mean(inputs * grad, axis=-1, keepdims=True) * scale * scale
        out_ref[...] = (base_ref[...] + scale * (grad - inputs * along)).astype(BF16)


def project_in_back(order, d_linear, a_in, d_inner, tokens, gain, base, pieces):
    total, block = d_linear.shape
    width = tokens.shape[1]
    step = 1024
    rows = pieces[0].shape[0]
    return call(
        in_back_kernel,
        "project_in_back",
        grid=(total // step,),
        in_specs=[
            SMEM,
            pl.BlockSpec((step, block), lambda c: (c, 0)),
            fixed(*a_in.shape),
            fixed(*d_inner.shape),
            fixed(block, width),
            fixed(1, width),
            fixed(block, width),
        ]
        + [pl.BlockSpec((rows, step), lambda c: (0, c))] * len(pieces),
        out_specs=fixed(block, width),
        out_shape=shape((block, width), BF16),
        scratch_shapes=[pltpu.VMEM((width, block), F32), pltpu.VMEM((block, width), F32)],
    )(order, d_linear, a_in, d_inner, tokens, gain, base, *pieces)


def hidden_back_kernel(l0, l1, l2, r0, r1, r2, hidden_ref, cot_ref, valid_ref, gain_ref, b_ref, dh_ref, gu_ref, inner_ref):
    half = l2.shape[1]
    for i, refs in enumerate(((l0, l1, l2), (r0, r1, r2))):
        part = slice(i * half, (i + 1) * half)
        grad = refs[0][0].astype(F32) + refs[1][0].astype(F32) + refs[2][...].astype(F32)
        dh_ref[:, part] = grad * gain_ref[:, part]
    hidden, grad = hidden_ref[...], dh_ref[...]
    scale = lax.rsqrt(jnp.mean(hidden * hidden, axis=-1, keepdims=True) + EPS)
    along = jnp.mean(hidden * grad, axis=-1, keepdims=True) * scale * scale
    grad = cot_ref[...].astype(F32) + scale * (grad - hidden * along)
    dh_ref[...] = grad
    low = (valid_ref[...] * grad).astype(BF16)
    gu_ref[...] = low
    inner_ref[...] = contract(low, b_ref[...], 1, 1).astype(BF16)


def hidden_back(left, right, hidden, cot, valid, gain, bo):
    block, width = hidden.shape
    return call(
        hidden_back_kernel,
        "hidden_back",
        flops=7e9,
        out_shape=[shape((block, width), F32), shape((block, width), BF16), shape((block, RANK), BF16)],
    )(*left, *right, hidden, cot, valid, gain, bo)


def gather_tokens(refs, whole_ref):
    block = refs[0].shape[0]
    for i, ref in enumerate(refs):
        whole_ref[i * block : (i + 1) * block, :] = ref[...]


def lower_back_kernel(g0, g1, g2, g3, weight_ref, b_ref, a_ref, out_ref, inner_ref, whole_ref):
    @pl.when(pl.program_id(0) == 0)
    def _():
        gather_tokens((g0, g1, g2, g3), whole_ref)
        inner_ref[...] = contract(whole_ref[...], b_ref[...], 1, 1).astype(BF16)

    sums = contract(whole_ref[...], weight_ref[...], 1, 1)
    out_ref[...] = (sums + contract(inner_ref[...], a_ref[...], 1, 0)).astype(BF16)


def lower_back(grads, weight, bd, ad):
    block, width = grads[0].shape
    units = weight.shape[0]
    step = 256
    tokens = 4 * block
    return call(
        lower_back_kernel,
        "lower_back",
        grid=(units // step,),
        in_specs=[fixed(block, width)] * 4
        + [
            pl.BlockSpec((step, width), lambda j: (j, 0)),
            fixed(RANK, width),
            pl.BlockSpec((RANK, step), lambda j: (0, j)),
        ],
        out_specs=[pl.BlockSpec((tokens, step), lambda j: (0, j)), fixed(tokens, RANK)],
        out_shape=[shape((tokens, units), BF16), shape((tokens, RANK), BF16)],
        scratch_shapes=[pltpu.VMEM((tokens, width), BF16)],
    )(*grads, weight, bd, ad)


def tokens_kernel(n0, n1, n2, n3, a_ref, whole_ref, low_ref):
    gather_tokens((n0, n1, n2, n3), whole_ref)
    low_ref[...] = contract(whole_ref[...], a_ref[...], 1, 1).astype(BF16)


def all_tokens(normed, a_gu):
    block, width = normed[0].shape
    return call(
        tokens_kernel,
        "all_tokens",
        out_shape=[shape((4 * block, width), BF16), shape((4 * block, 2 * RANK), BF16)],
    )(*normed, a_gu)


def units_kernel(
    whole_ref,
    low_ref,
    gate_ref,
    up_ref,
    bg_ref,
    bu_ref,
    ad_ref,
    d_act_ref,
    act_ref,
    dg_ref,
    du_ref,
    inner_ref,
):
    @pl.when(pl.program_id(0) == 0)
    def _():
        inner_ref[...] = jnp.zeros(inner_ref.shape, F32)

    low_gate, low_up = low_ref[:, :RANK], low_ref[:, RANK:]
    gate = contract(whole_ref[...], gate_ref[...], 1, 0) + contract(low_gate, bg_ref[...], 1, 0)
    up = contract(whole_ref[...], up_ref[...], 1, 0) + contract(low_up, bu_ref[...], 1, 0)
    d_act = d_act_ref[...].astype(F32)
    sig = jax.nn.sigmoid(gate)
    silu = gate * sig
    act = (silu * up).astype(BF16)
    d_gate = (d_act * up * (sig + silu * (1.0 - sig))).astype(BF16)
    d_up = (d_act * silu).astype(BF16)
    act_ref[...] = act
    dg_ref[...] = d_gate
    du_ref[...] = d_up
    inner_ref[:, :RANK] += contract(d_gate, bg_ref[...], 1, 1)
    inner_ref[:, RANK : 2 * RANK] += contract(d_up, bu_ref[...], 1, 1)
    inner_ref[:, 2 * RANK :] += contract(act, ad_ref[...], 1, 1)


def units(part, whole, low, both, bg, bu, ad, d_act):
    tokens, width = whole.shape
    half = both.shape[1] // 2
    step = 256
    steps = half // step
    here = pl.BlockSpec((RANK, step), lambda j: (0, part * steps + j))
    tile = pl.BlockSpec((tokens, step), lambda j: (0, j))
    return call(
        units_kernel,
        "units",
        grid=(steps,),
        in_specs=[
            fixed(tokens, width),
            fixed(tokens, 2 * RANK),
            pl.BlockSpec((width, step), lambda j: (0, j)),
            pl.BlockSpec((width, step), lambda j: (0, steps + j)),
            here,
            here,
            here,
            pl.BlockSpec((tokens, step), lambda j: (0, part * steps + j)),
        ],
        out_specs=[tile] * 3 + [fixed(tokens, 3 * RANK)],
        out_shape=[shape((tokens, half), BF16)] * 3 + [shape((tokens, 3 * RANK), F32)],
    )(whole, low, both, both, bg, bu, ad, d_act)


def units_grads_kernel(low_ref, d_down_ref, act_ref, dg_ref, du_ref, gbg_ref, gbu_ref, gad_ref):
    gbg_ref[...] = contract(low_ref[:, :RANK], dg_ref[...], 0, 0)
    gbu_ref[...] = contract(low_ref[:, RANK:], du_ref[...], 0, 0)
    gad_ref[...] = contract(d_down_ref[...], act_ref[...], 0, 0)


def units_grads(low, d_down, act, d_gate, d_up):
    tokens, half = act.shape
    step = 256
    tile = pl.BlockSpec((tokens, step), lambda j: (0, j))
    thin = pl.BlockSpec((RANK, step), lambda j: (0, j))
    return call(
        units_grads_kernel,
        "units_grads",
        grid=(half // step,),
        in_specs=[fixed(tokens, 2 * RANK), fixed(tokens, RANK), tile, tile, tile],
        out_specs=[thin] * 3,
        out_shape=[shape((RANK, half), F32)] * 3,
    )(low, d_down, act, d_gate, d_up)


def units_back_first_kernel(g_ref, u_ref, w_ref, out_ref):
    half = g_ref.shape[1]
    sums = contract(g_ref[...], w_ref[:, :half], 1, 1) + contract(u_ref[...], w_ref[:, half:], 1, 1)
    out_ref[...] = sums.astype(BF16)


def units_back_first(d_gate, d_up, both):
    tokens, half = d_gate.shape
    width = both.shape[0]
    step = 256
    return call(
        units_back_first_kernel,
        "units_back_first",
        grid=(width // step,),
        in_specs=[fixed(tokens, half)] * 2 + [pl.BlockSpec((step, 2 * half), lambda n: (n, 0))],
        out_specs=pl.BlockSpec((tokens, step), lambda n: (0, n)),
        out_shape=shape((tokens, width), BF16),
    )(d_gate, d_up, both)


def units_back_kernel(first_ref, g_ref, u_ref, w_ref, ia_ref, ib_ref, a_ref, keep_ref, give_ref):
    half = g_ref.shape[1]
    low = (ia_ref[...] + ib_ref[...]).astype(BF16)[:, : 2 * RANK]
    sums = first_ref[...].astype(F32) + contract(low, a_ref[...], 1, 0)
    sums = sums + contract(g_ref[...], w_ref[:, :half], 1, 1)
    sums = sums + contract(u_ref[...], w_ref[:, half:], 1, 1)
    sums = sums.astype(BF16)
    block = keep_ref.shape[1]
    keep_ref[0] = sums[:block]
    give_ref[0] = sums[block : 2 * block]
    keep_ref[1] = sums[2 * block : 3 * block]
    give_ref[1] = sums[3 * block :]


def units_back(part, parts, first, d_gate, d_up, both, inners, a_gu):
    tokens, half = d_gate.shape
    width = both.shape[0]
    step = 256
    steps = width // parts // step
    place = lambda n: part * steps + n
    out = pl.BlockSpec((2, tokens // 4, step), lambda n: (0, 0, n))
    return call(
        units_back_kernel,
        "units_back",
        grid=(steps,),
        in_specs=[
            pl.BlockSpec((tokens, step), lambda n: (0, place(n))),
            fixed(tokens, half),
            fixed(tokens, half),
            pl.BlockSpec((step, 2 * half), lambda n: (place(n), 0)),
            fixed(tokens, 3 * RANK),
            fixed(tokens, 3 * RANK),
            pl.BlockSpec((2 * RANK, step), lambda n: (0, place(n))),
        ],
        out_specs=[out, out],
        out_shape=[shape((2, tokens // 4, width // parts), BF16)] * 2,
    )(first, d_gate, d_up, both, *inners, a_gu)


def lower_kernel(
    aa_ref, ab_ref, weight_ref, ia_ref, ib_ref, b_ref, whole_ref, g0, g1, g2, g3, keep_ref, give_ref, grad_ref, grad_gu_ref
):
    inner = (ia_ref[...] + ib_ref[...]).astype(BF16)
    low = inner[:, 2 * RANK :]
    half = aa_ref.shape[1]
    sums = contract(low, b_ref[...], 1, 0)
    sums = sums + contract(aa_ref[...], weight_ref[:half], 1, 0)
    sums = sums + contract(ab_ref[...], weight_ref[half:], 1, 0)
    sums = sums.astype(BF16)
    block = g0.shape[0]
    grad = jnp.zeros(grad_ref.shape, F32)
    for i, g in enumerate((g0, g1, g2, g3)):
        out = give_ref if i % 2 else keep_ref
        out[i // 2] = sums[i * block : (i + 1) * block]
        grad = grad + contract(low[i * block : (i + 1) * block], g[...], 0, 0)
    grad_ref[...] = grad
    grad_gu_ref[...] = contract(inner[:, : 2 * RANK], whole_ref[...], 0, 0)


def lower(act_a, act_b, weight, inners, bd, grads, whole):
    block, width = grads[0].shape
    tokens, half = act_a.shape
    step = 256
    tile = pl.BlockSpec((block, step), lambda n: (0, n))
    thin = pl.BlockSpec((RANK, step), lambda n: (0, n))
    out = pl.BlockSpec((2, block, step), lambda n: (0, 0, n))
    return call(
        lower_kernel,
        "lower",
        grid=(width // step,),
        in_specs=[
            fixed(tokens, half),
            fixed(tokens, half),
            pl.BlockSpec((2 * half, step), lambda n: (0, n)),
            fixed(tokens, 3 * RANK),
            fixed(tokens, 3 * RANK),
            thin,
            pl.BlockSpec((tokens, step), lambda n: (0, n)),
        ]
        + [tile] * 4,
        out_specs=[out, out, thin, pl.BlockSpec((2 * RANK, step), lambda n: (0, n))],
        out_shape=[shape((2, block, width), BF16)] * 2
        + [shape((RANK, width), F32), shape((2 * RANK, width), F32)],
    )(act_a, act_b, weight, *inners, bd, whole, *grads)


def wide_heads(ref):
    return jnp.concatenate([ref[h * HD : (h + 1) * HD] for h in range(GROUP)], axis=1)


def attend_kernel(seq_ref, limit_ref, q_ref, kv0, kv1, kv2, kv3, o_ref, e_ref, r_ref):
    queries = wide_heads(q_ref)
    limit = limit_ref[...]
    total = jnp.zeros(limit.shape, F32)
    mixed = jnp.zeros(queries.shape, F32)
    for bit, ref in enumerate((kv0, kv1, kv2, kv3)):
        block = ref.shape[2]
        scores = contract(ref[0, :HD], queries, 0, 0)
        places = (seq_ref[0] ^ bit) * block + lax.broadcasted_iota(jnp.int32, scores.shape, 0)
        raised = jnp.where(places <= limit, jnp.exp(scores), 0.0)
        total = total + jnp.sum(raised, axis=0, keepdims=True)
        low = raised.astype(BF16)
        e_ref[0, bit] = low
        mixed = mixed + contract(ref[0, HD:], low, 1, 0)
    inverse = 1.0 / total
    r_ref[0] = inverse
    mixed = (mixed * inverse).astype(BF16)
    width = q_ref.shape[1]
    for h in range(GROUP):
        o_ref[h * HD : (h + 1) * HD] = mixed[:, h * width : (h + 1) * width]


def attend(seq, limit, queries, keys_values):
    block = keys_values[0].shape[2]
    width = queries.shape[1]
    wide = GROUP * width
    head_rows = pl.BlockSpec((GROUP * HD, width), lambda g: (g, 0))
    return call(
        attend_kernel,
        "attend",
        grid=(KV,),
        in_specs=[SMEM, fixed(1, wide), head_rows]
        + [pl.BlockSpec((1, 2 * HD, block), lambda g: (g, 0, 0))] * 4,
        out_specs=[
            head_rows,
            pl.BlockSpec((1, 4, block, wide), lambda g: (g, 0, 0, 0)),
            pl.BlockSpec((1, 1, wide), lambda g: (g, 0, 0)),
        ],
        out_shape=[
            shape(queries.shape, BF16),
            shape((KV, 4, block, wide), BF16),
            shape((KV, 1, wide), F32),
        ],
    )(seq[None], limit, queries, *keys_values)


def attend_back_kernel(q_ref, kv0, kv1, kv2, kv3, e_ref, r_ref, o_ref, do_ref, dq_ref, keep_ref, give_ref):
    width = q_ref.shape[1]
    queries = wide_heads(q_ref)
    grads = wide_heads(do_ref).astype(F32) * r_ref[0]
    dots = jnp.sum(grads * wide_heads(o_ref).astype(F32), axis=0, keepdims=True)
    grads = grads.astype(BF16)
    d_queries = jnp.zeros(queries.shape, F32)
    for bit, ref in enumerate((kv0, kv1, kv2, kv3)):
        out = give_ref if bit % 2 else keep_ref
        raised = e_ref[0, bit]
        d_probs = contract(ref[0, HD:], grads, 0, 0)
        d_scores = (raised.astype(F32) * (d_probs - dots)).astype(BF16)
        d_queries = d_queries + contract(ref[0, :HD], d_scores, 1, 0)
        out[bit // 2, 0, :HD] = contract(queries, d_scores, 1, 1).astype(BF16)
        out[bit // 2, 0, HD:] = contract(grads, raised, 1, 1).astype(BF16)
    for h in range(GROUP):
        dq_ref[h * HD : (h + 1) * HD] = d_queries[:, h * width : (h + 1) * width]


def attend_back(first, count, queries, keys_values, raised, inverse, mixed, d_mixed):
    block = keys_values[0].shape[2]
    width = queries.shape[1]
    wide = GROUP * width
    head_rows = pl.BlockSpec((GROUP * HD, width), lambda g: (first + g, 0))
    shares = pl.BlockSpec((2, 1, 2 * HD, block), lambda g: (0, g, 0, 0))
    return call(
        attend_back_kernel,
        "attend_back",
        grid=(count,),
        in_specs=[head_rows]
        + [pl.BlockSpec((1, 2 * HD, block), lambda g: (first + g, 0, 0))] * 4
        + [
            pl.BlockSpec((1, 4, block, wide), lambda g: (first + g, 0, 0, 0)),
            pl.BlockSpec((1, 1, wide), lambda g: (first + g, 0, 0)),
            head_rows,
            head_rows,
        ],
        out_specs=[pl.BlockSpec((GROUP * HD, width), lambda g: (g, 0)), shares, shares],
        out_shape=[
            shape((count * GROUP * HD, width), F32),
            shape((2, count, 2 * HD, block), BF16),
            shape((2, count, 2 * HD, block), BF16),
        ],
    )(queries, *keys_values, raised, inverse, mixed, d_mixed)


def pick_kernel(ids_ref, *refs):
    out_ref = refs[-1]
    for d in range(out_ref.shape[0]):
        parts = [ref[ids_ref[d]] for ref in refs[:-1]]
        out_ref[d] = jnp.concatenate(parts, axis=1)


def pick(ids, stacks):
    columns = sum(stack.shape[2] for stack in stacks)
    n_dp = ids.shape[0]
    return call(
        pick_kernel,
        "pick",
        in_specs=[SMEM] + [VMEM] * len(stacks),
        out_shape=shape((n_dp, RANK, columns), BF16),
    )(ids, *stacks)


def spread_kernel(widths, seq_ref, mine_ref, p1, p2, p3, *refs):
    (in_ref, grow_ref, ao_ref, bo_ref, gu_ref, bd_ref, bg_ref, bu_ref, ad_ref, all_ref) = refs
    local, each, thin = widths
    n_dp = mine_ref.shape[0]
    seq = seq_ref[0]
    base = 3 * local
    all_ref[seq] = mine_ref[:, :, base:]
    for bit, ref in ((1, p1), (2, p2), (3, p3)):
        all_ref[seq ^ bit] = ref[...]

    def factor(start, width):
        parts = [all_ref[j, d, :, start : start + width] for d in range(n_dp) for j in range(4)]
        return jnp.concatenate(parts, axis=1)

    wide = lambda m: factor(m * each, each)
    for i in range(3):
        in_ref[i * RANK : (i + 1) * RANK] = wide(i)
    grow_ref[...] = jnp.zeros(grow_ref.shape, BF16)
    n_query, n_key = 4 * n_dp * each, 4 * n_dp * thin
    grow_ref[:RANK, :n_query] = wide(3)
    for i in range(2):
        start = n_query + i * n_key
        grow_ref[(i + 1) * RANK : (i + 2) * RANK, start : start + n_key] = factor(9 * each + i * thin, thin)
    ao_ref[...] = wide(4)
    bo_ref[...] = wide(5)
    gu_ref[:RANK] = wide(6)
    gu_ref[RANK:] = wide(7)
    bd_ref[...] = wide(8)
    for i, ref in enumerate((bg_ref, bu_ref, ad_ref)):
        for d in range(n_dp):
            ref[:, d * local : (d + 1) * local] = mine_ref[d, :, i * local : (i + 1) * local]


def spread(seq, mine, others, widths):
    local, each, thin = widths
    n_dp = mine.shape[0]
    total = 4 * n_dp * each
    grown = total + 8 * n_dp * thin
    rows = [(3 * RANK, total), (3 * RANK, grown), (RANK, total), (RANK, total), (2 * RANK, total), (RANK, total)]
    rows += [(RANK, n_dp * local)] * 3
    return call(
        functools.partial(spread_kernel, widths),
        "spread",
        in_specs=[SMEM] + [VMEM] * 4,
        out_shape=[shape(dims, BF16) for dims in rows],
        scratch_shapes=[pltpu.VMEM((4,) + others[0].shape, BF16)],
    )(seq[None], mine, *others)


def pack_kernel(n_dp, count, seq_ref, *refs):
    ins, refs = refs[:count], refs[count:]
    alone, (keep_ref, give_ref, alone_ref, all_ref) = refs[:-4], refs[-4:]
    for d in range(n_dp):
        for j in range(4):
            parts = []
            for ref in ins:
                each = ref.shape[1] // (4 * n_dp)
                at = (d * 4 + j) * each
                parts.append(ref[:, at : at + each])
            all_ref[j, d] = jnp.concatenate(parts, axis=1).astype(BF16)
    seq = seq_ref[0]
    for bit in range(4):
        out = give_ref if bit % 2 else keep_ref
        out[bit // 2] = all_ref[seq ^ bit]
    for i in range(0, len(alone), 2):
        for half in range(2):
            size = alone[i].shape[1] // (n_dp // 2)
            for d in range(n_dp // 2):
                place = slice((i // 2) * size, (i // 2 + 1) * size)
                part = alone[i + half][:, d * size : (d + 1) * size]
                alone_ref[half * (n_dp // 2) + d, :, place] = part.astype(BF16)


def pack(seq, grads, n_dp, alone):
    columns = sum(g.shape[1] for g in grads) // (4 * n_dp)
    dims = (n_dp, RANK, columns)
    outs = [shape((2,) + dims, BF16)] * 2
    outs.append(shape((n_dp, RANK, sum(g.shape[1] for g in alone) // n_dp), BF16))
    return call(
        functools.partial(pack_kernel, n_dp, len(grads)),
        "pack",
        in_specs=[SMEM] + [VMEM] * (len(grads) + len(alone)),
        out_shape=outs,
        scratch_shapes=[pltpu.VMEM((4,) + dims, BF16)],
    )(seq[None], *grads, *alone)


def sort_kernel(widths, ids_ref, came_ref, *out_refs):
    came = [came_ref[d].astype(F32) for d in range(came_ref.shape[0])]
    for a in range(ADAPT):
        total = jnp.zeros(came[0].shape, F32)
        for d, value in enumerate(came):
            total = total + jnp.where(ids_ref[d] == a, value, 0.0)
        at = 0
        for ref, width in zip(out_refs, widths):
            part = total[:, at : at + width]
            ref[a] = part.T if width < 64 else part
            at += width


def sort(ids, came, widths):
    outs = call(
        functools.partial(sort_kernel, widths),
        "sort",
        in_specs=[SMEM, VMEM],
        out_shape=[shape((ADAPT, w, RANK) if w < 64 else (ADAPT, RANK, w), F32) for w in widths],
    )(ids, came)
    return [o if w < 64 else o.transpose(0, 2, 1) for o, w in zip(outs, widths)]


def shards(
    tokens,
    cotangent,
    lengths,
    adapter_ids,
    attn_gain,
    query_gain,
    key_gain,
    ffn_gain,
    w_query,
    w_key,
    w_value,
    w_out,
    gate_weight,
    w_up,
    w_down,
    a_query,
    b_query,
    a_key,
    b_key,
    a_value,
    b_value,
    a_out,
    b_out,
    a_gate,
    b_gate,
    a_up,
    b_up,
    a_down,
    b_down,
):
    n_dp = lax.axis_size("dp")
    seq = lax.axis_index("seq")
    _, block, width = tokens.shape
    length = lengths[0]
    positions = seq * block + jnp.arange(block)
    valid = (positions < length).astype(F32)[:, None]
    sources = ring_sources()
    clock = Clock()
    n_query, n_key = H * HD, KV * HD
    local, each, thin = b_gate.shape[1], a_query.shape[1], b_key.shape[1]
    widths = (local, each, thin)

    attn = Ring(jnp.concatenate([w_query, w_key, w_value, w_out], axis=1))
    first_came, age = None, 0
    queue = [attn.pieces[0]]
    sides, acrosses, corners, going = [], [], [], []
    arrived = slot = 0
    last = attn.steps - 1
    while len(corners) < n_dp + 1:
        waits, new = [], []
        if not attn.complete():
            new = attn.step(clock)
            waits += new
            if attn.complete():
                ended = new
                new = [new]
        elif first_came is not None:
            age += 1
            if age == 3 and len(first_ring.pieces) == 3:
                waits += first_came
                first_came = None
        elif not first_ring.complete():
            first_came, age = first_ring.step(lambda v: after(v, ended) if len(first_ring.pieces) == 1 else clock(v)), 0
        while len(acrosses) < len(queue) and len(going) < 2:
            acrosses.append(partner(clock(queue[len(acrosses)]), 2))
            going.append(len(acrosses))
        for _ in range(3):
            if len(corners) < arrived:
                corners.append(partner(clock(acrosses[len(corners)]), 1))
                waits.append(corners[-1])
            elif len(sides) < len(queue):
                sides.append(partner(clock(queue[len(sides)]), 1))
                waits.append(sides[-1])
        if slot == 0:
            slots_a, slots_b = columns_for_seq(gate_weight, w_up, n_dp)
            ids = lax.all_to_all(
                jnp.broadcast_to(adapter_ids[None], (n_dp, 128)), "dp", 0, 0, tiled=True
            )[:, 0]
            stacks = (b_gate, b_up, a_down, a_query, a_key, a_value, b_query, a_out, b_out)
            stacks += (a_gate, a_up, b_down, b_key, b_value)
            sent = pick(ids, [m.transpose(0, 2, 1) for m in stacks])
            waits += [sent, slots_a]
        if slot == 1:
            swapped_a = lax.all_to_all(clock(slots_a), "seq", 0, 0, tiled=True)
        if slot == 2:
            mine = lax.all_to_all(clock(sent), "dp", 0, 0, tiled=True)
            first_ring = Ring(jnp.concatenate([w_down, swapped_a.reshape(-1, width)], axis=0))
            waits.append(first_ring.pieces[0])
        if slot == last + 2:
            inputs = clock(tokens)[0].astype(F32)
            normed = rms_scale(inputs, attn_gain).astype(BF16)
            normed_t = normed.T
            cot = cotangent[0].astype(F32)
            grad_out = (valid * clock(cot)).astype(BF16)
            waits += [normed_t, grad_out]
        if going and (slot == 0 or len(going) == 2 or len(queue) == n_dp + 1):
            waits.append(acrosses[going[0] - 1])
        else:
            going = going[:0] + going
        clock.tick(*waits)
        if going and any(w is acrosses[going[0] - 1] for w in waits):
            arrived = going.pop(0)
        if slot == 2:
            queue.append(clock(mine)[..., 3 * local :])
        queue += [jnp.concatenate(p, axis=0) if isinstance(p, tuple) else p for p in new]
        slot += 1
    others = [sides.pop(5), acrosses.pop(5), corners.pop(5)]
    queue.pop(5)
    attn_pieces = []
    for group in zip(queue, sides, acrosses, corners):
        attn_pieces += group
    order = everywhere_order(sources)

    belt = Conveyor(clock, [lambda: swapped_b.reshape(-1, width)])
    if first_came is None and not first_ring.complete():
        first_came = first_ring.step(clock)
    if first_came is not None:
        belt.going.append((first_came, first_ring))
    a_in, b_in, ao, bo, a_gu, bd, bg, bu, ad = spread(seq, mine, clock(others), widths)
    inner = contract(normed, a_in, 1, 1).astype(BF16)

    linear = project_in(order, normed_t, inner, b_in, attn_pieces)
    query_lin = linear[:n_query].reshape(H, HD, block)
    key_lin = linear[n_query : n_query + n_key].reshape(KV, HD, block)
    value_lin = linear[n_query + n_key :].reshape(KV, HD, block)
    cosine, sine = rotary_tables(positions)
    scale = HD**-0.5
    query_prep = lambda v: prepare(v, query_gain, cosine, sine)
    key_prep = lambda v: prepare(v, key_gain, cosine, sine)
    keys_values = jnp.concatenate([key_prep(key_lin), value_lin], axis=1).astype(BF16)
    grads = seq_pieces(clock(grad_out))
    keys_values = seq_pieces(after(keys_values, grads[2]))
    queries = (query_prep(query_lin) * scale).astype(BF16).reshape(n_query, block)
    limit = jnp.minimum(positions, length - 1).astype(jnp.int32)
    limit = jnp.tile(limit, GROUP)[None, :]
    belt.advance(queries, keys_values[2])
    swapped_b = lax.all_to_all(after(slots_b, queries), "seq", 0, 0, tiled=True)
    mixed, raised, inverse = attend(seq, limit, queries, keys_values)
    belt.advance(mixed)

    inner_out = contract(ao, mixed, 1, 0).astype(BF16)
    hidden, normed_two = project_out(
        order, mixed, inner_out, bo, tokens[0], valid, ffn_gain[None], attn_pieces
    )

    n2 = seq_pieces(normed_two)
    while not first_ring.complete():
        belt.advance(normed_two)
    ring_b = belt.rings[0]
    begun = place(clock(first_ring.pieces[:-1]), sources, 2)
    belt.until(first_ring, begun)
    w_lower, both_a = finish(begun, first_ring.pieces, sources)
    d_act, d_down = lower_back(clock(grads), w_lower, bd, ad)
    belt.advance(d_act)
    n2, low_n2 = all_tokens(n2, a_gu)
    act_a, dg_a, du_a, inner_a = units(0, n2, low_n2, both_a, bg, bu, ad, d_act)
    belt.advance(act_a)
    first = units_back_first(clock(dg_a), du_a, both_a)
    gbg_a, gbu_a, gad_a = units_grads(low_n2, d_down, after(act_a, first), dg_a, du_a)
    while not ring_b.complete():
        belt.advance(gbg_a)
    begun = place(clock(ring_b.pieces[:-1]), sources, 1)
    belt.until(ring_b, begun)
    (both_b,) = finish(begun, ring_b.pieces, sources)
    act_b, dg_b, du_b, inner_b = units(1, n2, low_n2, both_b, bg, bu, ad, d_act)
    inners = (inner_a, inner_b)
    keep, give = units_back(0, 2, first, dg_b, du_b, both_b, inners, a_gu)
    left, sent = seq_shares(keep, give)
    keep, give = units_back(1, 2, after(first, sent), dg_b, du_b, both_b, inners, a_gu)
    right, sent = seq_shares(keep, give)

    keep, give, grad_bd, grad_a_gu = lower(
        act_a, after(act_b, sent), w_lower, inners, bd, grads, n2
    )

    d_hidden, grad_update, d_inner_out = hidden_back(
        after(left[:2], keep) + left[2:], after(right[:2], keep) + right[2:], hidden, cotangent[0], valid, ffn_gain[None], bo
    )
    lowered, sent = seq_shares(*after((keep, give), grad_update))
    d_mixed = project_out_back(order, after(grad_update, sent), ao, d_inner_out, attn_pieces)
    count = KV // 2
    back = lambda part, d_mixed: attend_back(
        part * count, count, queries, keys_values, raised, inverse, mixed, d_mixed
    )
    d_query, keep, give = back(0, d_mixed)
    gbg_b, gbu_b, gad_b = units_grads(low_n2, d_down, after(act_b, d_query), dg_b, du_b)
    give, gbg_b = after((give, gbg_b), lowered[2])
    first_kv, sent = seq_shares(keep, give)
    other_query, keep, give = back(1, after(d_mixed, sent))
    other_kv, sent = seq_shares(keep, give)

    first_kv = total(after(first_kv, other_query))
    d_query = after(jnp.concatenate([d_query, other_query], axis=0), first_kv)
    d_queries = d_query.reshape(H, HD, block) * scale
    d_kv = jnp.concatenate([first_kv, total(other_kv)], axis=0)
    d_query_lin = jax.vjp(query_prep, query_lin)[1](d_queries)[0]
    d_key_lin = jax.vjp(key_prep, key_lin)[1](d_kv[:, :HD])[0]
    d_linear = jnp.concatenate(
        [
            d_query_lin.reshape(n_query, block),
            d_key_lin.reshape(n_key, block),
            d_kv[:, HD:].reshape(n_key, block),
        ],
        axis=0,
    ).astype(BF16)
    output = (hidden + valid * total(after(lowered, d_linear))).astype(BF16)
    d_inner = contract(b_in, d_linear, 1, 0).astype(BF16)
    grad_tokens = project_in_back(
        order, d_linear, a_in, d_inner, tokens[0], attn_gain[None], d_hidden, attn_pieces
    )

    grad_ao = contract(d_inner_out, mixed, 0, 1)
    grad_bo = contract(inner_out, grad_update, 1, 0)
    grad_a_in = contract(d_inner, normed, 1, 0)
    grad_b_in = contract(inner, d_linear, 0, 1)
    q_end, k_end = n_query, n_query + n_key
    partial = [grad_ao, grad_bo, grad_a_gu[:RANK], grad_a_gu[RANK:], grad_bd]
    partial += [grad_a_in[i * RANK : (i + 1) * RANK] for i in range(3)]
    partial += [grad_b_in[:RANK, :q_end]]
    partial += [grad_b_in[RANK : 2 * RANK, q_end:k_end], grad_b_in[2 * RANK :, k_end:]]
    whole = (gbg_a, gbg_b, gbu_a, gbu_b, gad_a, gad_b)
    keep, give, whole = pack(seq, partial, n_dp, whole)
    (keep, arrived, across), _ = seq_shares(keep, give)
    summed = total((keep, arrived, across)).astype(BF16)
    summed = after(jnp.concatenate([summed, whole], axis=2), grad_tokens)
    sizes = [each] * 9 + [thin] * 2 + [local] * 3
    came = lax.all_to_all(summed, "dp", 0, 0, tiled=True)
    gao, gbo, gag, gau, gbd, gaq, gak, gav, gbq, gbk, gbv, gbg, gbu, gad = sort(ids, came, sizes)
    return (
        output[None],
        grad_tokens[None],
        gaq,
        gbq,
        gak,
        gbk,
        gav,
        gbv,
        gao,
        gbo,
        gag,
        gbg,
        gau,
        gbu,
        gad,
        gbd,
    )


def solution(mesh):
    tokens = P("dp", "seq", None)
    matrix = P(("dp", "seq"), None)
    stack = P(None, ("dp", "seq"), None)
    in_specs = (tokens, tokens, P("dp"), P("dp")) + (P(),) * 4 + (matrix,) * 7 + (stack,) * 14
    out_specs = (tokens, tokens) + (stack,) * 14
    return jax.shard_map(shards, mesh=mesh, in_specs=in_specs, out_specs=out_specs, check_vma=False)
```

```python
import functools

import jax
import jax.numpy as jnp
import numpy as np
from jax import lax
from jax.experimental import pallas as pl
from jax.experimental.pallas import tpu as pltpu
from jax.sharding import PartitionSpec as P

H = 32
KV = 8
HD = 64
GROUP = H // KV
ADAPT = 8
RANK = 16
EPS = 1e-05
F32 = jnp.float32
BF16 = jnp.bfloat16


def contract(left, right, left_dim, right_dim):
    return lax.dot_general(
        left, right, (((left_dim,), (right_dim,)), ((), ())), preferred_element_type=F32
    )


def rms_scale(operand, scaling, axis=-1):
    mean = jnp.mean(operand * operand, axis=axis, keepdims=True)
    return operand * lax.rsqrt(mean + EPS) * scaling


def rotary_tables(positions):
    frequency = jnp.power(1000000.0, -jnp.arange(HD // 2, dtype=F32) * 2.0 / HD)
    angles = frequency[:, None] * positions.astype(F32)[None, :]
    return jnp.cos(angles), jnp.sin(angles)


def prepare(linear, scaling, cosine, sine):
    normed = rms_scale(linear, scaling[:, None], axis=1)
    front, second = normed[:, : HD // 2], normed[:, HD // 2 :]
    return jnp.concatenate(
        [front * cosine - second * sine, second * cosine + front * sine], axis=1
    )


def after(value, *others):
    return lax.optimization_barrier((value, others))[0]


def ring_order(size):
    return list(range(0, size, 2)) + list(range(1, size, 2))[::-1]


def ring_pairs(size):
    order = ring_order(size)
    right = [(order[i], order[(i + 1) % size]) for i in range(size)]
    return right, [(b, a) for a, b in right]


def ring_offsets():
    offsets = [0]
    for step in range(1, (lax.axis_size("dp") - 1) // 2 + 1):
        offsets += [-step, step]
    return offsets + [lax.axis_size("dp") // 2]


class Ring:
    def __init__(self, own):
        self.pieces = [own]
        self.left = self.right = own
        self.steps = lax.axis_size("dp") // 2

    def complete(self):
        return len(self.pieces) == lax.axis_size("dp")

    def step(self, clock):
        size = lax.axis_size("dp")
        right, left = ring_pairs(size)
        if len(self.pieces) < size - 1:
            self.left = lax.ppermute(clock(self.left), "dp", right)
            self.right = lax.ppermute(clock(self.right), "dp", left)
            self.pieces += [self.left, self.right]
            return self.left, self.right
        half = self.left.shape[0] // 2
        last_left, last_right = clock((self.left, self.right))
        top = lax.ppermute(last_left[:half], "dp", right)
        bottom = lax.ppermute(last_right[half:], "dp", left)
        self.pieces.append((top, bottom))
        return top, bottom


def ring_sources():
    size = lax.axis_size("dp")
    here = lax.axis_index("dp")
    place = jnp.where(here % 2 == 0, here // 2, size - 1 - here // 2)
    sources = []
    for offset in ring_offsets():
        at = (place + offset + size) % size
        sources.append(jnp.where(at < size // 2, 2 * at, 2 * (size - 1 - at) + 1).astype(jnp.int32))
    return sources


class Clock:
    def __init__(self):
        self.done = ()

    def tick(self, *done):
        self.done = done

    def __call__(self, value):
        return after(value, self.done) if self.done else value


class Conveyor:
    def __init__(self, clock, waiting):
        self.clock = clock
        self.waiting = list(waiting)
        self.going = []
        self.rings = []

    def push(self):
        ring = Ring(self.waiting.pop(0)())
        self.going.append((ring.step(self.clock), ring))
        self.rings.append(ring)
        return ring

    def advance(self, *computed):
        if not self.going:
            self.clock.tick(self.clock.done, computed)
            return
        came, ring = self.going.pop(0)
        self.clock.tick(came, *computed)
        if not ring.complete():
            self.going.append((ring.step(self.clock), ring))
            if ring.complete() and self.waiting:
                self.push()

    def until(self, ring, *computed):
        self.clock.tick(self.clock.done, computed)
        while not ring.complete() or any(r is ring for _, r in self.going):
            self.advance(self.clock.done)


def partner(operand, bit):
    size = lax.axis_size("seq")
    return lax.ppermute(operand, "seq", [(i, i ^ bit) for i in range(size)])


def seq_pieces(own):
    across = partner(own, 2)
    return [own, partner(own, 1), across, partner(across, 1)]


def seq_shares(keep, give, wait=()):
    arrived = partner(give, 1)
    sent = (after(keep, wait)[1].astype(F32) + arrived[1].astype(F32)).astype(BF16)
    return (keep, arrived, partner(sent, 2)), sent


def total(shares):
    keep, arrived, across = shares
    return keep[0].astype(F32) + arrived[0].astype(F32) + across.astype(F32)


def everywhere_order(sources):
    seq = lax.axis_index("seq")
    return jnp.stack([s * 4 + (seq ^ bit) for s in sources for bit in range(4)]).astype(jnp.int32)


VMEM_LIMIT = 56 * 2**20
SMEM = pl.BlockSpec(memory_space=pltpu.SMEM)
VMEM = pl.BlockSpec(memory_space=pltpu.VMEM)


def call(kernel, name, flops=0, **options):
    return pl.pallas_call(
        kernel,
        compiler_params=pltpu.CompilerParams(vmem_limit_bytes=VMEM_LIMIT),
        cost_estimate=pl.CostEstimate(flops=int(flops), bytes_accessed=0, transcendentals=0),
        name=name,
        **options,
    )


def shape(dims, dtype):
    return jax.ShapeDtypeStruct(dims, dtype)


def fixed(*dims):
    return pl.BlockSpec(dims, lambda *_: (0,) * len(dims))


def columns_kernel(n_dp, gate_ref, up_ref, *out_refs):
    size = gate_ref.shape[1] // (4 * n_dp)
    for half, out in enumerate(out_refs):
        for m, ref in enumerate((gate_ref, up_ref)):
            for q in range(n_dp // 2):
                place = (m * (n_dp // 2) + q) * size
                for j in range(4):
                    start = ((half * (n_dp // 2) + q) * 4 + j) * size
                    out[j, :, place : place + size] = ref[:, start : start + size]


def columns_for_seq(gate, up, n_dp):
    rows, total = gate.shape
    return call(
        functools.partial(columns_kernel, n_dp),
        "columns",
        in_specs=[VMEM] * 2,
        out_shape=[shape((4, rows, total // 4), BF16)] * 2,
    )(gate, up)


ANY = pl.BlockSpec(memory_space=pl.ANY)


def place_kernel(count, sources_ref, *refs):
    pieces, outs, sems = refs[: -count - 1], refs[-count - 1 : -1], refs[-1]
    copies = []
    for i, piece in enumerate(pieces):
        rows = piece.shape[0] // count
        start = pl.multiple_of(sources_ref[i] * rows, rows)
        for j, out in enumerate(outs):
            part = piece.at[pl.ds(j * rows, rows)]
            copies.append(pltpu.make_async_copy(part, out.at[pl.ds(start, rows)], sems.at[i, j]))
    for copy in copies:
        copy.start()
    for copy in copies:
        copy.wait()


def finish_kernel(count, source_ref, *refs):
    (top_ref, bottom_ref), outs, sems = refs[count : count + 2], refs[count + 2 : -1], refs[-1]
    copies = []
    if count == 2:
        rows = top_ref.shape[0]
        start = pl.multiple_of(source_ref[0] * rows, rows)
        for i, piece in enumerate((top_ref, bottom_ref)):
            copies.append(pltpu.make_async_copy(piece, outs[i].at[pl.ds(start, rows)], sems.at[i]))
    else:
        rows = top_ref.shape[0]
        for i, piece in enumerate((top_ref, bottom_ref)):
            start = pl.multiple_of(source_ref[0] * (2 * rows), 2 * rows) + i * rows
            copies.append(pltpu.make_async_copy(piece, outs[0].at[pl.ds(start, rows)], sems.at[i]))
    for copy in copies:
        copy.start()
    for copy in copies:
        copy.wait()


def place(pieces, sources, count):
    rows, columns = pieces[0].shape
    most = len(pieces)
    return call(
        functools.partial(place_kernel, count),
        "place",
        in_specs=[SMEM] + [VMEM] * most,
        out_specs=[ANY] * count,
        out_shape=[shape(((most + 1) * rows // count, columns), BF16)] * count,
        scratch_shapes=[pltpu.SemaphoreType.DMA((most, count))],
    )(jnp.stack(sources[:-1]), *pieces)


def finish(begun, pieces, sources):
    count = len(begun)
    return call(
        functools.partial(finish_kernel, count),
        "finish",
        in_specs=[SMEM] + [ANY] * count + [VMEM] * 2,
        out_specs=[ANY] * count,
        out_shape=[shape(m.shape, BF16) for m in begun],
        scratch_shapes=[pltpu.SemaphoreType.DMA((2,))],
        input_output_aliases={i + 1: i for i in range(count)},
    )(sources[-1][None], *begun, *pieces[-1])


def gather_rows(order_ref, source_ref, target_ref, rows):
    total = source_ref.shape[0]
    wide = min(256, total)
    each = wide // rows
    for i in range(total // wide):
        blocks = []
        for j in range(each):
            start = pl.multiple_of(order_ref[i * each + j] * rows, rows)
            blocks.append(source_ref[pl.ds(start, rows), :])
        target_ref[:, i * wide : (i + 1) * wide] = jnp.concatenate(blocks, axis=0).T


def qkv_kernel(order_ref, normed_ref, inner_ref, b_ref, *refs):
    pieces, (out_ref, left_ref) = refs[:-2], refs[-2:]

    @pl.when(pl.program_id(0) == 0)
    def _():
        gather_rows(order_ref, normed_ref, left_ref, pieces[0].shape[0])

    width = pieces[0].shape[1]
    step = 512
    for c in range(0, width, step):
        right = jnp.concatenate([p[:, c : c + step] for p in pieces], axis=0)
        sums = contract(left_ref[...], right, 1, 0)
        sums = sums + contract(inner_ref[...], b_ref[:, c : c + step], 1, 0)
        out_ref[c : c + step, :] = sums.T


def project_in(order, normed_t, inner, b_in, pieces):
    width, tokens = normed_t.shape
    total = b_in.shape[1]
    step = 1024
    rows = pieces[0].shape[0]
    return call(
        qkv_kernel,
        "project_in",
        grid=(total // step,),
        in_specs=[
            SMEM,
            fixed(width, tokens),
            fixed(*inner.shape),
            pl.BlockSpec((b_in.shape[0], step), lambda c: (0, c)),
        ]
        + [pl.BlockSpec((rows, step), lambda c: (0, c))] * len(pieces),
        out_specs=pl.BlockSpec((step, tokens), lambda c: (c, 0)),
        out_shape=shape((total, tokens), F32),
        scratch_shapes=[pltpu.VMEM((tokens, width), BF16)],
    )(order, normed_t, inner, b_in, *pieces)


def out_kernel(order_ref, mixed_ref, inner_ref, b_ref, tokens_ref, valid_ref, gain_ref, *refs):
    pieces, (hidden_ref, normed_ref, left_ref) = refs[:-3], refs[-3:]
    c = pl.program_id(0)

    @pl.when(c == 0)
    def _():
        gather_rows(order_ref, mixed_ref, left_ref, pieces[0].shape[0])

    width = pieces[0].shape[1]
    right = jnp.concatenate([p[...] for p in pieces], axis=0)
    sums = contract(left_ref[...], right, 1, 0) + contract(inner_ref[...], b_ref[...], 0, 0)
    sums = tokens_ref[...].astype(F32) + valid_ref[...] * sums
    hidden_ref[:, pl.ds(pl.multiple_of(c * width, width), width)] = sums

    @pl.when(c == pl.num_programs(0) - 1)
    def _():
        hidden = hidden_ref[...]
        normed_ref[...] = rms_scale(hidden, gain_ref[...]).astype(BF16)


def project_out(order, mixed, inner, bo, tokens, valid, gain, pieces):
    features, block = mixed.shape
    width = tokens.shape[1]
    step = 1024
    rows = pieces[0].shape[0]
    skip = (pieces[0].shape[1] - width) // step
    return call(
        out_kernel,
        "project_out",
        grid=(width // step,),
        in_specs=[
            SMEM,
            fixed(features, block),
            fixed(*inner.shape),
            pl.BlockSpec((RANK, step), lambda c: (0, c)),
            pl.BlockSpec((block, step), lambda c: (0, c)),
            fixed(block, 1),
            fixed(1, width),
        ]
        + [pl.BlockSpec((rows, step), lambda c: (0, c + skip))] * len(pieces),
        out_specs=[fixed(block, width), fixed(block, width)],
        out_shape=[shape((block, width), F32), shape((block, width), BF16)],
        scratch_shapes=[pltpu.VMEM((block, features), BF16)],
    )(order, mixed, inner, bo, tokens, valid, gain, *pieces)


def scatter_products(order_ref, pieces, right, sums_ref, form):
    rows = pieces[0].shape[0]
    each = max(1, 256 // rows)
    for i in range(0, len(pieces), each):
        left = jnp.concatenate([p[...] for p in pieces[i : i + each]], axis=0)
        product = contract(left, right, 1, form)
        for j in range(each):
            start = pl.multiple_of(order_ref[i + j] * rows, rows)
            sums_ref[pl.ds(start, rows), :] += product[j * rows : (j + 1) * rows]


def out_back_kernel(order_ref, grad_ref, a_ref, inner_ref, *refs):
    pieces, (out_ref, sums_ref) = refs[:-2], refs[-2:]
    c = pl.program_id(0)

    @pl.when(c == 0)
    def _():
        sums_ref[...] = contract(a_ref[...], inner_ref[...], 0, 1)

    scatter_products(order_ref, pieces, grad_ref[...], sums_ref, 1)

    @pl.when(c == pl.num_programs(0) - 1)
    def _():
        out_ref[...] = sums_ref[...].astype(BF16)


def project_out_back(order, grad, ao, d_inner, pieces):
    block, width = grad.shape
    features = ao.shape[1]
    step = 1024
    rows = pieces[0].shape[0]
    skip = (pieces[0].shape[1] - width) // step
    return call(
        out_back_kernel,
        "project_out_back",
        grid=(width // step,),
        in_specs=[
            SMEM,
            pl.BlockSpec((block, step), lambda c: (0, c)),
            fixed(*ao.shape),
            fixed(*d_inner.shape),
        ]
        + [pl.BlockSpec((rows, step), lambda c: (0, c + skip))] * len(pieces),
        out_specs=fixed(features, block),
        out_shape=shape((features, block), BF16),
        scratch_shapes=[pltpu.VMEM((features, block), F32)],
    )(order, grad, ao, d_inner, *pieces)


def in_back_kernel(order_ref, grad_ref, a_ref, inner_ref, tokens_ref, gain_ref, base_ref, *refs):
    pieces, (out_ref, sums_ref, turned_ref) = refs[:-3], refs[-3:]
    c = pl.program_id(0)

    @pl.when(c == 0)
    def _():
        sums_ref[...] = contract(a_ref[...], inner_ref[...], 0, 0)

    scatter_products(order_ref, pieces, grad_ref[...], sums_ref, 0)

    @pl.when(c == pl.num_programs(0) - 1)
    def _():
        size = sums_ref.shape[1]
        for i in range(0, sums_ref.shape[0], size):
            turned_ref[:, i : i + size] = sums_ref[i : i + size, :].T
        inputs = tokens_ref[...].astype(F32)
        grad = turned_ref[...] * gain_ref[...]
        scale = lax.rsqrt(jnp.mean(inputs * inputs, axis=-1, keepdims=True) + EPS)
        along = jnp.mean(inputs * grad, axis=-1, keepdims=True) * scale * scale
        out_ref[...] = (base_ref[...] + scale * (grad - inputs * along)).astype(BF16)


def project_in_back(order, d_linear, a_in, d_inner, tokens, gain, base, pieces):
    total, block = d_linear.shape
    width = tokens.shape[1]
    step = 1024
    rows = pieces[0].shape[0]
    return call(
        in_back_kernel,
        "project_in_back",
        grid=(total // step,),
        in_specs=[
            SMEM,
            pl.BlockSpec((step, block), lambda c: (c, 0)),
            fixed(*a_in.shape),
            fixed(*d_inner.shape),
            fixed(block, width),
            fixed(1, width),
            fixed(block, width),
        ]
        + [pl.BlockSpec((rows, step), lambda c: (0, c))] * len(pieces),
        out_specs=fixed(block, width),
        out_shape=shape((block, width), BF16),
        scratch_shapes=[pltpu.VMEM((width, block), F32), pltpu.VMEM((block, width), F32)],
    )(order, d_linear, a_in, d_inner, tokens, gain, base, *pieces)


def hidden_back_kernel(l0, l1, l2, r0, r1, r2, hidden_ref, cot_ref, valid_ref, gain_ref, b_ref, dh_ref, gu_ref, inner_ref):
    half = l2.shape[1]
    for i, refs in enumerate(((l0, l1, l2), (r0, r1, r2))):
        part = slice(i * half, (i + 1) * half)
        grad = refs[0][0].astype(F32) + refs[1][0].astype(F32) + refs[2][...].astype(F32)
        dh_ref[:, part] = grad * gain_ref[:, part]
    hidden, grad = hidden_ref[...], dh_ref[...]
    scale = lax.rsqrt(jnp.mean(hidden * hidden, axis=-1, keepdims=True) + EPS)
    along = jnp.mean(hidden * grad, axis=-1, keepdims=True) * scale * scale
    grad = cot_ref[...].astype(F32) + scale * (grad - hidden * along)
    dh_ref[...] = grad
    low = (valid_ref[...] * grad).astype(BF16)
    gu_ref[...] = low
    inner_ref[...] = contract(low, b_ref[...], 1, 1).astype(BF16)


def hidden_back(left, right, hidden, cot, valid, gain, bo):
    block, width = hidden.shape
    rows = block // 4
    share = pl.BlockSpec((1, rows, width // 2), lambda i: (0, i, 0))
    across = pl.BlockSpec((rows, width // 2), lambda i: (i, 0))
    whole = pl.BlockSpec((rows, width), lambda i: (i, 0))
    return call(
        hidden_back_kernel,
        "hidden_back",
        flops=7e9,
        grid=(4,),
        in_specs=[share, share, across] * 2
        + [whole, whole, pl.BlockSpec((rows, 1), lambda i: (i, 0)), fixed(1, width), fixed(*bo.shape)],
        out_specs=[whole, whole, pl.BlockSpec((rows, RANK), lambda i: (i, 0))],
        out_shape=[shape((block, width), F32), shape((block, width), BF16), shape((block, RANK), BF16)],
    )(*left, *right, hidden, cot, valid, gain, bo)


def gather_tokens(refs, whole_ref):
    block = refs[0].shape[0]
    for i, ref in enumerate(refs):
        whole_ref[i * block : (i + 1) * block, :] = ref[...]


def lower_back_kernel(g0, g1, g2, g3, weight_ref, b_ref, a_ref, out_ref, inner_ref, whole_ref):
    @pl.when(pl.program_id(0) == 0)
    def _():
        gather_tokens((g0, g1, g2, g3), whole_ref)
        inner_ref[...] = contract(whole_ref[...], b_ref[...], 1, 1).astype(BF16)

    sums = contract(whole_ref[...], weight_ref[...], 1, 1)
    out_ref[...] = (sums + contract(inner_ref[...], a_ref[...], 1, 0)).astype(BF16)


def lower_back(grads, weight, bd, ad):
    block, width = grads[0].shape
    units = weight.shape[0]
    step = 256
    tokens = 4 * block
    return call(
        lower_back_kernel,
        "lower_back",
        grid=(units // step,),
        in_specs=[fixed(block, width)] * 4
        + [
            pl.BlockSpec((step, width), lambda j: (j, 0)),
            fixed(RANK, width),
            pl.BlockSpec((RANK, step), lambda j: (0, j)),
        ],
        out_specs=[pl.BlockSpec((tokens, step), lambda j: (0, j)), fixed(tokens, RANK)],
        out_shape=[shape((tokens, units), BF16), shape((tokens, RANK), BF16)],
        scratch_shapes=[pltpu.VMEM((tokens, width), BF16)],
    )(*grads, weight, bd, ad)


def tokens_kernel(n0, n1, n2, n3, a_ref, whole_ref, low_ref):
    gather_tokens((n0, n1, n2, n3), whole_ref)
    low_ref[...] = contract(whole_ref[...], a_ref[...], 1, 1).astype(BF16)


def all_tokens(normed, a_gu):
    block, width = normed[0].shape
    return call(
        tokens_kernel,
        "all_tokens",
        out_shape=[shape((4 * block, width), BF16), shape((4 * block, 2 * RANK), BF16)],
    )(*normed, a_gu)


def units_kernel(
    whole_ref,
    low_ref,
    gate_ref,
    up_ref,
    bg_ref,
    bu_ref,
    ad_ref,
    d_act_ref,
    act_ref,
    dg_ref,
    du_ref,
    inner_ref,
):
    @pl.when(pl.program_id(0) == 0)
    def _():
        inner_ref[...] = jnp.zeros(inner_ref.shape, F32)

    low_gate, low_up = low_ref[:, :RANK], low_ref[:, RANK:]
    gate = contract(whole_ref[...], gate_ref[...], 1, 0) + contract(low_gate, bg_ref[...], 1, 0)
    up = contract(whole_ref[...], up_ref[...], 1, 0) + contract(low_up, bu_ref[...], 1, 0)
    d_act = d_act_ref[...].astype(F32)
    sig = jax.nn.sigmoid(gate)
    silu = gate * sig
    act = (silu * up).astype(BF16)
    d_gate = (d_act * up * (sig + silu * (1.0 - sig))).astype(BF16)
    d_up = (d_act * silu).astype(BF16)
    act_ref[...] = act
    dg_ref[...] = d_gate
    du_ref[...] = d_up
    inner_ref[:, :RANK] += contract(d_gate, bg_ref[...], 1, 1)
    inner_ref[:, RANK : 2 * RANK] += contract(d_up, bu_ref[...], 1, 1)
    inner_ref[:, 2 * RANK :] += contract(act, ad_ref[...], 1, 1)


def units(part, whole, low, both, bg, bu, ad, d_act):
    tokens, width = whole.shape
    half = both.shape[1] // 2
    step = 256
    steps = half // step
    here = pl.BlockSpec((RANK, step), lambda j: (0, part * steps + j))
    tile = pl.BlockSpec((tokens, step), lambda j: (0, j))
    return call(
        units_kernel,
        "units",
        grid=(steps,),
        in_specs=[
            fixed(tokens, width),
            fixed(tokens, 2 * RANK),
            pl.BlockSpec((width, step), lambda j: (0, j)),
            pl.BlockSpec((width, step), lambda j: (0, steps + j)),
            here,
            here,
            here,
            pl.BlockSpec((tokens, step), lambda j: (0, part * steps + j)),
        ],
        out_specs=[tile] * 3 + [fixed(tokens, 3 * RANK)],
        out_shape=[shape((tokens, half), BF16)] * 3 + [shape((tokens, 3 * RANK), F32)],
    )(whole, low, both, both, bg, bu, ad, d_act)


def units_grads_kernel(low_ref, d_down_ref, act_ref, dg_ref, du_ref, gbg_ref, gbu_ref, gad_ref):
    gbg_ref[...] = contract(low_ref[:, :RANK], dg_ref[...], 0, 0)
    gbu_ref[...] = contract(low_ref[:, RANK:], du_ref[...], 0, 0)
    gad_ref[...] = contract(d_down_ref[...], act_ref[...], 0, 0)


def units_grads(low, d_down, act, d_gate, d_up):
    tokens, half = act.shape
    step = 256
    tile = pl.BlockSpec((tokens, step), lambda j: (0, j))
    thin = pl.BlockSpec((RANK, step), lambda j: (0, j))
    return call(
        units_grads_kernel,
        "units_grads",
        grid=(half // step,),
        in_specs=[fixed(tokens, 2 * RANK), fixed(tokens, RANK), tile, tile, tile],
        out_specs=[thin] * 3,
        out_shape=[shape((RANK, half), F32)] * 3,
    )(low, d_down, act, d_gate, d_up)


def units_back_first_kernel(g_ref, u_ref, w_ref, out_ref):
    half = g_ref.shape[1]
    sums = contract(g_ref[...], w_ref[:, :half], 1, 1) + contract(u_ref[...], w_ref[:, half:], 1, 1)
    out_ref[...] = sums.astype(BF16)


def units_back_first(d_gate, d_up, both):
    tokens, half = d_gate.shape
    width = both.shape[0]
    step = 256
    return call(
        units_back_first_kernel,
        "units_back_first",
        grid=(width // step,),
        in_specs=[fixed(tokens, half)] * 2 + [pl.BlockSpec((step, 2 * half), lambda n: (n, 0))],
        out_specs=pl.BlockSpec((tokens, step), lambda n: (0, n)),
        out_shape=shape((tokens, width), BF16),
    )(d_gate, d_up, both)


def units_back_kernel(first_ref, g_ref, u_ref, w_ref, ia_ref, ib_ref, a_ref, keep_ref, give_ref):
    half = g_ref.shape[1]
    low = (ia_ref[...] + ib_ref[...]).astype(BF16)[:, : 2 * RANK]
    sums = first_ref[...].astype(F32) + contract(low, a_ref[...], 1, 0)
    sums = sums + contract(g_ref[...], w_ref[:, :half], 1, 1)
    sums = sums + contract(u_ref[...], w_ref[:, half:], 1, 1)
    sums = sums.astype(BF16)
    block = keep_ref.shape[1]
    keep_ref[0] = sums[:block]
    give_ref[0] = sums[block : 2 * block]
    keep_ref[1] = sums[2 * block : 3 * block]
    give_ref[1] = sums[3 * block :]


def units_back(part, parts, first, d_gate, d_up, both, inners, a_gu):
    tokens, half = d_gate.shape
    width = both.shape[0]
    step = 256
    steps = width // parts // step
    place = lambda n: part * steps + n
    out = pl.BlockSpec((2, tokens // 4, step), lambda n: (0, 0, n))
    return call(
        units_back_kernel,
        "units_back",
        grid=(steps,),
        in_specs=[
            pl.BlockSpec((tokens, step), lambda n: (0, place(n))),
            fixed(tokens, half),
            fixed(tokens, half),
            pl.BlockSpec((step, 2 * half), lambda n: (place(n), 0)),
            fixed(tokens, 3 * RANK),
            fixed(tokens, 3 * RANK),
            pl.BlockSpec((2 * RANK, step), lambda n: (0, place(n))),
        ],
        out_specs=[out, out],
        out_shape=[shape((2, tokens // 4, width // parts), BF16)] * 2,
    )(first, d_gate, d_up, both, *inners, a_gu)


def lower_kernel(
    aa_ref, ab_ref, weight_ref, ia_ref, ib_ref, b_ref, whole_ref, g0, g1, g2, g3, keep_ref, give_ref, grad_ref, grad_gu_ref
):
    inner = (ia_ref[...] + ib_ref[...]).astype(BF16)
    low = inner[:, 2 * RANK :]
    half = aa_ref.shape[1]
    sums = contract(low, b_ref[...], 1, 0)
    sums = sums + contract(aa_ref[...], weight_ref[:half], 1, 0)
    sums = sums + contract(ab_ref[...], weight_ref[half:], 1, 0)
    sums = sums.astype(BF16)
    block = g0.shape[0]
    grad = jnp.zeros(grad_ref.shape, F32)
    for i, g in enumerate((g0, g1, g2, g3)):
        out = give_ref if i % 2 else keep_ref
        out[i // 2] = sums[i * block : (i + 1) * block]
        grad = grad + contract(low[i * block : (i + 1) * block], g[...], 0, 0)
    grad_ref[...] = grad
    grad_gu_ref[...] = contract(inner[:, : 2 * RANK], whole_ref[...], 0, 0)


def lower(act_a, act_b, weight, inners, bd, grads, whole):
    block, width = grads[0].shape
    tokens, half = act_a.shape
    step = 256
    tile = pl.BlockSpec((block, step), lambda n: (0, n))
    thin = pl.BlockSpec((RANK, step), lambda n: (0, n))
    out = pl.BlockSpec((2, block, step), lambda n: (0, 0, n))
    return call(
        lower_kernel,
        "lower",
        grid=(width // step,),
        in_specs=[
            fixed(tokens, half),
            fixed(tokens, half),
            pl.BlockSpec((2 * half, step), lambda n: (0, n)),
            fixed(tokens, 3 * RANK),
            fixed(tokens, 3 * RANK),
            thin,
            pl.BlockSpec((tokens, step), lambda n: (0, n)),
        ]
        + [tile] * 4,
        out_specs=[out, out, thin, pl.BlockSpec((2 * RANK, step), lambda n: (0, n))],
        out_shape=[shape((2, block, width), BF16)] * 2
        + [shape((RANK, width), F32), shape((2 * RANK, width), F32)],
    )(act_a, act_b, weight, *inners, bd, whole, *grads)


def wide_heads(ref):
    return jnp.concatenate([ref[h * HD : (h + 1) * HD] for h in range(GROUP)], axis=1)


def attend_kernel(seq_ref, limit_ref, q_ref, kv0, kv1, kv2, kv3, o_ref, e_ref, r_ref):
    queries = wide_heads(q_ref)
    limit = limit_ref[...]
    total = jnp.zeros(limit.shape, F32)
    mixed = jnp.zeros(queries.shape, F32)
    for bit, ref in enumerate((kv0, kv1, kv2, kv3)):
        block = ref.shape[2]
        scores = contract(ref[0, :HD], queries, 0, 0)
        places = (seq_ref[0] ^ bit) * block + lax.broadcasted_iota(jnp.int32, scores.shape, 0)
        raised = jnp.where(places <= limit, jnp.exp(scores), 0.0)
        total = total + jnp.sum(raised, axis=0, keepdims=True)
        low = raised.astype(BF16)
        e_ref[0, bit] = low
        mixed = mixed + contract(ref[0, HD:], low, 1, 0)
    inverse = 1.0 / total
    r_ref[0] = inverse
    mixed = (mixed * inverse).astype(BF16)
    width = q_ref.shape[1]
    for h in range(GROUP):
        o_ref[h * HD : (h + 1) * HD] = mixed[:, h * width : (h + 1) * width]


def attend(seq, limit, queries, keys_values):
    block = keys_values[0].shape[2]
    width = queries.shape[1]
    wide = GROUP * width
    head_rows = pl.BlockSpec((GROUP * HD, width), lambda g: (g, 0))
    return call(
        attend_kernel,
        "attend",
        grid=(KV,),
        in_specs=[SMEM, fixed(1, wide), head_rows]
        + [pl.BlockSpec((1, 2 * HD, block), lambda g: (g, 0, 0))] * 4,
        out_specs=[
            head_rows,
            pl.BlockSpec((1, 4, block, wide), lambda g: (g, 0, 0, 0)),
            pl.BlockSpec((1, 1, wide), lambda g: (g, 0, 0)),
        ],
        out_shape=[
            shape(queries.shape, BF16),
            shape((KV, 4, block, wide), BF16),
            shape((KV, 1, wide), F32),
        ],
    )(seq[None], limit, queries, *keys_values)


def attend_back_kernel(q_ref, kv0, kv1, kv2, kv3, e_ref, r_ref, o_ref, do_ref, dq_ref, keep_ref, give_ref):
    width = q_ref.shape[1]
    queries = wide_heads(q_ref)
    grads = wide_heads(do_ref).astype(F32) * r_ref[0]
    dots = jnp.sum(grads * wide_heads(o_ref).astype(F32), axis=0, keepdims=True)
    grads = grads.astype(BF16)
    d_queries = jnp.zeros(queries.shape, F32)
    for bit, ref in enumerate((kv0, kv1, kv2, kv3)):
        out = give_ref if bit % 2 else keep_ref
        raised = e_ref[0, bit]
        d_probs = contract(ref[0, HD:], grads, 0, 0)
        d_scores = (raised.astype(F32) * (d_probs - dots)).astype(BF16)
        d_queries = d_queries + contract(ref[0, :HD], d_scores, 1, 0)
        out[bit // 2, 0, :HD] = contract(queries, d_scores, 1, 1).astype(BF16)
        out[bit // 2, 0, HD:] = contract(grads, raised, 1, 1).astype(BF16)
    for h in range(GROUP):
        dq_ref[h * HD : (h + 1) * HD] = d_queries[:, h * width : (h + 1) * width]


def attend_back(first, count, queries, keys_values, raised, inverse, mixed, d_mixed):
    block = keys_values[0].shape[2]
    width = queries.shape[1]
    wide = GROUP * width
    head_rows = pl.BlockSpec((GROUP * HD, width), lambda g: (first + g, 0))
    shares = pl.BlockSpec((2, 1, 2 * HD, block), lambda g: (0, g, 0, 0))
    return call(
        attend_back_kernel,
        "attend_back",
        grid=(count,),
        in_specs=[head_rows]
        + [pl.BlockSpec((1, 2 * HD, block), lambda g: (first + g, 0, 0))] * 4
        + [
            pl.BlockSpec((1, 4, block, wide), lambda g: (first + g, 0, 0, 0)),
            pl.BlockSpec((1, 1, wide), lambda g: (first + g, 0, 0)),
            head_rows,
            head_rows,
        ],
        out_specs=[pl.BlockSpec((GROUP * HD, width), lambda g: (g, 0)), shares, shares],
        out_shape=[
            shape((count * GROUP * HD, width), F32),
            shape((2, count, 2 * HD, block), BF16),
            shape((2, count, 2 * HD, block), BF16),
        ],
    )(queries, *keys_values, raised, inverse, mixed, d_mixed)


def pick_kernel(ids_ref, *refs):
    out_ref = refs[-1]
    for d in range(out_ref.shape[0]):
        parts = [ref[ids_ref[d]] for ref in refs[:-1]]
        out_ref[d] = jnp.concatenate(parts, axis=1)


def pick(ids, stacks):
    columns = sum(stack.shape[2] for stack in stacks)
    n_dp = ids.shape[0]
    return call(
        pick_kernel,
        "pick",
        in_specs=[SMEM] + [VMEM] * len(stacks),
        out_shape=shape((n_dp, RANK, columns), BF16),
    )(ids, *stacks)


def spread_kernel(widths, seq_ref, mine_ref, p1, p2, p3, *refs):
    (in_ref, grow_ref, ao_ref, bo_ref, gu_ref, bd_ref, bg_ref, bu_ref, ad_ref, all_ref) = refs
    local, each, thin = widths
    n_dp = mine_ref.shape[0]
    seq = seq_ref[0]
    base = 3 * local
    all_ref[seq] = mine_ref[:, :, base:]
    for bit, ref in ((1, p1), (2, p2), (3, p3)):
        all_ref[seq ^ bit] = ref[...]

    def factor(start, width):
        parts = [all_ref[j, d, :, start : start + width] for d in range(n_dp) for j in range(4)]
        return jnp.concatenate(parts, axis=1)

    wide = lambda m: factor(m * each, each)
    for i in range(3):
        in_ref[i * RANK : (i + 1) * RANK] = wide(i)
    grow_ref[...] = jnp.zeros(grow_ref.shape, BF16)
    n_query, n_key = 4 * n_dp * each, 4 * n_dp * thin
    grow_ref[:RANK, :n_query] = wide(3)
    for i in range(2):
        start = n_query + i * n_key
        grow_ref[(i + 1) * RANK : (i + 2) * RANK, start : start + n_key] = factor(9 * each + i * thin, thin)
    ao_ref[...] = wide(4)
    bo_ref[...] = wide(5)
    gu_ref[:RANK] = wide(6)
    gu_ref[RANK:] = wide(7)
    bd_ref[...] = wide(8)
    for i, ref in enumerate((bg_ref, bu_ref, ad_ref)):
        for d in range(n_dp):
            ref[:, d * local : (d + 1) * local] = mine_ref[d, :, i * local : (i + 1) * local]


def spread(seq, mine, others, widths):
    local, each, thin = widths
    n_dp = mine.shape[0]
    total = 4 * n_dp * each
    grown = total + 8 * n_dp * thin
    rows = [(3 * RANK, total), (3 * RANK, grown), (RANK, total), (RANK, total), (2 * RANK, total), (RANK, total)]
    rows += [(RANK, n_dp * local)] * 3
    return call(
        functools.partial(spread_kernel, widths),
        "spread",
        in_specs=[SMEM] + [VMEM] * 4,
        out_shape=[shape(dims, BF16) for dims in rows],
        scratch_shapes=[pltpu.VMEM((4,) + others[0].shape, BF16)],
    )(seq[None], mine, *others)


def pack_kernel(n_dp, count, seq_ref, *refs):
    ins, refs = refs[:count], refs[count:]
    alone, (keep_ref, give_ref, alone_ref, all_ref) = refs[:-4], refs[-4:]
    for d in range(n_dp):
        for j in range(4):
            parts = []
            for ref in ins:
                each = ref.shape[1] // (4 * n_dp)
                at = (d * 4 + j) * each
                parts.append(ref[:, at : at + each])
            all_ref[j, d] = jnp.concatenate(parts, axis=1).astype(BF16)
    seq = seq_ref[0]
    for bit in range(4):
        out = give_ref if bit % 2 else keep_ref
        out[bit // 2] = all_ref[seq ^ bit]
    for i in range(0, len(alone), 2):
        for half in range(2):
            size = alone[i].shape[1] // (n_dp // 2)
            for d in range(n_dp // 2):
                place = slice((i // 2) * size, (i // 2 + 1) * size)
                part = alone[i + half][:, d * size : (d + 1) * size]
                alone_ref[half * (n_dp // 2) + d, :, place] = part.astype(BF16)


def pack(seq, grads, n_dp, alone):
    columns = sum(g.shape[1] for g in grads) // (4 * n_dp)
    dims = (n_dp, RANK, columns)
    outs = [shape((2,) + dims, BF16)] * 2
    outs.append(shape((n_dp, RANK, sum(g.shape[1] for g in alone) // n_dp), BF16))
    return call(
        functools.partial(pack_kernel, n_dp, len(grads)),
        "pack",
        in_specs=[SMEM] + [VMEM] * (len(grads) + len(alone)),
        out_shape=outs,
        scratch_shapes=[pltpu.VMEM((4,) + dims, BF16)],
    )(seq[None], *grads, *alone)


def sort_kernel(widths, ids_ref, came_ref, *out_refs):
    came = [came_ref[d].astype(F32) for d in range(came_ref.shape[0])]
    for a in range(ADAPT):
        total = jnp.zeros(came[0].shape, F32)
        for d, value in enumerate(came):
            total = total + jnp.where(ids_ref[d] == a, value, 0.0)
        at = 0
        for ref, width in zip(out_refs, widths):
            part = total[:, at : at + width]
            ref[a] = part.T if width < 64 else part
            at += width


def sort(ids, came, widths):
    outs = call(
        functools.partial(sort_kernel, widths),
        "sort",
        in_specs=[SMEM, VMEM],
        out_shape=[shape((ADAPT, w, RANK) if w < 64 else (ADAPT, RANK, w), F32) for w in widths],
    )(ids, came)
    return [o if w < 64 else o.transpose(0, 2, 1) for o, w in zip(outs, widths)]


def shards(
    tokens,
    cotangent,
    lengths,
    adapter_ids,
    attn_gain,
    query_gain,
    key_gain,
    ffn_gain,
    w_query,
    w_key,
    w_value,
    w_out,
    gate_weight,
    w_up,
    w_down,
    a_query,
    b_query,
    a_key,
    b_key,
    a_value,
    b_value,
    a_out,
    b_out,
    a_gate,
    b_gate,
    a_up,
    b_up,
    a_down,
    b_down,
):
    n_dp = lax.axis_size("dp")
    seq = lax.axis_index("seq")
    _, block, width = tokens.shape
    length = lengths[0]
    positions = seq * block + jnp.arange(block)
    valid = (positions < length).astype(F32)[:, None]
    sources = ring_sources()
    clock = Clock()
    n_query, n_key = H * HD, KV * HD
    local, each, thin = b_gate.shape[1], a_query.shape[1], b_key.shape[1]
    widths = (local, each, thin)

    attn = Ring(jnp.concatenate([w_query, w_key, w_value, w_out], axis=1))
    first_came, age = None, 0
    queue = [attn.pieces[0]]
    sides, acrosses, corners, going = [], [], [], []
    arrived = slot = 0
    last = attn.steps - 1
    while len(corners) < n_dp + 1:
        waits, new = [], []
        if not attn.complete():
            new = attn.step(clock)
            waits += new
            if attn.complete():
                ended = new
                new = [new]
        elif first_came is not None:
            age += 1
            if age == 3 and len(first_ring.pieces) == 3:
                waits += first_came
                first_came = None
        elif not first_ring.complete():
            first_came, age = first_ring.step(lambda v: after(v, ended) if len(first_ring.pieces) == 1 else clock(v)), 0
        while len(acrosses) < len(queue) and len(going) < 2:
            acrosses.append(partner(clock(queue[len(acrosses)]), 2))
            going.append(len(acrosses))
        for _ in range(3):
            if len(corners) < arrived:
                corners.append(partner(clock(acrosses[len(corners)]), 1))
                waits.append(corners[-1])
            elif len(sides) < len(queue):
                sides.append(partner(clock(queue[len(sides)]), 1))
                waits.append(sides[-1])
        if slot == 0:
            slots_a, slots_b = columns_for_seq(gate_weight, w_up, n_dp)
            ids = lax.all_to_all(
                jnp.broadcast_to(adapter_ids[None], (n_dp, 128)), "dp", 0, 0, tiled=True
            )[:, 0]
            stacks = (b_gate, b_up, a_down, a_query, a_key, a_value, b_query, a_out, b_out)
            stacks += (a_gate, a_up, b_down, b_key, b_value)
            sent = pick(ids, [m.transpose(0, 2, 1) for m in stacks])
            waits += [sent, slots_a]
        if slot == 1:
            swapped_a = lax.all_to_all(clock(slots_a), "seq", 0, 0, tiled=True)
        if slot == 2:
            mine = lax.all_to_all(clock(sent), "dp", 0, 0, tiled=True)
            first_ring = Ring(jnp.concatenate([w_down, swapped_a.reshape(-1, width)], axis=0))
            waits.append(first_ring.pieces[0])
        if slot == last + 2:
            inputs = clock(tokens)[0].astype(F32)
            normed = rms_scale(inputs, attn_gain).astype(BF16)
            normed_t = normed.T
            cot = cotangent[0].astype(F32)
            grad_out = (valid * clock(cot)).astype(BF16)
            waits += [normed_t, grad_out]
        if going and (slot == 0 or len(going) == 2 or len(queue) == n_dp + 1):
            waits.append(acrosses[going[0] - 1])
        else:
            going = going[:0] + going
        clock.tick(*waits)
        if going and any(w is acrosses[going[0] - 1] for w in waits):
            arrived = going.pop(0)
        if slot == 2:
            queue.append(clock(mine)[..., 3 * local :])
        queue += [jnp.concatenate(p, axis=0) if isinstance(p, tuple) else p for p in new]
        slot += 1
    others = [sides.pop(5), acrosses.pop(5), corners.pop(5)]
    queue.pop(5)
    attn_pieces = []
    for group in zip(queue, sides, acrosses, corners):
        attn_pieces += group
    order = everywhere_order(sources)

    belt = Conveyor(clock, [lambda: swapped_b.reshape(-1, width)])
    if first_came is None and not first_ring.complete():
        first_came = first_ring.step(clock)
    if first_came is not None:
        belt.going.append((first_came, first_ring))
    a_in, b_in, ao, bo, a_gu, bd, bg, bu, ad = spread(seq, mine, clock(others), widths)
    inner = contract(normed, a_in, 1, 1).astype(BF16)

    linear = project_in(order, normed_t, inner, b_in, attn_pieces)
    query_lin = linear[:n_query].reshape(H, HD, block)
    key_lin = linear[n_query : n_query + n_key].reshape(KV, HD, block)
    value_lin = linear[n_query + n_key :].reshape(KV, HD, block)
    cosine, sine = rotary_tables(positions)
    scale = HD**-0.5
    query_prep = lambda v: prepare(v, query_gain, cosine, sine)
    key_prep = lambda v: prepare(v, key_gain, cosine, sine)
    keys_values = jnp.concatenate([key_prep(key_lin), value_lin], axis=1).astype(BF16)
    grads = seq_pieces(clock(grad_out))
    keys_values = seq_pieces(after(keys_values, grads[2]))
    queries = (query_prep(query_lin) * scale).astype(BF16).reshape(n_query, block)
    limit = jnp.minimum(positions, length - 1).astype(jnp.int32)
    limit = jnp.tile(limit, GROUP)[None, :]
    belt.advance(queries, keys_values[2])
    swapped_b = lax.all_to_all(after(slots_b, queries), "seq", 0, 0, tiled=True)
    mixed, raised, inverse = attend(seq, limit, queries, keys_values)
    belt.advance(mixed)

    inner_out = contract(ao, mixed, 1, 0).astype(BF16)
    hidden, normed_two = project_out(
        order, mixed, inner_out, bo, tokens[0], valid, ffn_gain[None], attn_pieces
    )

    n2 = seq_pieces(normed_two)
    while not first_ring.complete():
        belt.advance(normed_two)
    ring_b = belt.rings[0]
    begun = place(clock(first_ring.pieces[:-1]), sources, 2)
    belt.until(first_ring, begun)
    w_lower, both_a = finish(begun, first_ring.pieces, sources)
    d_act, d_down = lower_back(clock(grads), w_lower, bd, ad)
    belt.advance(d_act)
    n2, low_n2 = all_tokens(n2, a_gu)
    act_a, dg_a, du_a, inner_a = units(0, n2, low_n2, both_a, bg, bu, ad, d_act)
    belt.advance(act_a)
    first = units_back_first(clock(dg_a), du_a, both_a)
    gbg_a, gbu_a, gad_a = units_grads(low_n2, d_down, after(act_a, first), dg_a, du_a)
    while not ring_b.complete():
        belt.advance(gbg_a)
    begun = place(clock(ring_b.pieces[:-1]), sources, 1)
    belt.until(ring_b, begun)
    (both_b,) = finish(begun, ring_b.pieces, sources)
    act_b, dg_b, du_b, inner_b = units(1, n2, low_n2, both_b, bg, bu, ad, d_act)
    inners = (inner_a, inner_b)
    keep, give = units_back(0, 2, first, dg_b, du_b, both_b, inners, a_gu)
    left, sent = seq_shares(keep, give)
    keep, give = units_back(1, 2, after(first, sent), dg_b, du_b, both_b, inners, a_gu)
    right, sent = seq_shares(keep, give)

    keep, give, grad_bd, grad_a_gu = lower(
        act_a, after(act_b, sent), w_lower, inners, bd, grads, n2
    )

    d_hidden, grad_update, d_inner_out = hidden_back(
        after(left[:2], keep) + left[2:], after(right[:2], keep) + right[2:], hidden, cotangent[0], valid, ffn_gain[None], bo
    )
    lowered, sent = seq_shares(*after((keep, give), grad_update))
    d_mixed = project_out_back(order, after(grad_update, sent), ao, d_inner_out, attn_pieces)
    count = KV // 2
    back = lambda part, d_mixed: attend_back(
        part * count, count, queries, keys_values, raised, inverse, mixed, d_mixed
    )
    d_query, keep, give = back(0, d_mixed)
    gbg_b, gbu_b, gad_b = units_grads(low_n2, d_down, after(act_b, d_query), dg_b, du_b)
    first_kv, sent = seq_shares(keep, give, (gbg_b, lowered[2]))
    other_query, keep, give = back(1, after(d_mixed, sent))
    other_kv, sent = seq_shares(keep, give)

    first_kv = total(after(first_kv, other_query))
    d_query = after(jnp.concatenate([d_query, other_query], axis=0), first_kv)
    d_queries = d_query.reshape(H, HD, block) * scale
    d_kv = jnp.concatenate([first_kv, total(other_kv)], axis=0)
    d_query_lin = jax.vjp(query_prep, query_lin)[1](d_queries)[0]
    d_key_lin = jax.vjp(key_prep, key_lin)[1](d_kv[:, :HD])[0]
    d_linear = jnp.concatenate(
        [
            d_query_lin.reshape(n_query, block),
            d_key_lin.reshape(n_key, block),
            d_kv[:, HD:].reshape(n_key, block),
        ],
        axis=0,
    ).astype(BF16)
    output = (hidden + valid * total(after(lowered, d_linear))).astype(BF16)
    d_inner = contract(b_in, d_linear, 1, 0).astype(BF16)
    grad_tokens = project_in_back(
        order, d_linear, a_in, d_inner, tokens[0], attn_gain[None], d_hidden, attn_pieces
    )

    grad_ao = contract(d_inner_out, mixed, 0, 1)
    grad_bo = contract(inner_out, grad_update, 1, 0)
    grad_a_in = contract(d_inner, normed, 1, 0)
    grad_b_in = contract(inner, d_linear, 0, 1)
    q_end, k_end = n_query, n_query + n_key
    partial = [grad_ao, grad_bo, grad_a_gu[:RANK], grad_a_gu[RANK:], grad_bd]
    partial += [grad_a_in[i * RANK : (i + 1) * RANK] for i in range(3)]
    partial += [grad_b_in[:RANK, :q_end]]
    partial += [grad_b_in[RANK : 2 * RANK, q_end:k_end], grad_b_in[2 * RANK :, k_end:]]
    whole = (gbg_a, gbg_b, gbu_a, gbu_b, gad_a, gad_b)
    keep, give, whole = pack(seq, partial, n_dp, whole)
    (keep, arrived, across), _ = seq_shares(keep, give)
    summed = total((keep, arrived, across)).astype(BF16)
    summed = after(jnp.concatenate([summed, whole], axis=2), output)
    sizes = [each] * 9 + [thin] * 2 + [local] * 3
    came = lax.all_to_all(summed, "dp", 0, 0, tiled=True)
    gao, gbo, gag, gau, gbd, gaq, gak, gav, gbq, gbk, gbv, gbg, gbu, gad = sort(ids, came, sizes)
    return (
        output[None],
        grad_tokens[None],
        gaq,
        gbq,
        gak,
        gbk,
        gav,
        gbv,
        gao,
        gbo,
        gag,
        gbg,
        gau,
        gbu,
        gad,
        gbd,
    )


def solution(mesh):
    tokens = P("dp", "seq", None)
    matrix = P(("dp", "seq"), None)
    stack = P(None, ("dp", "seq"), None)
    in_specs = (tokens, tokens, P("dp"), P("dp")) + (P(),) * 4 + (matrix,) * 7 + (stack,) * 14
    out_specs = (tokens, tokens) + (stack,) * 14
    return jax.shard_map(shards, mesh=mesh, in_specs=in_specs, out_specs=out_specs, check_vma=False)
```

```python
import functools

import jax
import jax.numpy as jnp
import numpy as np
from jax import lax
from jax.experimental import pallas as pl
from jax.experimental.pallas import tpu as pltpu
from jax.sharding import PartitionSpec as P

H = 32
KV = 8
HD = 64
GROUP = H // KV
ADAPT = 8
RANK = 16
EPS = 1e-05
F32 = jnp.float32
BF16 = jnp.bfloat16


def contract(left, right, left_dim, right_dim):
    return lax.dot_general(
        left, right, (((left_dim,), (right_dim,)), ((), ())), preferred_element_type=F32
    )


def rms_scale(operand, scaling, axis=-1):
    mean = jnp.mean(operand * operand, axis=axis, keepdims=True)
    return operand * lax.rsqrt(mean + EPS) * scaling


def rotary_tables(positions):
    frequency = jnp.power(1000000.0, -jnp.arange(HD // 2, dtype=F32) * 2.0 / HD)
    angles = frequency[:, None] * positions.astype(F32)[None, :]
    return jnp.cos(angles), jnp.sin(angles)


def prepare(linear, scaling, cosine, sine):
    normed = rms_scale(linear, scaling[:, None], axis=1)
    front, second = normed[:, : HD // 2], normed[:, HD // 2 :]
    return jnp.concatenate(
        [front * cosine - second * sine, second * cosine + front * sine], axis=1
    )


def after(value, *others):
    return lax.optimization_barrier((value, others))[0]


def ring_order(size):
    return list(range(0, size, 2)) + list(range(1, size, 2))[::-1]


def ring_pairs(size):
    order = ring_order(size)
    right = [(order[i], order[(i + 1) % size]) for i in range(size)]
    return right, [(b, a) for a, b in right]


def ring_offsets():
    offsets = [0]
    for step in range(1, (lax.axis_size("dp") - 1) // 2 + 1):
        offsets += [-step, step]
    return offsets + [lax.axis_size("dp") // 2]


class Ring:
    def __init__(self, own):
        self.pieces = [own]
        self.left = self.right = own
        self.steps = lax.axis_size("dp") // 2

    def complete(self):
        return len(self.pieces) == lax.axis_size("dp")

    def step(self, clock):
        size = lax.axis_size("dp")
        right, left = ring_pairs(size)
        if len(self.pieces) < size - 1:
            self.left = lax.ppermute(clock(self.left), "dp", right)
            self.right = lax.ppermute(clock(self.right), "dp", left)
            self.pieces += [self.left, self.right]
            return self.left, self.right
        half = self.left.shape[0] // 2
        last_left, last_right = clock((self.left, self.right))
        top = lax.ppermute(last_left[:half], "dp", right)
        bottom = lax.ppermute(last_right[half:], "dp", left)
        self.pieces.append((top, bottom))
        return top, bottom


def ring_sources():
    size = lax.axis_size("dp")
    here = lax.axis_index("dp")
    place = jnp.where(here % 2 == 0, here // 2, size - 1 - here // 2)
    sources = []
    for offset in ring_offsets():
        at = (place + offset + size) % size
        sources.append(jnp.where(at < size // 2, 2 * at, 2 * (size - 1 - at) + 1).astype(jnp.int32))
    return sources


class Clock:
    def __init__(self):
        self.done = ()

    def tick(self, *done):
        self.done = done

    def __call__(self, value):
        return after(value, self.done) if self.done else value


class Conveyor:
    def __init__(self, clock, waiting):
        self.clock = clock
        self.waiting = list(waiting)
        self.going = []
        self.rings = []

    def push(self):
        ring = Ring(self.waiting.pop(0)())
        self.going.append((ring.step(self.clock), ring))
        self.rings.append(ring)
        return ring

    def advance(self, *computed):
        if not self.going:
            self.clock.tick(self.clock.done, computed)
            return
        came, ring = self.going.pop(0)
        self.clock.tick(came, *computed)
        if not ring.complete():
            self.going.append((ring.step(self.clock), ring))
            if ring.complete() and self.waiting:
                self.push()

    def until(self, ring, *computed):
        self.clock.tick(self.clock.done, computed)
        while not ring.complete() or any(r is ring for _, r in self.going):
            self.advance(self.clock.done)


def partner(operand, bit):
    size = lax.axis_size("seq")
    return lax.ppermute(operand, "seq", [(i, i ^ bit) for i in range(size)])


def seq_pieces(own):
    across = partner(own, 2)
    return [own, partner(own, 1), across, partner(across, 1)]


def seq_shares(keep, give, wait=()):
    arrived = partner(give, 1)
    sent = (after(keep, wait)[1].astype(F32) + arrived[1].astype(F32)).astype(BF16)
    return (keep, arrived, partner(sent, 2)), sent


def total(shares):
    keep, arrived, across = shares
    return keep[0].astype(F32) + arrived[0].astype(F32) + across.astype(F32)


def everywhere_order(sources):
    seq = lax.axis_index("seq")
    return jnp.stack([s * 4 + (seq ^ bit) for s in sources for bit in range(4)]).astype(jnp.int32)


VMEM_LIMIT = 56 * 2**20
SMEM = pl.BlockSpec(memory_space=pltpu.SMEM)
VMEM = pl.BlockSpec(memory_space=pltpu.VMEM)


def call(kernel, name, flops=0, **options):
    return pl.pallas_call(
        kernel,
        compiler_params=pltpu.CompilerParams(vmem_limit_bytes=VMEM_LIMIT),
        cost_estimate=pl.CostEstimate(flops=int(flops), bytes_accessed=0, transcendentals=0),
        name=name,
        **options,
    )


def shape(dims, dtype):
    return jax.ShapeDtypeStruct(dims, dtype)


def fixed(*dims):
    return pl.BlockSpec(dims, lambda *_: (0,) * len(dims))


def columns_kernel(n_dp, gate_ref, up_ref, *out_refs):
    size = gate_ref.shape[1] // (4 * n_dp)
    for half, out in enumerate(out_refs):
        for m, ref in enumerate((gate_ref, up_ref)):
            for q in range(n_dp // 2):
                place = (m * (n_dp // 2) + q) * size
                for j in range(4):
                    start = ((half * (n_dp // 2) + q) * 4 + j) * size
                    out[j, :, place : place + size] = ref[:, start : start + size]


def columns_for_seq(gate, up, n_dp):
    rows, total = gate.shape
    return call(
        functools.partial(columns_kernel, n_dp),
        "columns",
        in_specs=[VMEM] * 2,
        out_shape=[shape((4, rows, total // 4), BF16)] * 2,
    )(gate, up)


ANY = pl.BlockSpec(memory_space=pl.ANY)


def place_kernel(count, sources_ref, *refs):
    pieces, outs, sems = refs[: -count - 1], refs[-count - 1 : -1], refs[-1]
    copies = []
    for i, piece in enumerate(pieces):
        rows = piece.shape[0] // count
        start = pl.multiple_of(sources_ref[i] * rows, rows)
        for j, out in enumerate(outs):
            part = piece.at[pl.ds(j * rows, rows)]
            copies.append(pltpu.make_async_copy(part, out.at[pl.ds(start, rows)], sems.at[i, j]))
    for copy in copies:
        copy.start()
    for copy in copies:
        copy.wait()


def finish_kernel(count, source_ref, *refs):
    (top_ref, bottom_ref), outs, sems = refs[count : count + 2], refs[count + 2 : -1], refs[-1]
    copies = []
    if count == 2:
        rows = top_ref.shape[0]
        start = pl.multiple_of(source_ref[0] * rows, rows)
        for i, piece in enumerate((top_ref, bottom_ref)):
            copies.append(pltpu.make_async_copy(piece, outs[i].at[pl.ds(start, rows)], sems.at[i]))
    else:
        rows = top_ref.shape[0]
        for i, piece in enumerate((top_ref, bottom_ref)):
            start = pl.multiple_of(source_ref[0] * (2 * rows), 2 * rows) + i * rows
            copies.append(pltpu.make_async_copy(piece, outs[0].at[pl.ds(start, rows)], sems.at[i]))
    for copy in copies:
        copy.start()
    for copy in copies:
        copy.wait()


def place(pieces, sources, count):
    rows, columns = pieces[0].shape
    most = len(pieces)
    return call(
        functools.partial(place_kernel, count),
        "place",
        in_specs=[SMEM] + [VMEM] * most,
        out_specs=[ANY] * count,
        out_shape=[shape(((most + 1) * rows // count, columns), BF16)] * count,
        scratch_shapes=[pltpu.SemaphoreType.DMA((most, count))],
    )(jnp.stack(sources[:-1]), *pieces)


def finish(begun, pieces, sources):
    count = len(begun)
    return call(
        functools.partial(finish_kernel, count),
        "finish",
        in_specs=[SMEM] + [ANY] * count + [VMEM] * 2,
        out_specs=[ANY] * count,
        out_shape=[shape(m.shape, BF16) for m in begun],
        scratch_shapes=[pltpu.SemaphoreType.DMA((2,))],
        input_output_aliases={i + 1: i for i in range(count)},
    )(sources[-1][None], *begun, *pieces[-1])


def gather_rows(order_ref, source_ref, target_ref, rows):
    total = source_ref.shape[0]
    wide = min(256, total)
    each = wide // rows
    for i in range(total // wide):
        blocks = []
        for j in range(each):
            start = pl.multiple_of(order_ref[i * each + j] * rows, rows)
            blocks.append(source_ref[pl.ds(start, rows), :])
        target_ref[:, i * wide : (i + 1) * wide] = jnp.concatenate(blocks, axis=0).T


def qkv_kernel(order_ref, normed_ref, inner_ref, b_ref, *refs):
    pieces, (out_ref, left_ref) = refs[:-2], refs[-2:]

    @pl.when(pl.program_id(0) == 0)
    def _():
        gather_rows(order_ref, normed_ref, left_ref, pieces[0].shape[0])

    width = pieces[0].shape[1]
    step = 512
    for c in range(0, width, step):
        right = jnp.concatenate([p[:, c : c + step] for p in pieces], axis=0)
        sums = contract(left_ref[...], right, 1, 0)
        sums = sums + contract(inner_ref[...], b_ref[:, c : c + step], 1, 0)
        out_ref[c : c + step, :] = sums.T


def project_in(order, normed_t, inner, b_in, pieces):
    width, tokens = normed_t.shape
    total = b_in.shape[1]
    step = 1024
    rows = pieces[0].shape[0]
    return call(
        qkv_kernel,
        "project_in",
        grid=(total // step,),
        in_specs=[
            SMEM,
            fixed(width, tokens),
            fixed(*inner.shape),
            pl.BlockSpec((b_in.shape[0], step), lambda c: (0, c)),
        ]
        + [pl.BlockSpec((rows, step), lambda c: (0, c))] * len(pieces),
        out_specs=pl.BlockSpec((step, tokens), lambda c: (c, 0)),
        out_shape=shape((total, tokens), F32),
        scratch_shapes=[pltpu.VMEM((tokens, width), BF16)],
    )(order, normed_t, inner, b_in, *pieces)


def out_kernel(order_ref, mixed_ref, inner_ref, b_ref, tokens_ref, valid_ref, gain_ref, *refs):
    pieces, (hidden_ref, normed_ref, left_ref) = refs[:-3], refs[-3:]
    c = pl.program_id(0)

    @pl.when(c == 0)
    def _():
        gather_rows(order_ref, mixed_ref, left_ref, pieces[0].shape[0])

    width = pieces[0].shape[1]
    right = jnp.concatenate([p[...] for p in pieces], axis=0)
    sums = contract(left_ref[...], right, 1, 0) + contract(inner_ref[...], b_ref[...], 0, 0)
    sums = tokens_ref[...].astype(F32) + valid_ref[...] * sums
    hidden_ref[:, pl.ds(pl.multiple_of(c * width, width), width)] = sums

    @pl.when(c == pl.num_programs(0) - 1)
    def _():
        hidden = hidden_ref[...]
        normed_ref[...] = rms_scale(hidden, gain_ref[...]).astype(BF16)


def project_out(order, mixed, inner, bo, tokens, valid, gain, pieces):
    features, block = mixed.shape
    width = tokens.shape[1]
    step = 1024
    rows = pieces[0].shape[0]
    skip = (pieces[0].shape[1] - width) // step
    return call(
        out_kernel,
        "project_out",
        grid=(width // step,),
        in_specs=[
            SMEM,
            fixed(features, block),
            fixed(*inner.shape),
            pl.BlockSpec((RANK, step), lambda c: (0, c)),
            pl.BlockSpec((block, step), lambda c: (0, c)),
            fixed(block, 1),
            fixed(1, width),
        ]
        + [pl.BlockSpec((rows, step), lambda c: (0, c + skip))] * len(pieces),
        out_specs=[fixed(block, width), fixed(block, width)],
        out_shape=[shape((block, width), F32), shape((block, width), BF16)],
        scratch_shapes=[pltpu.VMEM((block, features), BF16)],
    )(order, mixed, inner, bo, tokens, valid, gain, *pieces)


def scatter_products(order_ref, pieces, right, sums_ref, form):
    rows = pieces[0].shape[0]
    each = max(1, 256 // rows)
    for i in range(0, len(pieces), each):
        left = jnp.concatenate([p[...] for p in pieces[i : i + each]], axis=0)
        product = contract(left, right, 1, form)
        for j in range(each):
            start = pl.multiple_of(order_ref[i + j] * rows, rows)
            sums_ref[pl.ds(start, rows), :] += product[j * rows : (j + 1) * rows]


def out_back_kernel(order_ref, grad_ref, a_ref, inner_ref, *refs):
    pieces, (out_ref, sums_ref) = refs[:-2], refs[-2:]
    c = pl.program_id(0)

    @pl.when(c == 0)
    def _():
        sums_ref[...] = contract(a_ref[...], inner_ref[...], 0, 1)

    scatter_products(order_ref, pieces, grad_ref[...], sums_ref, 1)

    @pl.when(c == pl.num_programs(0) - 1)
    def _():
        out_ref[...] = sums_ref[...].astype(BF16)


def project_out_back(order, grad, ao, d_inner, pieces):
    block, width = grad.shape
    features = ao.shape[1]
    step = 1024
    rows = pieces[0].shape[0]
    skip = (pieces[0].shape[1] - width) // step
    return call(
        out_back_kernel,
        "project_out_back",
        grid=(width // step,),
        in_specs=[
            SMEM,
            pl.BlockSpec((block, step), lambda c: (0, c)),
            fixed(*ao.shape),
            fixed(*d_inner.shape),
        ]
        + [pl.BlockSpec((rows, step), lambda c: (0, c + skip))] * len(pieces),
        out_specs=fixed(features, block),
        out_shape=shape((features, block), BF16),
        scratch_shapes=[pltpu.VMEM((features, block), F32)],
    )(order, grad, ao, d_inner, *pieces)


def in_back_kernel(order_ref, grad_ref, a_ref, inner_ref, tokens_ref, gain_ref, base_ref, *refs):
    pieces, (out_ref, sums_ref, turned_ref) = refs[:-3], refs[-3:]
    c = pl.program_id(0)

    @pl.when(c == 0)
    def _():
        sums_ref[...] = contract(a_ref[...], inner_ref[...], 0, 0)

    scatter_products(order_ref, pieces, grad_ref[...], sums_ref, 0)

    @pl.when(c == pl.num_programs(0) - 1)
    def _():
        size = sums_ref.shape[1]
        for i in range(0, sums_ref.shape[0], size):
            turned_ref[:, i : i + size] = sums_ref[i : i + size, :].T
        inputs = tokens_ref[...].astype(F32)
        grad = turned_ref[...] * gain_ref[...]
        scale = lax.rsqrt(jnp.mean(inputs * inputs, axis=-1, keepdims=True) + EPS)
        along = jnp.mean(inputs * grad, axis=-1, keepdims=True) * scale * scale
        out_ref[...] = (base_ref[...] + scale * (grad - inputs * along)).astype(BF16)


def project_in_back(order, d_linear, a_in, d_inner, tokens, gain, base, pieces):
    total, block = d_linear.shape
    width = tokens.shape[1]
    step = 1024
    rows = pieces[0].shape[0]
    return call(
        in_back_kernel,
        "project_in_back",
        grid=(total // step,),
        in_specs=[
            SMEM,
            pl.BlockSpec((step, block), lambda c: (c, 0)),
            fixed(*a_in.shape),
            fixed(*d_inner.shape),
            fixed(block, width),
            fixed(1, width),
            fixed(block, width),
        ]
        + [pl.BlockSpec((rows, step), lambda c: (0, c))] * len(pieces),
        out_specs=fixed(block, width),
        out_shape=shape((block, width), BF16),
        scratch_shapes=[pltpu.VMEM((width, block), F32), pltpu.VMEM((block, width), F32)],
    )(order, d_linear, a_in, d_inner, tokens, gain, base, *pieces)


def hidden_back_kernel(l0, l1, l2, r0, r1, r2, hidden_ref, cot_ref, valid_ref, gain_ref, b_ref, dh_ref, gu_ref, inner_ref):
    half = l2.shape[1]
    for i, refs in enumerate(((l0, l1, l2), (r0, r1, r2))):
        part = slice(i * half, (i + 1) * half)
        grad = refs[0][0].astype(F32) + refs[1][0].astype(F32) + refs[2][...].astype(F32)
        dh_ref[:, part] = grad * gain_ref[:, part]
    hidden, grad = hidden_ref[...], dh_ref[...]
    scale = lax.rsqrt(jnp.mean(hidden * hidden, axis=-1, keepdims=True) + EPS)
    along = jnp.mean(hidden * grad, axis=-1, keepdims=True) * scale * scale
    grad = cot_ref[...].astype(F32) + scale * (grad - hidden * along)
    dh_ref[...] = grad
    low = (valid_ref[...] * grad).astype(BF16)
    gu_ref[...] = low
    inner_ref[...] = contract(low, b_ref[...], 1, 1).astype(BF16)


def hidden_back(left, right, hidden, cot, valid, gain, bo):
    block, width = hidden.shape
    rows = block // 4
    share = pl.BlockSpec((1, rows, width // 2), lambda i: (0, i, 0))
    across = pl.BlockSpec((rows, width // 2), lambda i: (i, 0))
    whole = pl.BlockSpec((rows, width), lambda i: (i, 0))
    return call(
        hidden_back_kernel,
        "hidden_back",
        flops=7e9,
        grid=(4,),
        in_specs=[share, share, across] * 2
        + [whole, whole, pl.BlockSpec((rows, 1), lambda i: (i, 0)), fixed(1, width), fixed(*bo.shape)],
        out_specs=[whole, whole, pl.BlockSpec((rows, RANK), lambda i: (i, 0))],
        out_shape=[shape((block, width), F32), shape((block, width), BF16), shape((block, RANK), BF16)],
    )(*left, *right, hidden, cot, valid, gain, bo)


def gather_tokens(refs, whole_ref):
    block = refs[0].shape[0]
    for i, ref in enumerate(refs):
        whole_ref[i * block : (i + 1) * block, :] = ref[...]


def lower_back_kernel(g0, g1, g2, g3, weight_ref, b_ref, a_ref, out_ref, inner_ref, whole_ref):
    @pl.when(pl.program_id(0) == 0)
    def _():
        gather_tokens((g0, g1, g2, g3), whole_ref)
        inner_ref[...] = contract(whole_ref[...], b_ref[...], 1, 1).astype(BF16)

    sums = contract(whole_ref[...], weight_ref[...], 1, 1)
    out_ref[...] = (sums + contract(inner_ref[...], a_ref[...], 1, 0)).astype(BF16)


def lower_back(grads, weight, bd, ad):
    block, width = grads[0].shape
    units = weight.shape[0]
    step = 512
    tokens = 4 * block
    return call(
        lower_back_kernel,
        "lower_back",
        grid=(units // step,),
        in_specs=[fixed(block, width)] * 4
        + [
            pl.BlockSpec((step, width), lambda j: (j, 0)),
            fixed(RANK, width),
            pl.BlockSpec((RANK, step), lambda j: (0, j)),
        ],
        out_specs=[pl.BlockSpec((tokens, step), lambda j: (0, j)), fixed(tokens, RANK)],
        out_shape=[shape((tokens, units), BF16), shape((tokens, RANK), BF16)],
        scratch_shapes=[pltpu.VMEM((tokens, width), BF16)],
    )(*grads, weight, bd, ad)


def tokens_kernel(n0, n1, n2, n3, a_ref, whole_ref, low_ref):
    gather_tokens((n0, n1, n2, n3), whole_ref)
    low_ref[...] = contract(whole_ref[...], a_ref[...], 1, 1).astype(BF16)


def all_tokens(normed, a_gu):
    block, width = normed[0].shape
    return call(
        tokens_kernel,
        "all_tokens",
        out_shape=[shape((4 * block, width), BF16), shape((4 * block, 2 * RANK), BF16)],
    )(*normed, a_gu)


def units_kernel(
    whole_ref,
    low_ref,
    gate_ref,
    up_ref,
    bg_ref,
    bu_ref,
    ad_ref,
    d_act_ref,
    act_ref,
    dg_ref,
    du_ref,
    inner_ref,
):
    @pl.when(pl.program_id(0) == 0)
    def _():
        inner_ref[...] = jnp.zeros(inner_ref.shape, F32)

    low_gate, low_up = low_ref[:, :RANK], low_ref[:, RANK:]
    gate = contract(whole_ref[...], gate_ref[...], 1, 0) + contract(low_gate, bg_ref[...], 1, 0)
    up = contract(whole_ref[...], up_ref[...], 1, 0) + contract(low_up, bu_ref[...], 1, 0)
    d_act = d_act_ref[...].astype(F32)
    sig = jax.nn.sigmoid(gate)
    silu = gate * sig
    act = (silu * up).astype(BF16)
    d_gate = (d_act * up * (sig + silu * (1.0 - sig))).astype(BF16)
    d_up = (d_act * silu).astype(BF16)
    act_ref[...] = act
    dg_ref[...] = d_gate
    du_ref[...] = d_up
    inner_ref[:, :RANK] += contract(d_gate, bg_ref[...], 1, 1)
    inner_ref[:, RANK : 2 * RANK] += contract(d_up, bu_ref[...], 1, 1)
    inner_ref[:, 2 * RANK :] += contract(act, ad_ref[...], 1, 1)


def units(part, whole, low, both, bg, bu, ad, d_act):
    tokens, width = whole.shape
    half = both.shape[1] // 2
    step = 256
    steps = half // step
    here = pl.BlockSpec((RANK, step), lambda j: (0, part * steps + j))
    tile = pl.BlockSpec((tokens, step), lambda j: (0, j))
    return call(
        units_kernel,
        "units",
        grid=(steps,),
        in_specs=[
            fixed(tokens, width),
            fixed(tokens, 2 * RANK),
            pl.BlockSpec((width, step), lambda j: (0, j)),
            pl.BlockSpec((width, step), lambda j: (0, steps + j)),
            here,
            here,
            here,
            pl.BlockSpec((tokens, step), lambda j: (0, part * steps + j)),
        ],
        out_specs=[tile] * 3 + [fixed(tokens, 3 * RANK)],
        out_shape=[shape((tokens, half), BF16)] * 3 + [shape((tokens, 3 * RANK), F32)],
    )(whole, low, both, both, bg, bu, ad, d_act)


def units_grads_kernel(low_ref, d_down_ref, act_ref, dg_ref, du_ref, gbg_ref, gbu_ref, gad_ref):
    gbg_ref[...] = contract(low_ref[:, :RANK], dg_ref[...], 0, 0)
    gbu_ref[...] = contract(low_ref[:, RANK:], du_ref[...], 0, 0)
    gad_ref[...] = contract(d_down_ref[...], act_ref[...], 0, 0)


def units_grads(low, d_down, act, d_gate, d_up):
    tokens, half = act.shape
    step = 256
    tile = pl.BlockSpec((tokens, step), lambda j: (0, j))
    thin = pl.BlockSpec((RANK, step), lambda j: (0, j))
    return call(
        units_grads_kernel,
        "units_grads",
        grid=(half // step,),
        in_specs=[fixed(tokens, 2 * RANK), fixed(tokens, RANK), tile, tile, tile],
        out_specs=[thin] * 3,
        out_shape=[shape((RANK, half), F32)] * 3,
    )(low, d_down, act, d_gate, d_up)


def units_back_first_kernel(g_ref, u_ref, w_ref, out_ref):
    half = g_ref.shape[1]
    sums = contract(g_ref[...], w_ref[:, :half], 1, 1) + contract(u_ref[...], w_ref[:, half:], 1, 1)
    out_ref[...] = sums.astype(BF16)


def units_back_first(d_gate, d_up, both):
    tokens, half = d_gate.shape
    width = both.shape[0]
    step = 512
    return call(
        units_back_first_kernel,
        "units_back_first",
        grid=(width // step,),
        in_specs=[fixed(tokens, half)] * 2 + [pl.BlockSpec((step, 2 * half), lambda n: (n, 0))],
        out_specs=pl.BlockSpec((tokens, step), lambda n: (0, n)),
        out_shape=shape((tokens, width), BF16),
    )(d_gate, d_up, both)


def units_back_kernel(first_ref, g_ref, u_ref, w_ref, ia_ref, ib_ref, a_ref, keep_ref, give_ref):
    half = g_ref.shape[1]
    low = (ia_ref[...] + ib_ref[...]).astype(BF16)[:, : 2 * RANK]
    sums = first_ref[...].astype(F32) + contract(low, a_ref[...], 1, 0)
    sums = sums + contract(g_ref[...], w_ref[:, :half], 1, 1)
    sums = sums + contract(u_ref[...], w_ref[:, half:], 1, 1)
    sums = sums.astype(BF16)
    block = keep_ref.shape[1]
    keep_ref[0] = sums[:block]
    give_ref[0] = sums[block : 2 * block]
    keep_ref[1] = sums[2 * block : 3 * block]
    give_ref[1] = sums[3 * block :]


def units_back(part, parts, first, d_gate, d_up, both, inners, a_gu):
    tokens, half = d_gate.shape
    width = both.shape[0]
    step = 256
    steps = width // parts // step
    place = lambda n: part * steps + n
    out = pl.BlockSpec((2, tokens // 4, step), lambda n: (0, 0, n))
    return call(
        units_back_kernel,
        "units_back",
        grid=(steps,),
        in_specs=[
            pl.BlockSpec((tokens, step), lambda n: (0, place(n))),
            fixed(tokens, half),
            fixed(tokens, half),
            pl.BlockSpec((step, 2 * half), lambda n: (place(n), 0)),
            fixed(tokens, 3 * RANK),
            fixed(tokens, 3 * RANK),
            pl.BlockSpec((2 * RANK, step), lambda n: (0, place(n))),
        ],
        out_specs=[out, out],
        out_shape=[shape((2, tokens // 4, width // parts), BF16)] * 2,
    )(first, d_gate, d_up, both, *inners, a_gu)


def lower_kernel(
    aa_ref, ab_ref, weight_ref, ia_ref, ib_ref, b_ref, whole_ref, g0, g1, g2, g3, keep_ref, give_ref, grad_ref, grad_gu_ref
):
    inner = (ia_ref[...] + ib_ref[...]).astype(BF16)
    low = inner[:, 2 * RANK :]
    half = aa_ref.shape[1]
    sums = contract(low, b_ref[...], 1, 0)
    sums = sums + contract(aa_ref[...], weight_ref[:half], 1, 0)
    sums = sums + contract(ab_ref[...], weight_ref[half:], 1, 0)
    sums = sums.astype(BF16)
    block = g0.shape[0]
    grad = jnp.zeros(grad_ref.shape, F32)
    for i, g in enumerate((g0, g1, g2, g3)):
        out = give_ref if i % 2 else keep_ref
        out[i // 2] = sums[i * block : (i + 1) * block]
        grad = grad + contract(low[i * block : (i + 1) * block], g[...], 0, 0)
    grad_ref[...] = grad
    grad_gu_ref[...] = contract(inner[:, : 2 * RANK], whole_ref[...], 0, 0)


def lower(act_a, act_b, weight, inners, bd, grads, whole):
    block, width = grads[0].shape
    tokens, half = act_a.shape
    step = 512
    tile = pl.BlockSpec((block, step), lambda n: (0, n))
    thin = pl.BlockSpec((RANK, step), lambda n: (0, n))
    out = pl.BlockSpec((2, block, step), lambda n: (0, 0, n))
    return call(
        lower_kernel,
        "lower",
        grid=(width // step,),
        in_specs=[
            fixed(tokens, half),
            fixed(tokens, half),
            pl.BlockSpec((2 * half, step), lambda n: (0, n)),
            fixed(tokens, 3 * RANK),
            fixed(tokens, 3 * RANK),
            thin,
            pl.BlockSpec((tokens, step), lambda n: (0, n)),
        ]
        + [tile] * 4,
        out_specs=[out, out, thin, pl.BlockSpec((2 * RANK, step), lambda n: (0, n))],
        out_shape=[shape((2, block, width), BF16)] * 2
        + [shape((RANK, width), F32), shape((2 * RANK, width), F32)],
    )(act_a, act_b, weight, *inners, bd, whole, *grads)


def wide_heads(ref):
    return jnp.concatenate([ref[h * HD : (h + 1) * HD] for h in range(GROUP)], axis=1)


def attend_kernel(seq_ref, limit_ref, q_ref, kv0, kv1, kv2, kv3, o_ref, e_ref, r_ref):
    queries = wide_heads(q_ref)
    limit = limit_ref[...]
    total = jnp.zeros(limit.shape, F32)
    mixed = jnp.zeros(queries.shape, F32)
    for bit, ref in enumerate((kv0, kv1, kv2, kv3)):
        block = ref.shape[2]
        scores = contract(ref[0, :HD], queries, 0, 0)
        places = (seq_ref[0] ^ bit) * block + lax.broadcasted_iota(jnp.int32, scores.shape, 0)
        raised = jnp.where(places <= limit, jnp.exp(scores), 0.0)
        total = total + jnp.sum(raised, axis=0, keepdims=True)
        low = raised.astype(BF16)
        e_ref[0, bit] = low
        mixed = mixed + contract(ref[0, HD:], low, 1, 0)
    inverse = 1.0 / total
    r_ref[0] = inverse
    mixed = (mixed * inverse).astype(BF16)
    width = q_ref.shape[1]
    for h in range(GROUP):
        o_ref[h * HD : (h + 1) * HD] = mixed[:, h * width : (h + 1) * width]


def attend(seq, limit, queries, keys_values):
    block = keys_values[0].shape[2]
    width = queries.shape[1]
    wide = GROUP * width
    head_rows = pl.BlockSpec((GROUP * HD, width), lambda g: (g, 0))
    return call(
        attend_kernel,
        "attend",
        grid=(KV,),
        in_specs=[SMEM, fixed(1, wide), head_rows]
        + [pl.BlockSpec((1, 2 * HD, block), lambda g: (g, 0, 0))] * 4,
        out_specs=[
            head_rows,
            pl.BlockSpec((1, 4, block, wide), lambda g: (g, 0, 0, 0)),
            pl.BlockSpec((1, 1, wide), lambda g: (g, 0, 0)),
        ],
        out_shape=[
            shape(queries.shape, BF16),
            shape((KV, 4, block, wide), BF16),
            shape((KV, 1, wide), F32),
        ],
    )(seq[None], limit, queries, *keys_values)


def attend_back_kernel(q_ref, kv0, kv1, kv2, kv3, e_ref, r_ref, o_ref, do_ref, dq_ref, keep_ref, give_ref):
    width = q_ref.shape[1]
    queries = wide_heads(q_ref)
    grads = wide_heads(do_ref).astype(F32) * r_ref[0]
    dots = jnp.sum(grads * wide_heads(o_ref).astype(F32), axis=0, keepdims=True)
    grads = grads.astype(BF16)
    d_queries = jnp.zeros(queries.shape, F32)
    for bit, ref in enumerate((kv0, kv1, kv2, kv3)):
        out = give_ref if bit % 2 else keep_ref
        raised = e_ref[0, bit]
        d_probs = contract(ref[0, HD:], grads, 0, 0)
        d_scores = (raised.astype(F32) * (d_probs - dots)).astype(BF16)
        d_queries = d_queries + contract(ref[0, :HD], d_scores, 1, 0)
        out[bit // 2, 0, :HD] = contract(queries, d_scores, 1, 1).astype(BF16)
        out[bit // 2, 0, HD:] = contract(grads, raised, 1, 1).astype(BF16)
    for h in range(GROUP):
        dq_ref[h * HD : (h + 1) * HD] = d_queries[:, h * width : (h + 1) * width]


def attend_back(first, count, queries, keys_values, raised, inverse, mixed, d_mixed):
    block = keys_values[0].shape[2]
    width = queries.shape[1]
    wide = GROUP * width
    head_rows = pl.BlockSpec((GROUP * HD, width), lambda g: (first + g, 0))
    shares = pl.BlockSpec((2, 1, 2 * HD, block), lambda g: (0, g, 0, 0))
    return call(
        attend_back_kernel,
        "attend_back",
        grid=(count,),
        in_specs=[head_rows]
        + [pl.BlockSpec((1, 2 * HD, block), lambda g: (first + g, 0, 0))] * 4
        + [
            pl.BlockSpec((1, 4, block, wide), lambda g: (first + g, 0, 0, 0)),
            pl.BlockSpec((1, 1, wide), lambda g: (first + g, 0, 0)),
            head_rows,
            head_rows,
        ],
        out_specs=[pl.BlockSpec((GROUP * HD, width), lambda g: (g, 0)), shares, shares],
        out_shape=[
            shape((count * GROUP * HD, width), F32),
            shape((2, count, 2 * HD, block), BF16),
            shape((2, count, 2 * HD, block), BF16),
        ],
    )(queries, *keys_values, raised, inverse, mixed, d_mixed)


def pick_kernel(ids_ref, *refs):
    out_ref = refs[-1]
    for d in range(out_ref.shape[0]):
        parts = [ref[ids_ref[d]] for ref in refs[:-1]]
        out_ref[d] = jnp.concatenate(parts, axis=1)


def pick(ids, stacks):
    columns = sum(stack.shape[2] for stack in stacks)
    n_dp = ids.shape[0]
    return call(
        pick_kernel,
        "pick",
        in_specs=[SMEM] + [VMEM] * len(stacks),
        out_shape=shape((n_dp, RANK, columns), BF16),
    )(ids, *stacks)


def spread_kernel(widths, seq_ref, mine_ref, p1, p2, p3, *refs):
    (in_ref, grow_ref, ao_ref, bo_ref, gu_ref, bd_ref, bg_ref, bu_ref, ad_ref, all_ref) = refs
    local, each, thin = widths
    n_dp = mine_ref.shape[0]
    seq = seq_ref[0]
    base = 3 * local
    all_ref[seq] = mine_ref[:, :, base:]
    for bit, ref in ((1, p1), (2, p2), (3, p3)):
        all_ref[seq ^ bit] = ref[...]

    def factor(start, width):
        parts = [all_ref[j, d, :, start : start + width] for d in range(n_dp) for j in range(4)]
        return jnp.concatenate(parts, axis=1)

    wide = lambda m: factor(m * each, each)
    for i in range(3):
        in_ref[i * RANK : (i + 1) * RANK] = wide(i)
    grow_ref[...] = jnp.zeros(grow_ref.shape, BF16)
    n_query, n_key = 4 * n_dp * each, 4 * n_dp * thin
    grow_ref[:RANK, :n_query] = wide(3)
    for i in range(2):
        start = n_query + i * n_key
        grow_ref[(i + 1) * RANK : (i + 2) * RANK, start : start + n_key] = factor(9 * each + i * thin, thin)
    ao_ref[...] = wide(4)
    bo_ref[...] = wide(5)
    gu_ref[:RANK] = wide(6)
    gu_ref[RANK:] = wide(7)
    bd_ref[...] = wide(8)
    for i, ref in enumerate((bg_ref, bu_ref, ad_ref)):
        for d in range(n_dp):
            ref[:, d * local : (d + 1) * local] = mine_ref[d, :, i * local : (i + 1) * local]


def spread(seq, mine, others, widths):
    local, each, thin = widths
    n_dp = mine.shape[0]
    total = 4 * n_dp * each
    grown = total + 8 * n_dp * thin
    rows = [(3 * RANK, total), (3 * RANK, grown), (RANK, total), (RANK, total), (2 * RANK, total), (RANK, total)]
    rows += [(RANK, n_dp * local)] * 3
    return call(
        functools.partial(spread_kernel, widths),
        "spread",
        in_specs=[SMEM] + [VMEM] * 4,
        out_shape=[shape(dims, BF16) for dims in rows],
        scratch_shapes=[pltpu.VMEM((4,) + others[0].shape, BF16)],
    )(seq[None], mine, *others)


def pack_kernel(n_dp, count, seq_ref, *refs):
    ins, refs = refs[:count], refs[count:]
    alone, (keep_ref, give_ref, alone_ref, all_ref) = refs[:-4], refs[-4:]
    for d in range(n_dp):
        for j in range(4):
            parts = []
            for ref in ins:
                each = ref.shape[1] // (4 * n_dp)
                at = (d * 4 + j) * each
                parts.append(ref[:, at : at + each])
            all_ref[j, d] = jnp.concatenate(parts, axis=1).astype(BF16)
    seq = seq_ref[0]
    for bit in range(4):
        out = give_ref if bit % 2 else keep_ref
        out[bit // 2] = all_ref[seq ^ bit]
    for i in range(0, len(alone), 2):
        for half in range(2):
            size = alone[i].shape[1] // (n_dp // 2)
            for d in range(n_dp // 2):
                place = slice((i // 2) * size, (i // 2 + 1) * size)
                part = alone[i + half][:, d * size : (d + 1) * size]
                alone_ref[half * (n_dp // 2) + d, :, place] = part.astype(BF16)


def pack(seq, grads, n_dp, alone):
    columns = sum(g.shape[1] for g in grads) // (4 * n_dp)
    dims = (n_dp, RANK, columns)
    outs = [shape((2,) + dims, BF16)] * 2
    outs.append(shape((n_dp, RANK, sum(g.shape[1] for g in alone) // n_dp), BF16))
    return call(
        functools.partial(pack_kernel, n_dp, len(grads)),
        "pack",
        in_specs=[SMEM] + [VMEM] * (len(grads) + len(alone)),
        out_shape=outs,
        scratch_shapes=[pltpu.VMEM((4,) + dims, BF16)],
    )(seq[None], *grads, *alone)


def sort_kernel(widths, ids_ref, came_ref, *out_refs):
    came = [came_ref[d].astype(F32) for d in range(came_ref.shape[0])]
    for a in range(ADAPT):
        total = jnp.zeros(came[0].shape, F32)
        for d, value in enumerate(came):
            total = total + jnp.where(ids_ref[d] == a, value, 0.0)
        at = 0
        for ref, width in zip(out_refs, widths):
            part = total[:, at : at + width]
            ref[a] = part.T if width < 64 else part
            at += width


def sort(ids, came, widths):
    outs = call(
        functools.partial(sort_kernel, widths),
        "sort",
        in_specs=[SMEM, VMEM],
        out_shape=[shape((ADAPT, w, RANK) if w < 64 else (ADAPT, RANK, w), F32) for w in widths],
    )(ids, came)
    return [o if w < 64 else o.transpose(0, 2, 1) for o, w in zip(outs, widths)]


def shards(
    tokens,
    cotangent,
    lengths,
    adapter_ids,
    attn_gain,
    query_gain,
    key_gain,
    ffn_gain,
    w_query,
    w_key,
    w_value,
    w_out,
    gate_weight,
    w_up,
    w_down,
    a_query,
    b_query,
    a_key,
    b_key,
    a_value,
    b_value,
    a_out,
    b_out,
    a_gate,
    b_gate,
    a_up,
    b_up,
    a_down,
    b_down,
):
    n_dp = lax.axis_size("dp")
    seq = lax.axis_index("seq")
    _, block, width = tokens.shape
    length = lengths[0]
    positions = seq * block + jnp.arange(block)
    valid = (positions < length).astype(F32)[:, None]
    sources = ring_sources()
    clock = Clock()
    n_query, n_key = H * HD, KV * HD
    local, each, thin = b_gate.shape[1], a_query.shape[1], b_key.shape[1]
    widths = (local, each, thin)

    attn = Ring(jnp.concatenate([w_query, w_key, w_value, w_out], axis=1))
    first_came, age = None, 0
    queue = [attn.pieces[0]]
    sides, acrosses, corners, going = [], [], [], []
    arrived = slot = 0
    last = attn.steps - 1
    while len(corners) < n_dp + 1:
        waits, new = [], []
        if not attn.complete():
            new = attn.step(clock)
            waits += new
            if attn.complete():
                ended = new
                new = [new]
        elif first_came is not None:
            age += 1
            if age == 3 and len(first_ring.pieces) == 3:
                waits += first_came
                first_came = None
        elif not first_ring.complete():
            first_came, age = first_ring.step(lambda v: after(v, ended) if len(first_ring.pieces) == 1 else clock(v)), 0
        while len(acrosses) < len(queue) and len(going) < 2:
            acrosses.append(partner(clock(queue[len(acrosses)]), 2))
            going.append(len(acrosses))
        for _ in range(3):
            if len(corners) < arrived:
                corners.append(partner(clock(acrosses[len(corners)]), 1))
                waits.append(corners[-1])
            elif len(sides) < len(queue):
                sides.append(partner(clock(queue[len(sides)]), 1))
                waits.append(sides[-1])
        if slot == 0:
            slots_a, slots_b = columns_for_seq(gate_weight, w_up, n_dp)
            ids = lax.all_to_all(
                jnp.broadcast_to(adapter_ids[None], (n_dp, 128)), "dp", 0, 0, tiled=True
            )[:, 0]
            stacks = (b_gate, b_up, a_down, a_query, a_key, a_value, b_query, a_out, b_out)
            stacks += (a_gate, a_up, b_down, b_key, b_value)
            sent = pick(ids, [m.transpose(0, 2, 1) for m in stacks])
            waits += [sent, slots_a]
        if slot == 1:
            swapped_a = lax.all_to_all(clock(slots_a), "seq", 0, 0, tiled=True)
        if slot == 2:
            mine = lax.all_to_all(clock(sent), "dp", 0, 0, tiled=True)
            first_ring = Ring(jnp.concatenate([w_down, swapped_a.reshape(-1, width)], axis=0))
            waits.append(first_ring.pieces[0])
        if slot == last + 2:
            inputs = clock(tokens)[0].astype(F32)
            normed = rms_scale(inputs, attn_gain).astype(BF16)
            normed_t = normed.T
            cot = cotangent[0].astype(F32)
            grad_out = (valid * clock(cot)).astype(BF16)
            waits += [normed_t, grad_out]
        if going and (slot == 0 or len(going) == 2 or len(queue) == n_dp + 1):
            waits.append(acrosses[going[0] - 1])
        else:
            going = going[:0] + going
        clock.tick(*waits)
        if going and any(w is acrosses[going[0] - 1] for w in waits):
            arrived = going.pop(0)
        if slot == 2:
            queue.append(clock(mine)[..., 3 * local :])
        queue += [jnp.concatenate(p, axis=0) if isinstance(p, tuple) else p for p in new]
        slot += 1
    others = [sides.pop(5), acrosses.pop(5), corners.pop(5)]
    queue.pop(5)
    attn_pieces = []
    for group in zip(queue, sides, acrosses, corners):
        attn_pieces += group
    order = everywhere_order(sources)

    belt = Conveyor(clock, [lambda: swapped_b.reshape(-1, width)])
    if first_came is None and not first_ring.complete():
        first_came = first_ring.step(clock)
    if first_came is not None:
        belt.going.append((first_came, first_ring))
    a_in, b_in, ao, bo, a_gu, bd, bg, bu, ad = spread(seq, mine, clock(others), widths)
    inner = contract(normed, a_in, 1, 1).astype(BF16)

    linear = project_in(order, normed_t, inner, b_in, attn_pieces)
    query_lin = linear[:n_query].reshape(H, HD, block)
    key_lin = linear[n_query : n_query + n_key].reshape(KV, HD, block)
    value_lin = linear[n_query + n_key :].reshape(KV, HD, block)
    cosine, sine = rotary_tables(positions)
    scale = HD**-0.5
    query_prep = lambda v: prepare(v, query_gain, cosine, sine)
    key_prep = lambda v: prepare(v, key_gain, cosine, sine)
    keys_values = jnp.concatenate([key_prep(key_lin), value_lin], axis=1).astype(BF16)
    grads = seq_pieces(clock(grad_out))
    keys_values = seq_pieces(after(keys_values, grads[2]))
    queries = (query_prep(query_lin) * scale).astype(BF16).reshape(n_query, block)
    limit = jnp.minimum(positions, length - 1).astype(jnp.int32)
    limit = jnp.tile(limit, GROUP)[None, :]
    belt.advance(queries, keys_values[2])
    swapped_b = lax.all_to_all(after(slots_b, queries), "seq", 0, 0, tiled=True)
    mixed, raised, inverse = attend(seq, limit, queries, keys_values)
    belt.advance(mixed)

    inner_out = contract(ao, mixed, 1, 0).astype(BF16)
    hidden, normed_two = project_out(
        order, mixed, inner_out, bo, tokens[0], valid, ffn_gain[None], attn_pieces
    )

    n2 = seq_pieces(normed_two)
    while not first_ring.complete():
        belt.advance(normed_two)
    ring_b = belt.rings[0]
    begun = place(clock(first_ring.pieces[:-1]), sources, 2)
    belt.until(first_ring, begun)
    w_lower, both_a = finish(begun, first_ring.pieces, sources)
    d_act, d_down = lower_back(clock(grads), w_lower, bd, ad)
    belt.advance(d_act)
    n2, low_n2 = all_tokens(n2, a_gu)
    act_a, dg_a, du_a, inner_a = units(0, n2, low_n2, both_a, bg, bu, ad, d_act)
    belt.advance(act_a)
    first = units_back_first(clock(dg_a), du_a, both_a)
    gbg_a, gbu_a, gad_a = units_grads(low_n2, d_down, after(act_a, first), dg_a, du_a)
    while not ring_b.complete():
        belt.advance(gbg_a)
    begun = place(clock(ring_b.pieces[:-1]), sources, 1)
    belt.until(ring_b, begun)
    (both_b,) = finish(begun, ring_b.pieces, sources)
    act_b, dg_b, du_b, inner_b = units(1, n2, low_n2, both_b, bg, bu, ad, d_act)
    inners = (inner_a, inner_b)
    keep, give = units_back(0, 2, first, dg_b, du_b, both_b, inners, a_gu)
    left, sent = seq_shares(keep, give)
    keep, give = units_back(1, 2, after(first, sent), dg_b, du_b, both_b, inners, a_gu)
    right, sent = seq_shares(keep, give)

    keep, give, grad_bd, grad_a_gu = lower(
        act_a, after(act_b, sent), w_lower, inners, bd, grads, n2
    )

    d_hidden, grad_update, d_inner_out = hidden_back(
        after(left[:2], keep) + left[2:], after(right[:2], keep) + right[2:], hidden, cotangent[0], valid, ffn_gain[None], bo
    )
    lowered, sent = seq_shares(*after((keep, give), grad_update))
    d_mixed = project_out_back(order, after(grad_update, sent), ao, d_inner_out, attn_pieces)
    count = KV // 2
    back = lambda part, d_mixed: attend_back(
        part * count, count, queries, keys_values, raised, inverse, mixed, d_mixed
    )
    d_query, keep, give = back(0, d_mixed)
    gbg_b, gbu_b, gad_b = units_grads(low_n2, d_down, after(act_b, d_query), dg_b, du_b)
    first_kv, sent = seq_shares(keep, give, (gbg_b, lowered[2]))
    other_query, keep, give = back(1, after(d_mixed, sent))
    other_kv, sent = seq_shares(keep, give)

    first_kv = total(after(first_kv, other_query))
    d_query = after(jnp.concatenate([d_query, other_query], axis=0), first_kv)
    d_queries = d_query.reshape(H, HD, block) * scale
    d_kv = jnp.concatenate([first_kv, total(other_kv)], axis=0)
    d_query_lin = jax.vjp(query_prep, query_lin)[1](d_queries)[0]
    d_key_lin = jax.vjp(key_prep, key_lin)[1](d_kv[:, :HD])[0]
    d_linear = jnp.concatenate(
        [
            d_query_lin.reshape(n_query, block),
            d_key_lin.reshape(n_key, block),
            d_kv[:, HD:].reshape(n_key, block),
        ],
        axis=0,
    ).astype(BF16)
    output = (hidden + valid * total(after(lowered, d_linear))).astype(BF16)
    d_inner = contract(b_in, d_linear, 1, 0).astype(BF16)
    grad_tokens = project_in_back(
        order, d_linear, a_in, d_inner, tokens[0], attn_gain[None], d_hidden, attn_pieces
    )

    grad_ao = contract(d_inner_out, mixed, 0, 1)
    grad_bo = contract(inner_out, grad_update, 1, 0)
    grad_a_in = contract(d_inner, normed, 1, 0)
    grad_b_in = contract(inner, d_linear, 0, 1)
    q_end, k_end = n_query, n_query + n_key
    partial = [grad_ao, grad_bo, grad_a_gu[:RANK], grad_a_gu[RANK:], grad_bd]
    partial += [grad_a_in[i * RANK : (i + 1) * RANK] for i in range(3)]
    partial += [grad_b_in[:RANK, :q_end]]
    partial += [grad_b_in[RANK : 2 * RANK, q_end:k_end], grad_b_in[2 * RANK :, k_end:]]
    whole = (gbg_a, gbg_b, gbu_a, gbu_b, gad_a, gad_b)
    keep, give, whole = pack(seq, partial, n_dp, whole)
    (keep, arrived, across), _ = seq_shares(keep, give)
    summed = total((keep, arrived, across)).astype(BF16)
    summed = after(jnp.concatenate([summed, whole], axis=2), output)
    sizes = [each] * 9 + [thin] * 2 + [local] * 3
    came = lax.all_to_all(summed, "dp", 0, 0, tiled=True)
    gao, gbo, gag, gau, gbd, gaq, gak, gav, gbq, gbk, gbv, gbg, gbu, gad = sort(ids, came, sizes)
    return (
        output[None],
        grad_tokens[None],
        gaq,
        gbq,
        gak,
        gbk,
        gav,
        gbv,
        gao,
        gbo,
        gag,
        gbg,
        gau,
        gbu,
        gad,
        gbd,
    )


def solution(mesh):
    tokens = P("dp", "seq", None)
    matrix = P(("dp", "seq"), None)
    stack = P(None, ("dp", "seq"), None)
    in_specs = (tokens, tokens, P("dp"), P("dp")) + (P(),) * 4 + (matrix,) * 7 + (stack,) * 14
    out_specs = (tokens, tokens) + (stack,) * 14
    return jax.shard_map(shards, mesh=mesh, in_specs=in_specs, out_specs=out_specs, check_vma=False)
```
